32 devices in a mesh: fsdp: 4 (over y, core), tp: 8 (over z, x).
Axes of the slice: x: 2, y: 2, z: 4, core: 2. Of those that a mesh axis runs over, the one named last changes fastest.
Arguments:
- tokens: bfloat16 [16384, 1024], P(('fsdp', 'tp')), may hold values from -6 to 6
- segment_ids: int32 [16, 1024], P('fsdp'), may hold values from 0 to 3, never falling along the last dimension, each value on 1 to 768 neighbouring positions
- w_qkv: bfloat16 [1024, 3, 1024], P('fsdp', None, 'tp'), may hold values from -0.1875 to 0.1875
- b_qv: float32 [2, 1024], replicated, may hold values from -3 to 3
- w_out: bfloat16 [1024, 1024], P('fsdp', 'tp'), may hold values from -1.5 to 1.5
- b_out: float32 [1024], replicated, may hold values from -3 to 3
- w_up: bfloat16 [1024, 4096], P('fsdp', 'tp'), may hold values from -0.1875 to 0.1875
- b_up: float32 [4096], replicated, may hold values from -3 to 3
- w_down: bfloat16 [1024, 4096], P('fsdp', 'tp'), may hold values from -0.09375 to 0.09375
- b_down: float32 [1024], replicated, may hold values from -3 to 3
- ln1_gain: float32 [1024], replicated, may hold values from 0.1 to 1.9
- ln1_shift: float32 [1024], replicated, may hold values from -2 to 2
- ln2_gain: float32 [1024], replicated, may hold values from 0.1 to 1.9
- ln2_shift: float32 [1024], replicated, may hold values from -2 to 2
- grad_out: bfloat16 [16384, 1024], P(('fsdp', 'tp')), may hold values from -6 to 6
Outputs:
- result: bfloat16 [16384, 1024], P(('fsdp', 'tp'))
- token_grad: bfloat16 [16384, 1024], P(('fsdp', 'tp'))
- grad_w_qkv: float32 [1024, 3, 1024], P('fsdp', None, 'tp')
- grad_b_qv: float32 [2, 1024], replicated
- grad_w_out: float32 [1024, 1024], P('fsdp', 'tp')
- grad_b_out: float32 [1024], replicated
- grad_w_up: float32 [1024, 4096], P('fsdp', 'tp')
- grad_b_up: float32 [4096], replicated
- grad_w_down: float32 [1024, 4096], P('fsdp', 'tp')
- grad_b_down: float32 [1024], replicated
- grad_ln1_gain: float32 [1024], replicated
- grad_ln1_shift: float32 [1024], replicated
- grad_ln2_gain: float32 [1024], replicated
- grad_ln2_shift: float32 [1024], replicated
The draws below stay inside these ranges and needn't reach their ends.
Inputs may be any that keep to these rules, and one draw needn't show every extreme that they name: `segment_ids`: along a sequence the ids never fall; each of the 4 documents of a sequence is a run of 1 to 768 tokens, and some run has exactly 768.
All inputs are finite; a program needn't handle non-finite values.
Results may differ from the reference program's by a relative error of at most 0.017.
Values may be sent and summed in bfloat16 or wider, within the bound.
No kernel may reach another device: no remote copies, remote signals or barrier semaphores. Data moves between devices by JAX's collectives and lax.ppermute only.
A program may use at most 192 MiB of HBM per device.

```python
import math
import jax
import jax.numpy as jnp
import numpy as np
from jax import lax

D = 1024
HEADS = 16
HEAD_DIM = 64
FF = 4096
SEQ_LEN = 1024
SEQS = 4
SEQ_ALL = 16
TOKENS = 16384
DOCS = 4
DOC_MOST = 768
N_FSDP = 4


def block_scale(rng, dims, shards, least, high):
    def one(position, blocks):
        draws = jax.random.uniform(jax.random.fold_in(jax.random.fold_in(rng, 6), position), (blocks,), jnp.float32, least / len(shards), high / len(shards))
        return jnp.repeat(jnp.exp(draws), dims[position] // blocks).reshape((-1,) + (1,) * (len(dims) - position - 1))

    factor_of = one(*shards[0])
    for cut in shards[1:]:
        factor_of = factor_of * one(*cut)
    return factor_of


def profile(amount, total, limit, lean):
    loads = [(1 << 20) // math.isqrt(rank ** lean) + 1 for rank in range(2, amount + 1)]
    rest, given = total - limit - (amount - 1), [1] * (amount - 1)
    while rest > 0:
        free = [i for i in range(amount - 1) if given[i] < limit]
        mass, remaining = sum([loads[i] for i in free]), rest
        for i in free:
            addition = min(limit - given[i], max(1, remaining * loads[i] // mass), rest)
            given[i] = given[i] + addition
            rest = rest - addition
    return np.array([limit] + given)


def ragged(stream_key, number_of, total, most, lean):
    if number_of == 2:
        one = jax.random.randint(stream_key, (), max(1, total - most), min(most, total - 1) + 1)
        return jnp.stack([one, total - one])
    tallies = jnp.asarray(profile(number_of, total, most, lean), jnp.int32)
    pairs = (number_of - 1) // 2
    source_of, sink = tallies[1:1 + 2 * pairs:2], tallies[2:2 + 2 * pairs:2]
    slack = jnp.minimum(source_of - 1, most - sink)
    moved = jax.random.randint(jax.random.fold_in(stream_key, 1), (pairs,), 0, 1 << 20) % (slack + 1)
    tallies = tallies.at[1:1 + 2 * pairs:2].set(source_of - moved).at[2:2 + 2 * pairs:2].set(sink + moved)
    return tallies[jax.random.permutation(jax.random.fold_in(stream_key, 2), number_of)]


def scatter_about(rng, extent, spread, most, split=(), kind=jnp.bfloat16):
    factor_of = block_scale(rng, extent, split, -0.22, 0.18) if split else 1.0
    values = jax.random.normal(rng, extent, jnp.float32) * spread * factor_of
    return jnp.minimum(jnp.maximum(values, -most), most).astype(kind)


def setup_inputs(seed: int = 0) -> dict:
    key_list = jax.random.split(jax.random.key(seed), 16)
    return {
        "tokens": scatter_about(key_list[0], (TOKENS, D), 1.0, 6.0, ((0, 32),)),
        "segment_ids": jax.vmap(lambda own: jnp.searchsorted(jnp.cumsum(ragged(own, DOCS, SEQ_LEN, DOC_MOST, 0)), jnp.arange(SEQ_LEN), side="right"))(jax.random.split(key_list[1], SEQ_ALL)).reshape((SEQ_ALL, SEQ_LEN)).astype(jnp.int32),
        "w_qkv": scatter_about(key_list[2], (D, 3, D), D ** -0.5, 0.1875, ((0, 4), (2, 8))),
        "b_qv": scatter_about(key_list[3], (2, D), 0.5, 3.0, (), jnp.float32),
        "w_out": scatter_about(key_list[4], (D, D), (D // 64) ** -0.5, 1.5, ((0, 4), (1, 8))),
        "b_out": scatter_about(key_list[5], (D,), 0.5, 3.0, (), jnp.float32),
        "w_up": scatter_about(key_list[6], (D, FF), D ** -0.5, 0.1875, ((0, 4), (1, 8))),
        "b_up": scatter_about(key_list[7], (FF,), 0.5, 3.0, (), jnp.float32),
        "w_down": scatter_about(key_list[8], (D, FF), FF ** -0.5, 0.09375, ((0, 4), (1, 8))),
        "b_down": scatter_about(key_list[9], (D,), 0.5, 3.0, (), jnp.float32),
        "ln1_gain": jnp.clip(1.0 + 0.18 * jax.random.normal(key_list[10], (D,), jnp.float32), 0.1, 1.9),
        "ln1_shift": scatter_about(key_list[11], (D,), 0.3, 2.0, (), jnp.float32),
        "ln2_gain": jnp.clip(1.0 + 0.18 * jax.random.normal(key_list[12], (D,), jnp.float32), 0.1, 1.9),
        "ln2_shift": scatter_about(key_list[13], (D,), 0.3, 2.0, (), jnp.float32),
        "grad_out": scatter_about(key_list[14], (TOKENS, D), 1.0, 6.0, ((0, 32),)),
    }


@jax.custom_vjp
def low(v):
    return lax.optimization_barrier(v.astype(jnp.bfloat16)).astype(jnp.float32)

@jax.custom_vjp
def low_back(v):
    return v

def low_keep(v):
    return (low(v), None)

def low_pass(kept, grad):
    return (grad,)

def back_keep(v):
    return (v, None)

def back_low(kept, grad):
    return (low(grad),)
low.defvjp(low_keep, low_pass)
low_back.defvjp(back_keep, back_low)
EPS = 1e-05
HIGH = lax.Precision.HIGHEST

def norm_rows(values, gain, shift):
    centred = values - lax.optimization_barrier(jnp.mean(values, axis=-1, keepdims=True))
    inverse = lax.rsqrt(lax.optimization_barrier(jnp.mean(centred * centred, axis=-1, keepdims=True)) + EPS)
    return centred * inverse * gain + shift

def attend_one(item):
    query, key, value, segment = item
    length = query.shape[0]
    place = jnp.arange(length, dtype=jnp.int32)
    allowed = (segment[:, None] == segment[None, :]) & (place[None, :] <= place[:, None])
    scores = jnp.einsum('qhd,khd->hqk', query, key, precision=HIGH) * HEAD_DIM ** (-0.5)
    scores = low_back(scores)
    scores = jnp.where(allowed[None], scores, -1e+30)
    probs = low(jax.nn.softmax(scores, axis=-1))
    return jnp.einsum('hqk,khd->qhd', probs, value, precision=HIGH)

def layer(values, segment, weights):
    w_qkv, b_qv, w_out, b_out, w_up, b_up, w_down, b_down, ln1_gain, ln1_shift, ln2_gain, ln2_shift = weights
    rows_here = values.shape[0]
    first = low(norm_rows(values, ln1_gain, ln1_shift))
    proj = jnp.einsum('rd,dcf->rcf', first, w_qkv, precision=HIGH)
    query = low(low_back(proj[:, 0] + b_qv[0]))
    key = low(low_back(proj[:, 1]))
    value = low(low_back(proj[:, 2] + b_qv[1]))
    shape_four = (segment.shape[0], segment.shape[1], HEADS, HEAD_DIM)
    mixed = lax.map(jax.checkpoint(attend_one), (query.reshape(shape_four), key.reshape(shape_four), value.reshape(shape_four), segment))
    mixed = low(low_back(mixed.reshape(rows_here, D)))
    branch = low_back(jnp.dot(mixed, w_out.T, precision=HIGH))
    middle = values + branch + b_out
    second = low(norm_rows(middle, ln2_gain, ln2_shift))
    pre_gelu = low_back(jnp.dot(second, w_up, precision=HIGH) + b_up)
    gelu_low = low(jax.nn.gelu(pre_gelu, approximate=True))
    down = low_back(jnp.dot(gelu_low, w_down.T, precision=HIGH))
    return middle + down + b_down

def reference(tokens, segment_ids, w_qkv, b_qv, w_out, b_out, w_up, b_up, w_down, b_down, ln1_gain, ln1_shift, ln2_gain, ln2_shift, grad_out):
    params = tuple((p.astype(jnp.float32) for p in (w_qkv, b_qv, w_out, b_out, w_up, b_up, w_down, b_down, ln1_gain, ln1_shift, ln2_gain, ln2_shift)))
    segments = segment_ids.reshape(N_FSDP, SEQS, SEQ_LEN)

    def forward(values, weights):
        rows = values.reshape(N_FSDP, SEQS * SEQ_LEN, D)
        stepper = jax.checkpoint(lambda pair: layer(pair[0], pair[1], weights))
        return lax.map(stepper, (rows, segments)).reshape(TOKENS, D)
    result, pullback = jax.vjp(forward, tokens.astype(jnp.float32), params)
    token_grad, grads = pullback(grad_out.astype(jnp.float32))
    return (result.astype(jnp.bfloat16), token_grad.astype(jnp.bfloat16), grads[0], grads[1], grads[2], grads[3], grads[4], grads[5], grads[6], grads[7], grads[8], grads[9], grads[10], grads[11])
```

```python
import functools

import jax
import jax.numpy as jnp
from jax import lax
from jax.experimental import pallas as pl
from jax.experimental.pallas import tpu as pltpu
from jax.sharding import Mesh, PartitionSpec as P

HEAD_DIM = 64
EPS = 1e-05
BF = jnp.bfloat16
F32 = jnp.float32
NT = (((1,), (1,)), ((), ()))
MIB = 1 << 20


def dot(a, b):
    return jnp.dot(a, b, preferred_element_type=F32)


def dot_nt(a, b):
    return lax.dot_general(a, b, NT, preferred_element_type=F32)


def aligned(value, multiple):
    return pl.multiple_of(value, multiple)


class Layout:
    def __init__(self, ny, nz, rows):
        self.ny, self.nz, self.rows = ny, nz, rows
        self.a = max(16, rows * 5 // 8 // 16 * 16)
        self.b = rows - self.a

    def row_block(self, pos, dy, dc):
        return lax.rem(pos[0] + dy, self.ny) * 2 + lax.rem(pos[1] + dc, 2)

    def col_block(self, pos, dz, dx):
        return lax.rem(pos[2] + dz, self.nz) * 2 + lax.rem(pos[3] + dx, 2)


def fetch(value, axis, size, shift):
    return lax.ppermute(value, axis, [(s, (s - shift) % size) for s in range(size)])


def deliver(value, axis, size, shift):
    return lax.ppermute(value, axis, [(s, (s + shift) % size) for s in range(size)])


def around(value, axis, size):
    return [value] + [fetch(value, axis, size, shift) for shift in range(1, size)]


def gather_group(lay, shard):
    top, low = shard[: lay.a], shard[lay.a :]
    top = jnp.stack(around(top, "tz", lay.nz))
    low = jnp.stack(around(low, "fy", lay.ny))
    top = jnp.stack(around(top, "tx", 2))
    low = jnp.stack(around(low, "tz", lay.nz))
    own = around(top, "fy", lay.ny) + around(low, "tx", 2)
    return own + [fetch(t, "c", 2, 1) for t in own]


def start_loads(lay, pos, refs, first, width, whole, sem):
    for dc in range(2):
        mine = refs[dc * (lay.ny + 2) : (dc + 1) * (lay.ny + 2)]
        for dz in range(lay.nz):
            for dx in range(2):
                k = lay.col_block(pos, dz, dx)
                cols = pl.ds(aligned(k * width, width), width)
                for dy in range(lay.ny):
                    start = aligned(lay.row_block(pos, dy, dc) * lay.rows, lay.rows)
                    pltpu.make_async_copy(
                        mine[dy].at[dx, dz, :, pl.ds(first, width)],
                        whole.at[pl.ds(start, lay.a), cols],
                        sem.at[k],
                    ).start()
                    pltpu.make_async_copy(
                        mine[lay.ny + dx].at[dz, dy, :, pl.ds(first, width)],
                        whole.at[pl.ds(aligned(start + lay.a, 16), lay.b), cols],
                        sem.at[k],
                    ).start()


def wait_load(k, width, whole, sem):
    cols = pl.ds(aligned(k * width, width), width)
    pltpu.make_async_copy(whole.at[:, cols], whole.at[:, cols], sem.at[k]).wait()


def kernel_call(body, pos, grid, ins, in_specs, outs, out_specs, scratch, flops, moved):
    return pl.pallas_call(
        body,
        out_shape=outs,
        grid_spec=pltpu.PrefetchScalarGridSpec(
            num_scalar_prefetch=1,
            grid=grid,
            in_specs=in_specs,
            out_specs=out_specs,
            scratch_shapes=scratch,
        ),
        compiler_params=pltpu.CompilerParams(
            dimension_semantics=("arbitrary",) * len(grid), vmem_limit_bytes=60 * MIB
        ),
        cost_estimate=pl.CostEstimate(flops=flops, bytes_accessed=moved, transcendentals=0),
    )(pos, *ins)


def shape(dims, dtype):
    return jax.ShapeDtypeStruct(dims, dtype)


def full(dims):
    return pl.BlockSpec(dims, lambda *_: (0,) * len(dims))


def at_cols(rows, width):
    return pl.BlockSpec((rows, width), lambda k, *_: (0, k))


def at_lead(*dims):
    return pl.BlockSpec((1,) + dims, lambda k, *_: (k,) + (0,) * len(dims))


ANY = pl.BlockSpec(memory_space=pl.ANY)


def norm_parts(values):
    centred = values - jnp.mean(values, axis=-1, keepdims=True)
    inverse = lax.rsqrt(jnp.mean(centred * centred, axis=-1, keepdims=True) + EPS)
    return centred * inverse, inverse


def norm_backward(grad, unit, inverse, gain):
    scaled = grad * gain
    return inverse * (
        scaled
        - jnp.mean(scaled, axis=-1, keepdims=True)
        - unit * jnp.mean(scaled * unit, axis=-1, keepdims=True)
    )


def qkv_call(lay, pos, first, bias_q, bias_v, weights, width):
    both, dim = first.shape
    rows = both // 2
    blocks = 2 * lay.nz
    n = len(weights)

    def body(pos_ref, first_ref, bq_ref, bv_ref, *rest):
        refs, (q_ref, k_ref, v_ref, whole, sem) = rest[:n], rest[n:]
        k = pl.program_id(0)

        @pl.when(k == 0)
        def _():
            start_loads(lay, pos_ref, refs, 0, 3 * width, whole, sem)

        wait_load(k, 3 * width, whole, sem)
        start = k * (3 * width)
        own = dot(first_ref[rows:], whole[:, pl.ds(aligned(start, width), 3 * width)])
        q_ref[0] = ((own[:, :width] + bq_ref[...]).astype(BF) * HEAD_DIM**-0.5).astype(BF)
        k_ref[0, rows:] = own[:, width : 2 * width].astype(BF)
        v_ref[0, rows:] = (own[:, 2 * width :] + bv_ref[...]).astype(BF)
        prev = dot(first_ref[:rows], whole[:, pl.ds(aligned(start + width, width), 2 * width)])
        k_ref[0, :rows] = prev[:, :width].astype(BF)
        v_ref[0, :rows] = (prev[:, width:] + bv_ref[...]).astype(BF)

    return kernel_call(
        body,
        pos,
        (blocks,),
        (first, bias_q, bias_v, *weights),
        [full((both, dim)), at_cols(1, width), at_cols(1, width)] + [ANY] * n,
        [
            shape((blocks, rows, width), BF),
            shape((blocks, both, width), BF),
            shape((blocks, both, width), BF),
        ],
        [at_lead(rows, width), at_lead(both, width), at_lead(both, width)],
        [pltpu.VMEM((dim, blocks * 3 * width), BF), pltpu.SemaphoreType.DMA((blocks,))],
        2 * dim * blocks * width * rows * 5,
        14 * MIB,
    )


def mask_bias(seg_k, seg_q, rows):
    both = seg_k.shape[0]
    key_at = lax.broadcasted_iota(jnp.int32, (both, rows), 0) - (both - rows)
    query_at = lax.broadcasted_iota(jnp.int32, (both, rows), 1)
    return jnp.where((seg_k == seg_q) & (key_at <= query_at), 0.0, -1e30).astype(F32)


def head_only(block, head):
    lane = lax.broadcasted_iota(jnp.int32, block.shape, 1)
    inside = (lane >= head * HEAD_DIM) & (lane < (head + 1) * HEAD_DIM)
    return jnp.where(inside, block, jnp.zeros_like(block))


def attend_call(pos, query, key, value, seg_k, seg_q):
    blocks, both, width = key.shape
    rows = query.shape[1]
    heads = width // HEAD_DIM
    step = min(rows, 256)

    def body(pos_ref, q_ref, k_ref, v_ref, sk_ref, sq_ref, mixed_ref, lse_ref, bias, out_t):
        @pl.when(pl.program_id(0) == 0)
        def _():
            bias[...] = mask_bias(sk_ref[...], sq_ref[...], rows)

        value_t = v_ref[0].T
        for tile in range(rows // step):
            here = slice(tile * step, (tile + 1) * step)
            keys = both - rows + (tile + 1) * step
            for head in range(heads):
                lanes = slice(head * HEAD_DIM, (head + 1) * HEAD_DIM)
                scores = dot_nt(k_ref[0, :keys], head_only(q_ref[0, here], head))
                scores = scores + bias[:keys, here]
                top = jnp.max(scores, axis=0, keepdims=True)
                expo = jnp.exp(scores - top)
                total = jnp.sum(expo, axis=0, keepdims=True)
                out = dot(value_t[lanes, :keys], expo.astype(BF))
                out_t[lanes, here] = out * (1.0 / total)
                lse_ref[0, head : head + 1, here] = top + jnp.log(total)
        mixed_ref[...] = out_t[...].T.astype(BF)

    return kernel_call(
        body,
        pos,
        (blocks,),
        (query, key, value, seg_k, seg_q),
        [at_lead(rows, width), at_lead(both, width), at_lead(both, width), full((both, 1)), full((1, rows))],
        [shape((rows, blocks * width), BF), shape((blocks, heads, rows), F32)],
        [at_cols(rows, width), at_lead(heads, rows)],
        [pltpu.VMEM((both, rows), F32), pltpu.VMEM((width, rows), F32)],
        blocks * heads * rows * both * 256 * 4,
        8 * MIB,
    )


def branch_call(lay, pos, mixed, tokens, b_out, gain, shift, weights, first, width):
    rows, dim = tokens.shape
    blocks = 2 * lay.nz
    n = len(weights)

    def body(pos_ref, mixed_ref, tok_ref, bias_ref, gain_ref, shift_ref, *rest):
        refs, (middle_ref, second_ref, whole, sem) = rest[:n], rest[n:]
        start_loads(lay, pos_ref, refs, first, width, whole, sem)
        for k in range(blocks):
            wait_load(k, width, whole, sem)
        branch = dot_nt(mixed_ref[...], whole[...])
        middle = tok_ref[...].astype(F32) + branch + bias_ref[...]
        middle_ref[...] = middle
        second_ref[...] = (norm_parts(middle)[0] * gain_ref[...] + shift_ref[...]).astype(BF)

    return kernel_call(
        body,
        pos,
        (),
        (mixed, tokens, b_out, gain, shift, *weights),
        [full(mixed.shape), full(tokens.shape)] + [full((1, dim))] * 3 + [ANY] * n,
        [shape((rows, dim), F32), shape((rows, dim), BF)],
        [full((rows, dim)), full((rows, dim))],
        [pltpu.VMEM((dim, blocks * width), BF), pltpu.SemaphoreType.DMA((blocks,))],
        2 * rows * dim * blocks * width,
        7 * MIB,
    )


def up_call(lay, pos, second, b_up, weights, width):
    rows, dim = second.shape
    blocks = 2 * lay.nz
    n = len(weights)

    def body(pos_ref, second_ref, bias_ref, *rest):
        refs, (gelu_ref, slope_ref, whole, sem) = rest[:n], rest[n:]
        k = pl.program_id(0)

        @pl.when(k == 0)
        def _():
            start_loads(lay, pos_ref, refs, 0, width, whole, sem)

        wait_load(k, width, whole, sem)
        u = dot(second_ref[...], whole[:, pl.ds(aligned(k * width, width), width)]) + bias_ref[...]
        scale = 0.7978845608028654
        square = u * u
        th = jnp.tanh(u * (scale + (scale * 0.044715) * square))
        half = 0.5 + 0.5 * th
        gelu_ref[...] = (u * half).astype(BF)
        slope = half + (0.5 * u) * (1.0 - th * th) * (scale + (3.0 * scale * 0.044715) * square)
        slope_ref[...] = slope.astype(BF)

    return kernel_call(
        body,
        pos,
        (blocks,),
        (second, b_up, *weights),
        [full(second.shape), at_cols(1, width)] + [ANY] * n,
        [shape((rows, blocks * width), BF)] * 2,
        [at_cols(rows, width)] * 2,
        [pltpu.VMEM((dim, blocks * width), BF), pltpu.SemaphoreType.DMA((blocks,))],
        2 * rows * dim * blocks * width,
        17 * MIB,
    )


def ffn_back_call(lay, pos, gelu, slope, grad, middle, b_down, gain, w_down, w_up, width):
    rows, dim = middle.shape
    blocks = 2 * lay.nz
    n = len(w_down)

    def body(pos_ref, gelu_ref, slope_ref, grad_ref, middle_ref, bias_ref, gain_ref, *rest):
        down_refs, up_refs = rest[:n], rest[n : 2 * n]
        pre_ref, hidden_ref, result_ref, mgrad_ref, low_ref, sums_ref = rest[2 * n : 2 * n + 6]
        down, up, acc_down, acc_second, sem_down, sem_up = rest[2 * n + 6 :]
        k = pl.program_id(0)

        @pl.when(k == 0)
        def _():
            start_loads(lay, pos_ref, down_refs, 0, width, down, sem_down)
            start_loads(lay, pos_ref, up_refs, 0, width, up, sem_up)
            acc_down[...] = jnp.zeros_like(acc_down)
            acc_second[...] = jnp.zeros_like(acc_second)

        cols = pl.ds(aligned(k * width, width), width)
        wait_load(k, width, down, sem_down)
        acc_down[...] += dot_nt(gelu_ref[...], down[:, cols])
        pre = (dot(grad_ref[...], down[:, cols]) * slope_ref[...].astype(F32)).astype(BF)
        pre_ref[...] = pre
        hidden_ref[...] = jnp.sum(pre.astype(F32), axis=0, keepdims=True)
        wait_load(k, width, up, sem_up)
        acc_second[...] += dot_nt(pre, up[:, cols])

        @pl.when(k == blocks - 1)
        def _():
            values = middle_ref[...]
            result_ref[...] = (values + acc_down[...] + bias_ref[...]).astype(BF)
            unit, inverse = norm_parts(values)
            second_grad = acc_second[...]
            sums_ref[0:1] = jnp.sum(second_grad * unit, axis=0, keepdims=True)
            sums_ref[1:2] = jnp.sum(second_grad, axis=0, keepdims=True)
            out = grad_ref[...].astype(F32)
            sums_ref[3:4] = jnp.sum(out, axis=0, keepdims=True)
            out = out + norm_backward(second_grad, unit, inverse, gain_ref[...])
            sums_ref[2:3] = jnp.sum(out, axis=0, keepdims=True)
            mgrad_ref[...] = out
            low_ref[...] = out.astype(BF)

    return kernel_call(
        body,
        pos,
        (blocks,),
        (gelu, slope, grad, middle, b_down, gain, *w_down, *w_up),
        [at_cols(rows, width)] * 2
        + [full((rows, dim))] * 2
        + [full((1, dim))] * 2
        + [ANY] * (2 * n),
        [
            shape((rows, blocks * width), BF),
            shape((1, blocks * width), F32),
            shape((rows, dim), BF),
            shape((rows, dim), F32),
            shape((rows, dim), BF),
            shape((4, dim), F32),
        ],
        [at_cols(rows, width), at_cols(1, width)] + [full((rows, dim))] * 3 + [full((4, dim))],
        [
            pltpu.VMEM((dim, blocks * width), BF),
            pltpu.VMEM((dim, blocks * width), BF),
            pltpu.VMEM((rows, dim), F32),
            pltpu.VMEM((rows, dim), F32),
            pltpu.SemaphoreType.DMA((blocks,)),
            pltpu.SemaphoreType.DMA((blocks,)),
        ],
        6 * rows * dim * blocks * width,
        36 * MIB,
    )


def mixed_grad_call(lay, pos, low, weights, first, width):
    rows, dim = low.shape
    blocks = 2 * lay.nz
    n = len(weights)

    def body(pos_ref, low_ref, *rest):
        refs, (out_ref, whole, sem) = rest[:n], rest[n:]
        start_loads(lay, pos_ref, refs, first, width, whole, sem)
        for k in range(blocks):
            wait_load(k, width, whole, sem)
        out_ref[...] = dot(low_ref[...], whole[...]).astype(BF)

    return kernel_call(
        body,
        pos,
        (),
        (low, *weights),
        [full((rows, dim))] + [ANY] * n,
        [shape((rows, blocks * width), BF)],
        [full((rows, blocks * width))],
        [pltpu.VMEM((dim, blocks * width), BF), pltpu.SemaphoreType.DMA((blocks,))],
        2 * rows * dim * blocks * width,
        4 * MIB,
    )[0]


def attend_back_call(pos, query, key, value, seg_k, seg_q, lse, mixed_grad):
    blocks, both, width = key.shape
    rows = query.shape[1]
    heads = width // HEAD_DIM
    step = min(rows, 256)

    def body(pos_ref, q_ref, k_ref, v_ref, sk_ref, sq_ref, lse_ref, grad_ref, *rest):
        dq_ref, dk_ref, dv_ref, sums_ref, bias, dq_t, dk, dv = rest

        @pl.when(pl.program_id(0) == 0)
        def _():
            bias[...] = mask_bias(sk_ref[...], sq_ref[...], rows)

        key_t = k_ref[0].T
        dk[...] = jnp.zeros_like(dk)
        dv[...] = jnp.zeros_like(dv)
        for tile in range(rows // step):
            here = slice(tile * step, (tile + 1) * step)
            keys = both - rows + (tile + 1) * step
            for head in range(heads):
                lanes = slice(head * HEAD_DIM, (head + 1) * HEAD_DIM)
                q_head = head_only(q_ref[0, here], head)
                g_head = head_only(grad_ref[here], head)
                scores = dot_nt(k_ref[0, :keys], q_head) + bias[:keys, here]
                probs = jnp.exp(scores - lse_ref[0, head : head + 1, here])
                prob_grad = dot_nt(v_ref[0, :keys], g_head)
                inner = jnp.sum(probs * prob_grad, axis=0, keepdims=True)
                score_grad = (probs * (prob_grad - inner)).astype(BF)
                dv[:keys] += dot(probs.astype(BF), g_head)
                dk[:keys] += dot(score_grad, q_head)
                dq_t[lanes, here] = dot(key_t[lanes, :keys], score_grad)
        dq = (dq_t[...].T * HEAD_DIM**-0.5).astype(BF)
        dv_low = dv[...].astype(BF)
        dq_ref[0] = dq
        dk_ref[0] = dk[...].astype(BF)
        dv_ref[0] = dv_low
        sums_ref[0:1] = jnp.sum(dq.astype(F32), axis=0, keepdims=True)
        sums_ref[1:2] = jnp.sum(dv_low.astype(F32), axis=0, keepdims=True)

    return kernel_call(
        body,
        pos,
        (blocks,),
        (query, key, value, seg_k, seg_q, lse, mixed_grad),
        [
            at_lead(rows, width),
            at_lead(both, width),
            at_lead(both, width),
            full((both, 1)),
            full((1, rows)),
            at_lead(heads, rows),
            at_cols(rows, width),
        ],
        [
            shape((blocks, rows, width), BF),
            shape((blocks, both, width), BF),
            shape((blocks, both, width), BF),
            shape((2, blocks * width), F32),
        ],
        [at_lead(rows, width), at_lead(both, width), at_lead(both, width), at_cols(2, width)],
        [
            pltpu.VMEM((both, rows), F32),
            pltpu.VMEM((width, rows), F32),
            pltpu.VMEM((both, width), F32),
            pltpu.VMEM((both, width), F32),
        ],
        blocks * heads * rows * both * 256 * 8,
        12 * MIB,
    )


def first_grad_call(lay, pos, dq, dk, dv, prev, own, weights, width):
    rows, dim = own.shape
    blocks = 2 * lay.nz
    n = len(weights)

    def body(pos_ref, dq_ref, dk_ref, dv_ref, prev_ref, own_ref, *rest):
        refs, (back_ref, grad_ref, sums_ref, whole, acc, sem) = rest[:n], rest[n:]
        k = pl.program_id(0)

        @pl.when(k == 0)
        def _():
            start_loads(lay, pos_ref, refs, 0, 3 * width, whole, sem)
            acc[...] = jnp.zeros_like(acc)

        wait_load(k, 3 * width, whole, sem)
        start = k * (3 * width)
        part = jnp.concatenate([dk_ref[0, :rows], dv_ref[0, :rows]], axis=1)
        acc[:rows] += dot_nt(part, whole[:, pl.ds(aligned(start + width, width), 2 * width)])
        part = jnp.concatenate([dq_ref[0], dk_ref[0, rows:], dv_ref[0, rows:]], axis=1)
        acc[rows:] += dot_nt(part, whole[:, pl.ds(aligned(start, width), 3 * width)])

        @pl.when(k == blocks - 1)
        def _():
            back = acc[:rows]
            grad = acc[rows:]
            back_ref[...] = back.astype(BF)
            grad_ref[...] = grad
            unit_prev = norm_parts(prev_ref[...].astype(F32))[0]
            unit = norm_parts(own_ref[...].astype(F32))[0]
            sums_ref[0:1] = jnp.sum(back * unit_prev + grad * unit, axis=0, keepdims=True)
            sums_ref[1:2] = jnp.sum(back + grad, axis=0, keepdims=True)

    return kernel_call(
        body,
        pos,
        (blocks,),
        (dq, dk, dv, prev, own, *weights),
        [at_lead(rows, width), at_lead(2 * rows, width), at_lead(2 * rows, width)]
        + [full((rows, dim))] * 2
        + [ANY] * n,
        [shape((rows, dim), BF), shape((rows, dim), F32), shape((2, dim), F32)],
        [full((rows, dim)), full((rows, dim)), full((2, dim))],
        [
            pltpu.VMEM((dim, blocks * 3 * width), BF),
            pltpu.VMEM((2 * rows, dim), F32),
            pltpu.SemaphoreType.DMA((blocks,)),
        ],
        2 * dim * blocks * width * rows * 5,
        16 * MIB,
    )


def spans(lay):
    tops = [dy * 2 * lay.nz * lay.a for dy in range(lay.ny + 1)]
    lows = [tops[-1] + dx * lay.nz * lay.ny * lay.b for dx in range(3)]
    return tops, lows


def half_grad_call(lay, pos, half, columns, lefts, tile, operands, specs, received, flops):
    tops, lows = spans(lay)
    ny, nz, a, b = lay.ny, lay.nz, lay.a, lay.b
    n = len(operands)

    def body(pos_ref, *refs):
        ins, rest = refs[:n], refs[n:]
        got, rest = (rest[0], rest[1:]) if half == 0 else (None, rest)
        outs, scratch = rest[: ny + 2] if half == 0 else rest[:1], rest[(ny + 2) if half == 0 else 1 :]
        turned = []
        for index, ref in zip(lefts, scratch):
            ref[...] = ins[index][...].T
            turned.append(ref)

        def column(dz, dx):
            k = lay.col_block(pos_ref, dz, dx)
            for dy in range(ny):
                start = aligned(lay.row_block(pos_ref, dy, half) * lay.rows, lay.rows)
                left = [ref[pl.ds(start, lay.rows)] for ref in turned]
                block = tile(left, ins, k)
                top_at = aligned(tops[dy] + (dx * nz + dz) * a, 16)
                low_at = aligned(lows[dx] + (dz * ny + dy) * b, 16)
                if half == 0:
                    top = block[:a] + got[pl.ds(top_at, a)].astype(F32)
                    low = block[a:] + got[pl.ds(low_at, b)].astype(F32)
                    outs[dy][dx, dz] = top.astype(BF)
                    outs[ny + dx][dz, dy] = low.astype(BF)
                else:
                    outs[0][pl.ds(top_at, a)] = block[:a].astype(BF)
                    outs[0][pl.ds(low_at, b)] = block[a:].astype(BF)

        def step(dz, carry):
            for dx in range(2):
                column(dz, dx)
            return carry

        lax.fori_loop(0, nz, step, 0)

    total = lows[2]
    if half == 0:
        operands = (*operands, received)
        specs = specs + [full((total, columns))]
        outs = [shape((2, nz, a, columns), BF)] * ny + [shape((nz, ny, b, columns), BF)] * 2
        out_specs = [full(o.shape) for o in outs]
    else:
        outs = [shape((total, columns), BF)]
        out_specs = [full((total, columns))]
    scratch = [
        pltpu.VMEM((operands[index].shape[1], operands[index].shape[0]), BF) for index in lefts
    ]
    return kernel_call(
        body, pos, (), operands, specs, outs, out_specs, scratch, flops, 12 * MIB
    )


def sum_call(pos, groups, outs, build):
    flat = [r for g in groups for r in g]

    def body(pos_ref, *refs):
        ins, given = refs[: len(flat)], refs[len(flat) :]
        at, sums = 0, []
        for g in groups:
            mine = ins[at : at + len(g)]
            at += len(g)
            sums.append(lambda index, mine=mine: sum(
                (r[index].astype(F32) for r in mine[1:]), mine[0][index].astype(F32)
            ))
        build(sums, given)

    moved = sum(2 * r.size for r in flat) + sum(2 * o.size for o in outs)
    return kernel_call(
        body, pos, (), flat, [full(r.shape) for r in flat], outs, [full(o.shape) for o in outs], [],
        moved, moved,
    )


def scatter_group(lay, pos, parts, columns):
    ny, nz, a, b = lay.ny, lay.nz, lay.a, lay.b
    tops, lows = parts[:ny], parts[ny:]
    tops = [tops[0]] + [deliver(tops[s], "fy", ny, s) for s in range(1, ny)]
    lows = [lows[0], deliver(lows[1], "tx", 2, 1)]

    def build(sums, given):
        for dx in range(2):
            given[dx][...] = sums[0](dx).astype(BF)
        for dz in range(nz):
            given[2 + dz][...] = sums[1](dz).astype(BF)

    out = sum_call(
        pos, [tops, lows],
        [shape((nz, a, columns), BF)] * 2 + [shape((ny, b, columns), BF)] * nz, build,
    )
    tops = [out[0], deliver(out[1], "tx", 2, 1)]
    lows = [out[2]] + [deliver(out[2 + s], "tz", nz, s) for s in range(1, nz)]

    def build(sums, given):
        for dz in range(nz):
            given[dz][...] = sums[0](dz).astype(BF)
        for dy in range(ny):
            given[nz + dy][...] = sums[1](dy).astype(BF)

    out = sum_call(
        pos, [tops, lows],
        [shape((a, columns), BF)] * nz + [shape((b, columns), BF)] * ny, build,
    )
    tops = [out[0]] + [deliver(out[s], "tz", nz, s) for s in range(1, nz)]
    lows = [out[nz]] + [deliver(out[nz + s], "fy", ny, s) for s in range(1, ny)]

    def build(sums, given):
        given[0][:a] = sums[0](slice(None))
        given[0][a:] = sums[1](slice(None))

    return sum_call(pos, [tops, lows], [shape((a + b, columns), F32)], build)[0]


def weight_grad(lay, pos, columns, lefts, tile, operands, specs, flops):
    away = half_grad_call(lay, pos, 1, columns, lefts, tile, operands, specs, None, flops)[0]
    received = fetch(away, "c", 2, 1)
    parts = half_grad_call(lay, pos, 0, columns, lefts, tile, operands, specs, received, flops)
    return scatter_group(lay, pos, parts, columns)


def per_device(
    sizes,
    tokens,
    segment_ids,
    w_qkv,
    b_qv,
    w_out,
    b_out,
    w_up,
    b_up,
    w_down,
    b_down,
    ln1_gain,
    ln1_shift,
    ln2_gain,
    ln2_shift,
    grad_out,
):
    ny, nz = sizes
    rows, dim = tokens.shape
    length = segment_ids.shape[1]
    width = w_qkv.shape[2]
    hidden = w_up.shape[1]
    lay = Layout(ny, nz, w_qkv.shape[0])
    axes = ("fy", "c", "tz", "tx")
    pos = jnp.stack([lax.axis_index(axis) for axis in axes]).astype(jnp.int32)
    row = lambda v: v.reshape(1, -1)

    tokens_prev = lax.ppermute(tokens, "tx", [(0, 1)])
    qkv_parts = gather_group(lay, w_qkv.reshape(lay.rows, 3 * width))
    up_shard, tied = lax.optimization_barrier(
        (jnp.concatenate([w_up, w_out], axis=1), tokens_prev)
    )
    up_parts = gather_group(lay, up_shard)
    down_parts = gather_group(lay, w_down)

    tp_index = pos[2] * 2 + pos[3]
    sequence = tp_index // 2
    later = pos[3] > 0
    ids = lax.dynamic_slice_in_dim(segment_ids, sequence, 1, 0)
    seg_q = jnp.where(later, ids[:, rows:], ids[:, :rows])
    seg_prev = jnp.where(later, ids[:, :rows], -1)
    seg_k = jnp.concatenate([seg_prev, seg_q], axis=1).reshape(length, 1)

    both = jnp.concatenate([tokens_prev, tokens], axis=0).astype(F32)
    first = (norm_parts(both)[0] * ln1_gain + ln1_shift).astype(BF)
    query, key, value = qkv_call(lay, pos, first, b_qv[0:1], b_qv[1:2], qkv_parts, width)
    mixed, lse = attend_call(pos, query, key, value, seg_k, seg_q)
    middle, second = branch_call(
        lay, pos, mixed, tokens, row(b_out), row(ln2_gain), row(ln2_shift), up_parts, hidden, width
    )
    gelu, slope = up_call(lay, pos, second, row(b_up), up_parts, hidden)

    whole = lambda v: full(v.shape)
    block = lambda ref, k, size: ref[:, pl.ds(aligned(k * size, size), size)]

    def down_tile(left, ins, k):
        return dot(left[0], block(ins[1], k, hidden))

    grad_w_down = weight_grad(
        lay, pos, hidden, (0,), down_tile, (grad_out, gelu), [whole(grad_out), whole(gelu)],
        rows * dim * gelu.shape[1],
    )

    pre, grad_b_up, result, middle_grad, middle_low, sums2 = ffn_back_call(
        lay, pos, gelu, slope, grad_out, middle, row(b_down), row(ln2_gain), down_parts, up_parts, hidden
    )

    def up_tile(left, ins, k):
        return jnp.concatenate(
            [dot(left[0], block(ins[1], k, hidden)), dot(left[1], block(ins[3], k, width))], axis=1
        )

    grad_up_out = weight_grad(
        lay, pos, hidden + width, (0, 2), up_tile, (second, pre, middle_low, mixed),
        [whole(second), whole(pre), whole(middle_low), whole(mixed)],
        rows * dim * (gelu.shape[1] + dim),
    )

    mixed_grad = mixed_grad_call(lay, pos, middle_low, up_parts, hidden, width)
    dq, dk, dv, sums_qv = attend_back_call(pos, query, key, value, seg_k, seg_q, lse, mixed_grad)

    def qkv_tile(left, ins, k):
        late = left[0][:, rows:]
        return jnp.concatenate(
            [dot(late, ins[1][k]), dot(left[0], ins[2][k]), dot(left[0], ins[3][k])], axis=1
        )

    back, first_grad, sums1 = first_grad_call(
        lay, pos, dq, dk, dv, tokens_prev, tokens, qkv_parts, width
    )
    grad_qkv = weight_grad(
        lay, pos, 3 * width, (0,), qkv_tile, (first, dq, dk, dv),
        [whole(first), whole(dq), whole(dk), whole(dv)],
        rows * dim * dim * 5,
    )

    first_grad = first_grad + lax.ppermute(back, "tx", [(1, 0)]).astype(F32)
    unit, inverse = norm_parts(tokens.astype(F32))
    token_grad = (middle_grad + norm_backward(first_grad, unit, inverse, ln1_gain)).astype(BF)

    early = lax.psum(jnp.concatenate([sums2.reshape(-1), grad_b_up.reshape(-1)]), axes)
    late = lax.psum(jnp.concatenate([sums1.reshape(-1), sums_qv.reshape(-1)]), axes)
    return (
        result,
        token_grad,
        grad_qkv.reshape(lay.rows, 3, width),
        late[2 * dim :].reshape(2, -1),
        grad_up_out[:, hidden:],
        early[2 * dim : 3 * dim],
        grad_up_out[:, :hidden],
        early[4 * dim :],
        grad_w_down,
        early[3 * dim : 4 * dim],
        late[:dim],
        late[dim : 2 * dim],
        early[:dim],
        early[dim : 2 * dim],
    )


def solution(mesh):
    n_fsdp, n_tp = mesh.devices.shape
    fine = Mesh(
        mesh.devices.reshape(n_fsdp // 2, 2, n_tp // 2, 2), ("fy", "c", "tz", "tx")
    )
    fsdp, tp, every = ("fy", "c"), ("tz", "tx"), ("fy", "c", "tz", "tx")
    tile = P(fsdp, tp)
    ins = (
        P(every, None),
        P(fsdp, None),
        P(fsdp, None, tp),
        P(),
        tile,
        P(),
        tile,
        P(),
        tile,
        P(),
        P(),
        P(),
        P(),
        P(),
        P(every, None),
    )
    outs = (
        P(every, None),
        P(every, None),
        P(fsdp, None, tp),
        P(),
        tile,
        P(),
        tile,
        P(),
        tile,
        P(),
        P(),
        P(),
        P(),
        P(),
    )
    return jax.shard_map(
        functools.partial(per_device, (n_fsdp // 2, n_tp // 2)),
        mesh=fine,
        in_specs=ins,
        out_specs=outs,
        check_vma=False,
    )
```

```python
import functools

import jax
import jax.numpy as jnp
from jax import lax
from jax.experimental import pallas as pl
from jax.experimental.pallas import tpu as pltpu
from jax.sharding import Mesh, PartitionSpec as P

HEAD_DIM = 64
EPS = 1e-05
BF = jnp.bfloat16
F32 = jnp.float32
NT = (((1,), (1,)), ((), ()))
TN = (((0,), (0,)), ((), ()))
MIB = 1 << 20


def dot(a, b):
    return jnp.dot(a, b, preferred_element_type=F32)


def dot_nt(a, b):
    return lax.dot_general(a, b, NT, preferred_element_type=F32)


def dot_tn(a, b):
    return lax.dot_general(a, b, TN, preferred_element_type=F32)


def aligned(value, multiple):
    return pl.multiple_of(value, multiple)


class Layout:
    def __init__(self, ny, nz, rows):
        self.ny, self.nz, self.rows = ny, nz, rows
        self.near = nz // 2

    def row_start(self, pos, dy, dc):
        block = lax.bitwise_xor(pos[0], jnp.int32(dy)) * 2 + lax.bitwise_xor(pos[1], jnp.int32(dc))
        return pl.multiple_of(block * self.rows, self.rows)

    def z_block(self, pos, dz):
        return lax.bitwise_xor(pos[2], jnp.int32(dz))

    def x_block(self, pos, dx):
        return lax.bitwise_xor(pos[3], jnp.int32(dx))


def trade(value, axis, size, distance):
    return lax.ppermute(value, axis, [(s, s ^ distance) for s in range(size)])


def around(value, axis, size):
    return [value] + [trade(value, axis, size, d) for d in range(1, size)]


class Gather:
    def __init__(self, lay, shard):
        self.lay, self.top, self.low = lay, [shard], []

    def one(self):
        near = self.lay.near
        pieces = around(self.top[0], "tz", self.lay.nz)
        self.top, self.low = pieces[:near], pieces[near:]

    def two(self):
        self.top = around(jnp.stack(self.top), "tx", 2)
        self.low = around(jnp.stack(self.low), "fy", self.lay.ny)

    def three(self):
        self.top = around(jnp.stack(self.top), "fy", self.lay.ny)
        self.low = around(jnp.stack(self.low), "tx", 2)

    def swap(self, which):
        if which == 0:
            self.twin = [trade(self.top[0], "c", 2, 1), trade(self.low[0], "c", 2, 1)]
        else:
            late = [trade(t, "c", 2, 1) for t in self.top[1:] + self.low[1:]]
            ny = self.lay.ny
            self.parts = self.top + self.low + [
                self.twin[0], *late[: ny - 1], self.twin[1], *late[ny - 1 :]
            ]


def stage(*things):
    values = []
    for thing in things:
        values.append((thing.top, thing.low) if isinstance(thing, (Gather, Scatter)) else thing)
    values = lax.optimization_barrier(values)
    back = []
    for thing, value in zip(things, values):
        if isinstance(thing, (Gather, Scatter)):
            thing.top, thing.low = value
        else:
            back.append(value)
    return back[0] if len(back) == 1 else back


def start_loads(lay, pos, refs, wants, sem):
    for dz in range(lay.nz):
        for dx in range(2):
            k = lay.z_block(pos, dz) * 2 + lay.x_block(pos, dx)
            for dc in range(2):
                mine = refs[dc * (lay.ny + 2) : (dc + 1) * (lay.ny + 2)]
                for dy in range(lay.ny):
                    start = lay.row_start(pos, dy, dc)
                    if len(refs) == 1:
                        block = refs[0].at[start // lay.rows * (2 * lay.nz) + k]
                    elif dz < lay.near:
                        block = mine[dy].at[dx, dz]
                    else:
                        block = mine[lay.ny + dx].at[dy, dz - lay.near]
                    for i, (first, width, whole) in enumerate(wants):
                        pltpu.make_async_copy(
                            block.at[:, pl.ds(first, width)],
                            whole.at[pl.ds(start, lay.rows), pl.ds(aligned(k * width, width), width)],
                            sem.at[dz, i],
                        ).start()


def wait_loads(lay, pos, dz, wants, sem):
    for i, (first, width, whole) in enumerate(wants):
        start = lax.bitwise_xor(pos[2], jnp.int32(dz)) * (2 * width)
        cols = whole.at[:, pl.ds(aligned(start, width), 2 * width)]
        pltpu.make_async_copy(cols, cols, sem.at[dz, i]).wait()


def kernel_call(body, pos, grid, ins, in_specs, outs, out_specs, scratch, aliases={}):
    return pl.pallas_call(
        body,
        out_shape=outs,
        grid_spec=pltpu.PrefetchScalarGridSpec(
            num_scalar_prefetch=1,
            grid=grid,
            in_specs=in_specs,
            out_specs=out_specs,
            scratch_shapes=scratch,
        ),
        input_output_aliases=aliases,
        compiler_params=pltpu.CompilerParams(
            dimension_semantics=("arbitrary",) * len(grid), vmem_limit_bytes=60 * MIB
        ),
        cost_estimate=pl.CostEstimate(flops=1000, bytes_accessed=1000, transcendentals=0),
    )(pos, *ins)


def shape(dims, dtype):
    return jax.ShapeDtypeStruct(dims, dtype)


def full(dims):
    return pl.BlockSpec(dims, lambda *_: (0,) * len(dims))


def at_cols(rows, width, place=lambda k, pos: k):
    return pl.BlockSpec((rows, width), lambda k, pos: (0, place(k, pos)))


def at_lead(lead, *dims, place=lambda k, pos: k):
    return pl.BlockSpec((lead,) + dims, lambda k, pos: (place(k, pos),) + (0,) * len(dims))


def z_place(k, pos):
    return lax.bitwise_xor(pos[2], k)


ANY = pl.BlockSpec(memory_space=pl.ANY)


def norm_parts(values):
    centred = values - jnp.mean(values, axis=-1, keepdims=True)
    inverse = lax.rsqrt(jnp.mean(centred * centred, axis=-1, keepdims=True) + EPS)
    return centred * inverse, inverse


def norm_backward(grad, unit, inverse, gain):
    scaled = grad * gain
    return inverse * (
        scaled
        - jnp.mean(scaled, axis=-1, keepdims=True)
        - unit * jnp.mean(scaled * unit, axis=-1, keepdims=True)
    )


def qkv_call(lay, pos, first, bias_q, bias_v, weights, width):
    both, dim = first.shape
    rows = both // 2
    blocks = 2 * lay.nz
    n = len(weights)

    def body(pos_ref, first_ref, bq_ref, bv_ref, *rest):
        refs, (q_ref, k_ref, v_ref, whole_q, whole_kv, sem) = rest[:n], rest[n:]
        wants = ((0, width, whole_q), (width, 2 * width, whole_kv))
        dz = pl.program_id(0)

        @pl.when(dz == 0)
        def _():
            start_loads(lay, pos_ref, refs, wants, sem)

        wait_loads(lay, pos_ref, dz, wants, sem)
        z = z_place(dz, pos_ref)
        kv = dot(first_ref[...], whole_kv[:, pl.ds(aligned(z * 4 * width, width), 4 * width)])
        q = dot(first_ref[rows:], whole_q[:, pl.ds(aligned(z * 2 * width, width), 2 * width)])
        q = ((q + bq_ref[...]).astype(BF) * HEAD_DIM**-0.5).astype(BF)
        for x in range(2):
            q_ref[x] = q[:, x * width : (x + 1) * width]
            k_ref[x] = kv[:, 2 * x * width : (2 * x + 1) * width].astype(BF)
            bias = bv_ref[:, x * width : (x + 1) * width]
            v_ref[x] = (kv[:, (2 * x + 1) * width : (2 * x + 2) * width] + bias).astype(BF)

    return kernel_call(
        body,
        pos,
        (lay.nz,),
        (first, bias_q, bias_v, *weights),
        [full((both, dim)), at_cols(1, 2 * width, z_place), at_cols(1, 2 * width, z_place)] + [ANY] * n,
        [
            shape((blocks, rows, width), BF),
            shape((blocks, both, width), BF),
            shape((blocks, both, width), BF),
        ],
        [
            at_lead(2, rows, width, place=z_place),
            at_lead(2, both, width, place=z_place),
            at_lead(2, both, width, place=z_place),
        ],
        [
            pltpu.VMEM((dim, blocks * width), BF),
            pltpu.VMEM((dim, blocks * 2 * width), BF),
            pltpu.SemaphoreType.DMA((lay.nz, 2)),
        ],
    )


def mask_bias(seg_k, seg_q, rows):
    both = seg_k.shape[0]
    key_at = lax.broadcasted_iota(jnp.int32, (both, rows), 0) - (both - rows)
    query_at = lax.broadcasted_iota(jnp.int32, (both, rows), 1)
    return jnp.where((seg_k == seg_q) & (key_at <= query_at), 0.0, -1e30).astype(F32)


def head_only(block, head):
    lane = lax.broadcasted_iota(jnp.int32, block.shape, 1)
    inside = (lane >= head * HEAD_DIM) & (lane < (head + 1) * HEAD_DIM)
    return jnp.where(inside, block, jnp.zeros_like(block))


def attend_call(pos, query, key, value, seg_k, seg_q):
    blocks, both, width = key.shape
    rows = query.shape[1]
    heads = width // HEAD_DIM
    step = min(rows, 128)

    def body(pos_ref, q_ref, k_ref, v_ref, sk_ref, sq_ref, mixed_ref, exact_ref, lse_ref, bias):
        @pl.when(pl.program_id(0) == 0)
        def _():
            bias[...] = mask_bias(sk_ref[...], sq_ref[...], rows)

        for tile in range(rows // step):
            here = slice(tile * step, (tile + 1) * step)
            keys = both - rows + (tile + 1) * step
            outs = []
            for head in range(heads):
                scores = dot_nt(k_ref[0, :keys], head_only(q_ref[0, here], head)) + bias[:keys, here]
                top = jnp.max(scores, axis=0, keepdims=True)
                expo = jnp.exp(scores - top)
                total = jnp.sum(expo, axis=0, keepdims=True)
                share = jnp.broadcast_to(1.0 / total, (8, step)).T[:, :1]
                outs.append(dot_tn(expo.astype(BF), v_ref[0, :keys]) * share)
                lse_ref[0, head : head + 1, here] = top + jnp.log(total)
            lane = lax.broadcasted_iota(jnp.int32, outs[0].shape, 1)
            out = outs[0]
            for head in range(1, heads):
                out = jnp.where(lane < head * HEAD_DIM, out, outs[head])
            exact_ref[here] = out
            mixed_ref[here] = out.astype(BF)

    return kernel_call(
        body,
        pos,
        (blocks,),
        (query, key, value, seg_k, seg_q),
        [at_lead(1, rows, width), at_lead(1, both, width), at_lead(1, both, width), full((both, 1)), full((1, rows))],
        [
            shape((rows, blocks * width), BF),
            shape((rows, blocks * width), F32),
            shape((blocks, heads, rows), F32),
        ],
        [at_cols(rows, width), at_cols(rows, width), at_lead(1, heads, rows)],
        [pltpu.VMEM((both, rows), F32)],
    )


def branch_call(lay, pos, mixed, tokens, b_out, gain, shift, weights, first, width):
    rows, dim = tokens.shape
    blocks = 2 * lay.nz
    n = len(weights)

    def body(pos_ref, mixed_ref, tok_ref, bias_ref, gain_ref, shift_ref, *rest):
        refs, (middle_ref, second_ref, whole, sem) = rest[:n], rest[n:]
        wants = ((first, width, whole),)
        start_loads(lay, pos_ref, refs, wants, sem)
        for dz in range(lay.nz):
            wait_loads(lay, pos_ref, dz, wants, sem)
        branch = dot_nt(mixed_ref[...], whole[...])
        middle = tok_ref[...].astype(F32) + branch + bias_ref[...]
        middle_ref[...] = middle
        second_ref[...] = (norm_parts(middle)[0] * gain_ref[...] + shift_ref[...]).astype(BF)

    return kernel_call(
        body,
        pos,
        (),
        (mixed, tokens, b_out, gain, shift, *weights),
        [full(mixed.shape), full(tokens.shape)] + [full((1, dim))] * 3 + [ANY] * n,
        [shape((rows, dim), F32), shape((rows, dim), BF)],
        [full((rows, dim)), full((rows, dim))],
        [pltpu.VMEM((dim, blocks * width), BF), pltpu.SemaphoreType.DMA((lay.nz, 1))],
    )


def up_call(lay, pos, second, b_up, weights, width):
    rows, dim = second.shape
    blocks = 2 * lay.nz
    n = len(weights)

    def body(pos_ref, second_ref, bias_ref, *rest):
        refs, (gelu_ref, slope_ref, whole, sem) = rest[:n], rest[n:]
        wants = ((0, width, whole),)
        dz = pl.program_id(0)

        @pl.when(dz == 0)
        def _():
            start_loads(lay, pos_ref, refs, wants, sem)

        wait_loads(lay, pos_ref, dz, wants, sem)
        z = z_place(dz, pos_ref)
        for x in range(2):
            here = slice(x * width, (x + 1) * width)
            cols = pl.ds(aligned((z * 2 + x) * width, width), width)
            u = dot(second_ref[...], whole[:, cols]) + bias_ref[:, here]
            scale = 0.7978845608028654
            square = u * u
            half = 0.5 + 0.5 * jnp.tanh(u * (scale + (scale * 0.044715) * square))
            gelu = u * half
            gelu_ref[:, here] = gelu.astype(BF)
            bend = 2.0 * scale + (6.0 * scale * 0.044715) * square
            slope_ref[:, here] = (half + gelu * (1.0 - half) * bend).astype(BF)

    return kernel_call(
        body,
        pos,
        (lay.nz,),
        (second, b_up, *weights),
        [full(second.shape), at_cols(1, 2 * width, z_place)] + [ANY] * n,
        [shape((rows, blocks * width), BF)] * 2,
        [at_cols(rows, 2 * width, z_place)] * 2,
        [pltpu.VMEM((dim, blocks * width), BF), pltpu.SemaphoreType.DMA((lay.nz, 1))],
    )


def result_call(lay, pos, gelu, middle, b_down, weights, width):
    rows, dim = middle.shape
    blocks = 2 * lay.nz
    n = len(weights)

    def body(pos_ref, gelu_ref, middle_ref, bias_ref, *rest):
        refs, (result_ref, whole, acc, sem) = rest[:n], rest[n:]
        wants = ((0, width, whole),)
        dz = pl.program_id(0)

        @pl.when(dz == 0)
        def _():
            start_loads(lay, pos_ref, refs, wants, sem)
            acc[...] = middle_ref[...] + bias_ref[...]

        wait_loads(lay, pos_ref, dz, wants, sem)
        cols = pl.ds(aligned(z_place(dz, pos_ref) * 2 * width, width), 2 * width)
        acc[...] += dot_nt(gelu_ref[...], whole[:, cols])

        @pl.when(dz == lay.nz - 1)
        def _():
            result_ref[...] = acc[...].astype(BF)

    return kernel_call(
        body,
        pos,
        (lay.nz,),
        (gelu, middle, b_down, *weights),
        [at_cols(rows, 2 * width, z_place), full((rows, dim)), full((1, dim))] + [ANY] * n,
        [shape((rows, dim), BF)],
        [full((rows, dim))],
        [
            pltpu.VMEM((dim, blocks * width), BF),
            pltpu.VMEM((rows, dim), F32),
            pltpu.SemaphoreType.DMA((lay.nz, 1)),
        ],
    )[0]


def pre_call(lay, pos, slope, grad, weights, width):
    rows, dim = grad.shape
    blocks = 2 * lay.nz
    n = len(weights)

    def body(pos_ref, slope_ref, grad_ref, *rest):
        refs, (pre_ref, hidden_ref, whole, sem) = rest[:n], rest[n:]
        wants = ((0, width, whole),)
        dz = pl.program_id(0)

        @pl.when(dz == 0)
        def _():
            start_loads(lay, pos_ref, refs, wants, sem)

        wait_loads(lay, pos_ref, dz, wants, sem)
        cols = pl.ds(aligned(z_place(dz, pos_ref) * 2 * width, width), 2 * width)
        pre = (dot(grad_ref[...], whole[:, cols]) * slope_ref[...].astype(F32)).astype(BF)
        pre_ref[...] = pre
        hidden_ref[...] = jnp.sum(pre.astype(F32), axis=0, keepdims=True)

    return kernel_call(
        body,
        pos,
        (lay.nz,),
        (slope, grad, *weights),
        [at_cols(rows, 2 * width, z_place), full((rows, dim))] + [ANY] * n,
        [shape((rows, blocks * width), BF), shape((1, blocks * width), F32)],
        [at_cols(rows, 2 * width, z_place), at_cols(1, 2 * width, z_place)],
        [pltpu.VMEM((dim, blocks * width), BF), pltpu.SemaphoreType.DMA((lay.nz, 1))],
    )


def second_back_call(lay, pos, pre, grad, middle, gain, weights, width):
    rows, dim = middle.shape
    blocks = 2 * lay.nz
    n = len(weights)

    def body(pos_ref, pre_ref, grad_ref, middle_ref, gain_ref, *rest):
        refs, (mgrad_ref, low_ref, sums_ref, whole, acc, sem) = rest[:n], rest[n:]
        wants = ((0, width, whole),)
        dz = pl.program_id(0)

        @pl.when(dz == 0)
        def _():
            start_loads(lay, pos_ref, refs, wants, sem)
            acc[...] = jnp.zeros_like(acc)

        wait_loads(lay, pos_ref, dz, wants, sem)
        cols = pl.ds(aligned(z_place(dz, pos_ref) * 2 * width, width), 2 * width)
        acc[...] += dot_nt(pre_ref[...], whole[:, cols])

        @pl.when(dz == lay.nz - 1)
        def _():
            unit, inverse = norm_parts(middle_ref[...])
            second_grad = acc[...]
            sums_ref[0:1] = jnp.sum(second_grad * unit, axis=0, keepdims=True)
            sums_ref[1:2] = jnp.sum(second_grad, axis=0, keepdims=True)
            out = grad_ref[...].astype(F32)
            sums_ref[3:4] = jnp.sum(out, axis=0, keepdims=True)
            out = out + norm_backward(second_grad, unit, inverse, gain_ref[...])
            sums_ref[2:3] = jnp.sum(out, axis=0, keepdims=True)
            mgrad_ref[...] = out
            low_ref[...] = out.astype(BF)

    return kernel_call(
        body,
        pos,
        (lay.nz,),
        (pre, grad, middle, gain, *weights),
        [at_cols(rows, 2 * width, z_place)] + [full((rows, dim))] * 2 + [full((1, dim))] + [ANY] * n,
        [shape((rows, dim), F32), shape((rows, dim), BF), shape((4, dim), F32)],
        [full((rows, dim))] * 2 + [full((4, dim))],
        [
            pltpu.VMEM((dim, blocks * width), BF),
            pltpu.VMEM((rows, dim), F32),
            pltpu.SemaphoreType.DMA((lay.nz, 1)),
        ],
    )


def mixed_grad_call(lay, pos, low, weights, first, width):
    rows, dim = low.shape
    blocks = 2 * lay.nz
    n = len(weights)

    def body(pos_ref, low_ref, *rest):
        refs, (out_ref, whole, sem) = rest[:n], rest[n:]
        wants = ((first, width, whole),)
        start_loads(lay, pos_ref, refs, wants, sem)
        for dz in range(lay.nz):
            wait_loads(lay, pos_ref, dz, wants, sem)
        out_ref[...] = dot(low_ref[...], whole[...]).astype(BF)

    return kernel_call(
        body,
        pos,
        (),
        (low, *weights),
        [full((rows, dim))] + [ANY] * n,
        [shape((rows, blocks * width), BF)],
        [full((rows, blocks * width))],
        [pltpu.VMEM((dim, blocks * width), BF), pltpu.SemaphoreType.DMA((lay.nz, 1))],
    )[0]


def attend_back_call(pos, span, query, key, value, seg_k, seg_q, lse, mixed_grad, exact, earlier=()):
    blocks, both, width = key.shape
    rows = query.shape[1]
    heads = width // HEAD_DIM
    step = min(rows, 256)
    begin = span[0]
    n = len(earlier)

    def body(pos_ref, q_ref, k_ref, v_ref, sk_ref, sq_ref, lse_ref, grad_ref, exact_ref, *rest):
        dq_ref, dk_ref, dv_ref, sums_ref, bias, dq_t, dk, dv = rest[n:]

        @pl.when(pl.program_id(0) == 0)
        def _():
            bias[...] = mask_bias(sk_ref[...], sq_ref[...], rows)

        key_t = k_ref[0].T
        inner_t = (grad_ref[...].astype(F32) * exact_ref[...]).T
        dk[...] = jnp.zeros_like(dk)
        dv[...] = jnp.zeros_like(dv)
        for tile in range(rows // step):
            here = slice(tile * step, (tile + 1) * step)
            keys = both - rows + (tile + 1) * step
            for head in range(heads):
                lanes = slice(head * HEAD_DIM, (head + 1) * HEAD_DIM)
                q_head = head_only(q_ref[0, here], head)
                g_head = head_only(grad_ref[here], head)
                scores = dot_nt(k_ref[0, :keys], q_head) + bias[:keys, here]
                probs = jnp.exp(scores - lse_ref[0, head : head + 1, here])
                prob_grad = dot_nt(v_ref[0, :keys], g_head)
                inner = jnp.sum(inner_t[lanes, here], axis=0, keepdims=True)
                score_grad = (probs * (prob_grad - inner)).astype(BF)
                dv[:keys] += dot(probs.astype(BF), g_head)
                dk[:keys] += dot(score_grad, q_head)
                dq_t[lanes, here] = dot(key_t[lanes, :keys], score_grad)
        dq = (dq_t[...].T * HEAD_DIM**-0.5).astype(BF)
        dv_low = dv[...].astype(BF)
        dq_ref[0] = dq
        dk_ref[0] = dk[...].astype(BF)
        dv_ref[0] = dv_low
        sums_ref[0:1] = jnp.sum(dq.astype(F32), axis=0, keepdims=True)
        sums_ref[1:2] = jnp.sum(dv_low.astype(F32), axis=0, keepdims=True)

    at = lambda k, pos: k + begin
    return kernel_call(
        body,
        pos,
        (span[1] - span[0],),
        (query, key, value, seg_k, seg_q, lse, mixed_grad, exact, *earlier),
        [
            at_lead(1, rows, width, place=at),
            at_lead(1, both, width, place=at),
            at_lead(1, both, width, place=at),
            full((both, 1)),
            full((1, rows)),
            at_lead(1, heads, rows, place=at),
            at_cols(rows, width, at),
            at_cols(rows, width, at),
        ]
        + [ANY] * n,
        [
            shape((blocks, rows, width), BF),
            shape((blocks, both, width), BF),
            shape((blocks, both, width), BF),
            shape((2, blocks * width), F32),
        ],
        [
            at_lead(1, rows, width, place=at),
            at_lead(1, both, width, place=at),
            at_lead(1, both, width, place=at),
            at_cols(2, width, at),
        ],
        [
            pltpu.VMEM((both, rows), F32),
            pltpu.VMEM((width, rows), F32),
            pltpu.VMEM((both, width), F32),
            pltpu.VMEM((both, width), F32),
        ],
        {9: 0, 10: 1, 11: 2, 12: 3} if n else {},
    )


def sides(ref, which, rows):
    here = slice(0, rows) if which == 0 else slice(rows, 2 * rows)
    return [ref[x, here] for x in range(2)]


def first_grad_prev_call(lay, pos, dk, dv, tokens, weights, width):
    rows, dim = tokens.shape
    blocks = 2 * lay.nz
    n = len(weights)

    def body(pos_ref, dk_ref, dv_ref, tok_ref, *rest):
        refs, (grad_ref, sums_ref, whole, acc, sem) = rest[:n], rest[n:]
        wants = ((width, 2 * width, whole),)
        dz = pl.program_id(0)

        @pl.when(dz == 0)
        def _():
            start_loads(lay, pos_ref, refs, wants, sem)
            acc[...] = jnp.zeros_like(acc)

        wait_loads(lay, pos_ref, dz, wants, sem)
        keys, values = sides(dk_ref, 0, rows), sides(dv_ref, 0, rows)
        part = jnp.concatenate([keys[0], values[0], keys[1], values[1]], axis=1)
        cols = pl.ds(aligned(z_place(dz, pos_ref) * 4 * width, width), 4 * width)
        acc[...] += dot_nt(part, whole[:, cols])

        @pl.when(dz == lay.nz - 1)
        def _():
            grad = acc[...]
            grad_ref[...] = grad.astype(BF)
            unit = norm_parts(tok_ref[...].astype(F32))[0]
            sums_ref[0:1] = jnp.sum(grad * unit, axis=0, keepdims=True)
            sums_ref[1:2] = jnp.sum(grad, axis=0, keepdims=True)

    both = at_lead(2, rows, width, place=z_place)
    return kernel_call(
        body,
        pos,
        (lay.nz,),
        (dk, dv, tokens, *weights),
        [both, both, full((rows, dim))] + [ANY] * n,
        [shape((rows, dim), BF), shape((2, dim), F32)],
        [full((rows, dim)), full((2, dim))],
        [
            pltpu.VMEM((dim, blocks * 2 * width), BF),
            pltpu.VMEM((rows, dim), F32),
            pltpu.SemaphoreType.DMA((lay.nz, 1)),
        ],
    )


def first_grad_own_call(lay, pos, dq, dk, dv, tokens, weights, width):
    rows, dim = tokens.shape
    blocks = 2 * lay.nz
    n = len(weights)

    def body(pos_ref, dq_ref, dk_ref, dv_ref, tok_ref, *rest):
        refs, (grad_ref, sums_ref, whole_q, whole_kv, sem) = rest[:n], rest[n:]
        wants = ((0, width, whole_q), (width, 2 * width, whole_kv))
        dz = pl.program_id(0)

        @pl.when(dz == 0)
        def _():
            start_loads(lay, pos_ref, refs, wants, sem)
            grad_ref[...] = jnp.zeros_like(grad_ref)

        wait_loads(lay, pos_ref, dz, wants, sem)
        z = z_place(dz, pos_ref)
        keys, values = sides(dk_ref, 1, rows), sides(dv_ref, 1, rows)
        part = jnp.concatenate([keys[0], values[0], keys[1], values[1]], axis=1)
        more = dot_nt(part, whole_kv[:, pl.ds(aligned(z * 4 * width, width), 4 * width)])
        part = jnp.concatenate([dq_ref[0], dq_ref[1]], axis=1)
        more += dot_nt(part, whole_q[:, pl.ds(aligned(z * 2 * width, width), 2 * width)])
        grad_ref[...] += more

        @pl.when(dz == lay.nz - 1)
        def _():
            grad = grad_ref[...]
            unit = norm_parts(tok_ref[...].astype(F32))[0]
            sums_ref[0:1] = jnp.sum(grad * unit, axis=0, keepdims=True)
            sums_ref[1:2] = jnp.sum(grad, axis=0, keepdims=True)

    both = at_lead(2, 2 * rows, width, place=z_place)
    return kernel_call(
        body,
        pos,
        (lay.nz,),
        (dq, dk, dv, tokens, *weights),
        [at_lead(2, rows, width, place=z_place), both, both, full((rows, dim))] + [ANY] * n,
        [shape((rows, dim), F32), shape((2, dim), F32)],
        [full((rows, dim)), full((2, dim))],
        [
            pltpu.VMEM((dim, blocks * width), BF),
            pltpu.VMEM((dim, blocks * 2 * width), BF),
            pltpu.SemaphoreType.DMA((lay.nz, 2)),
        ],
    )


def half_grad_call(lay, pos, *, half, columns, lefts, tile, operands, specs, received):
    ny, nz, near, rows = lay.ny, lay.nz, lay.near, lay.rows
    n = len(operands)

    def body(pos_ref, *refs):
        ins, rest = refs[:n], refs[n:]
        got, rest = (rest[0], rest[1:]) if half == 0 else (None, rest)
        count = ny + 2 if half == 0 else 1
        outs, turned, spare = rest[:count], rest[count : count + len(lefts)], rest[count + len(lefts) :]
        dz = pl.program_id(0)

        @pl.when(dz == 0)
        def _():
            for index, ref in zip(lefts, turned):
                if rows % 128:
                    spare[0][...] = ins[index][...].T
                for dy in range(ny):
                    span = pl.ds(lay.row_start(pos_ref, dy, half), rows)
                    piece = spare[0][span] if rows % 128 else ins[index][:, span].T
                    ref[dy * rows : (dy + 1) * rows] = piece

        def make(put):
            blocks = tile(turned, ins, [lay.x_block(pos_ref, dx) for dx in range(2)])
            for dx in range(2):
                for dy in range(ny):
                    block = blocks[dx][dy * rows : (dy + 1) * rows]
                    if half == 0:
                        block = block + got[0, dx, dy].astype(F32)
                    put(dx, dy, block.astype(BF))

        if half == 1:

            def put(dx, dy, block):
                outs[0][0, dx, dy] = block

            make(put)
            return

        @pl.when(dz < near)
        def _():
            def put(dx, dy, block):
                outs[dy][0, dx] = block

            make(put)

        @pl.when(dz >= near)
        def _():
            def put(dx, dy, block):
                outs[ny + dx][0, dy] = block

            make(put)

    def step(*dims, at=lambda dz: dz):
        return pl.BlockSpec((1,) + dims, lambda dz, pos: (at(dz),) + (0,) * len(dims))

    if half == 0:
        operands = (*operands, received)
        specs = [*specs, step(2, ny, rows, columns)]
        outs = [shape((near, 2, rows, columns), BF)] * ny + [shape((nz - near, ny, rows, columns), BF)] * 2
        out_specs = [step(2, rows, columns, at=lambda dz: jnp.minimum(dz, near - 1))] * ny
        out_specs += [step(ny, rows, columns, at=lambda dz: jnp.maximum(dz - near, 0))] * 2
    else:
        outs = [shape((nz, 2, ny, rows, columns), BF)]
        out_specs = [step(2, ny, rows, columns)]
    scratch = [pltpu.VMEM((ny * rows, operands[index].shape[0]), BF) for index in lefts]
    if rows % 128:
        scratch.append(pltpu.VMEM(operands[lefts[0]].shape[::-1], BF))
    return kernel_call(body, pos, (nz,), operands, specs, outs, out_specs, scratch)


def sum_call(pos, groups, outs, build, steps=1):
    cut = lambda dims: (dims[0] // steps,) + dims[1:]
    spec = lambda r: pl.BlockSpec(cut(r.shape), lambda k, pos: (k,) + (0,) * (len(r.shape) - 1))
    flat = [r for g in groups for r in g]

    def body(pos_ref, *refs):
        ins, given = refs[: len(flat)], refs[len(flat) :]
        at, sums = 0, []
        for g in groups:
            mine = ins[at : at + len(g)]
            at += len(g)
            sums.append(lambda index, mine=mine: sum(
                (r[index].astype(F32) for r in mine[1:]), mine[0][index].astype(F32)
            ))
        build(sums, given)

    return kernel_call(
        body, pos, (steps,), flat, [spec(r) for r in flat], outs, [spec(o) for o in outs], []
    )


class Scatter:
    def __init__(self, lay, pos, columns, lefts, tile, operands, specs):
        self.lay, self.pos, self.columns = lay, pos, columns
        self.half = functools.partial(
            half_grad_call, lay, pos, columns=columns, lefts=lefts, tile=tile, operands=operands,
            specs=specs,
        )

    def away(self):
        self.sent = self.half(half=1, received=None)[0]

    def swap(self):
        self.received = trade(self.sent, "c", 2, 1)

    def own(self):
        parts = self.half(half=0, received=self.received)
        self.top, self.low = parts[: self.lay.ny], parts[self.lay.ny :]

    def send_one(self):
        self.top = [self.top[0]] + [trade(self.top[d], "fy", self.lay.ny, d) for d in range(1, self.lay.ny)]
        self.low = [self.low[0], trade(self.low[1], "tx", 2, 1)]

    def sum_one(self):
        ny, rows, near, far = self.lay.ny, self.lay.rows, self.lay.near, self.lay.nz - self.lay.near

        def build(sums, given):
            for dx in range(2):
                given[dx][...] = sums[0]((slice(None), dx)).astype(BF)
            for dy in range(ny):
                given[2 + dy][...] = sums[1]((slice(None), dy)).astype(BF)

        outs = [shape((near, rows, self.columns), BF)] * 2 + [shape((far, rows, self.columns), BF)] * ny
        out = sum_call(self.pos, [self.top, self.low], outs, build, near if near == far else 1)
        self.top, self.low = out[:2], out[2:]

    def send_two(self):
        self.top = [self.top[0], trade(self.top[1], "tx", 2, 1)]
        self.low = [self.low[0]] + [trade(self.low[d], "fy", self.lay.ny, d) for d in range(1, self.lay.ny)]

    def sum_two(self):
        near, nz = self.lay.near, self.lay.nz

        def build(sums, given):
            for dz in range(nz):
                given[dz][...] = (sums[0](dz) if dz < near else sums[1](dz - near)).astype(BF)

        outs = [shape((self.lay.rows, self.columns), BF)] * nz
        self.top = sum_call(self.pos, [self.top, self.low], outs, build)
        self.low = []

    def send_three(self):
        self.top = [self.top[0]] + [trade(self.top[d], "tz", self.lay.nz, d) for d in range(1, self.lay.nz)]

    def sum_three(self, cuts):
        outs = [shape((self.lay.rows, *c) if isinstance(c, tuple) else (self.lay.rows, c), F32) for c in cuts]

        def build(sums, given):
            at = 0
            for ref, c in zip(given, cuts):
                if isinstance(c, tuple):
                    for i in range(c[0]):
                        ref[:, i, :] = sums[0]((slice(None), slice(at, at + c[1])))
                        at += c[1]
                else:
                    ref[...] = sums[0]((slice(None), slice(at, at + c)))
                    at += c

        self.out = sum_call(self.pos, [self.top], outs, build)


def per_device(
    sizes,
    tokens,
    segment_ids,
    w_qkv,
    b_qv,
    w_out,
    b_out,
    w_up,
    b_up,
    w_down,
    b_down,
    ln1_gain,
    ln1_shift,
    ln2_gain,
    ln2_shift,
    grad_out,
):
    ny, nz = sizes
    rows, dim = tokens.shape
    length = segment_ids.shape[1]
    width = w_qkv.shape[2]
    hidden = w_up.shape[1]
    lay = Layout(ny, nz, w_qkv.shape[0])
    axes = ("fy", "c", "tz", "tx")
    pos = jnp.stack([lax.axis_index(axis) for axis in axes]).astype(jnp.int32)
    row = lambda v: v.reshape(1, -1)

    blocks = 2 * nz
    half = nz
    up_parts = [lax.all_gather(jnp.concatenate([w_up, w_out], axis=1), axes, axis=0, tiled=False)]
    qkv = Gather(lay, w_qkv.reshape(lay.rows, 3 * width))
    down = Gather(lay, w_down)
    qkv.one()
    tokens_prev = lax.ppermute(tokens, "tx", [(0, 1)])
    qkv.low, tokens_prev = stage(qkv.low, tokens_prev)
    qkv.two()
    qkv.three()
    qkv.swap(0)

    sequence = (pos[2] * 2 + pos[3]) // 2
    later = pos[3] > 0
    ids = lax.dynamic_slice_in_dim(segment_ids, sequence, 1, 0)
    seg_q = jnp.where(later, ids[:, rows:], ids[:, :rows])
    seg_prev = jnp.where(later, ids[:, :rows], -1)
    seg_k = jnp.concatenate([seg_prev, seg_q], axis=1).reshape(length, 1)
    both = jnp.concatenate([tokens_prev, tokens], axis=0).astype(F32)
    first = (norm_parts(both)[0] * ln1_gain + ln1_shift).astype(BF)
    first, seg_k, seg_q = stage(qkv, down, first, seg_k, seg_q)
    qkv.swap(1)
    down.one()
    qkv.parts, first = stage(qkv.parts, first)
    query, key, value = qkv_call(lay, pos, first, b_qv[0:1], b_qv[1:2], qkv.parts, width)
    mixed, exact, lse = attend_call(pos, query, key, value, seg_k, seg_q)
    mixed, up_parts = stage(down, mixed, up_parts)
    down.two()
    middle, second = branch_call(
        lay, pos, mixed, tokens, row(b_out), row(ln2_gain), row(ln2_shift), up_parts, hidden, width
    )
    middle, second = stage(down, middle, second)
    down.three()
    down.swap(0)
    gelu, slope = up_call(lay, pos, second, row(b_up), up_parts, hidden)

    whole = lambda v: full(v.shape)
    at_z = lambda size: at_cols(rows, 2 * size, z_place)
    block = lambda ref, x, size: ref[:, pl.ds(aligned(x * size, size), size)]

    def down_tile(left, ins, xs):
        return [dot(left[0][...], block(ins[1], x, hidden)) for x in xs]

    grad_down = Scatter(
        lay, pos, hidden, (0,), down_tile, (grad_out, gelu), [whole(grad_out), at_z(hidden)]
    )
    grad_down.away()
    grad_down.swap()
    grad_down.own()
    slope = stage(grad_down, down, slope)
    down.swap(1)
    grad_down.send_one()
    pre, grad_b_up = pre_call(lay, pos, slope, grad_out, down.parts, hidden)
    middle_grad, middle_low, sums2 = second_back_call(
        lay, pos, pre, grad_out, middle, row(ln2_gain), up_parts, hidden
    )

    def up_tile(left, ins, xs):
        return [
            jnp.concatenate(
                [dot(left[0][...], block(ins[1], x, hidden)), dot(left[1][...], block(ins[3], x, width))],
                axis=1,
            )
            for x in xs
        ]

    grad_up = Scatter(
        lay, pos, hidden + width, (0, 2), up_tile, (second, pre, middle_low, mixed),
        [whole(second), at_z(hidden), whole(middle_low), at_z(width)],
    )
    mixed_grad = mixed_grad_call(lay, pos, middle_low, up_parts, hidden, width)
    grad_up.away()
    grad_up.sent, mixed_grad = stage(grad_down, grad_up.sent, mixed_grad)
    grad_down.sum_one()
    grad_up.sent, mixed_grad = stage(grad_down, grad_up.sent, mixed_grad)
    grad_down.send_two()
    grad_up.swap()
    partial = attend_back_call(pos, (0, half), query, key, value, seg_k, seg_q, lse, mixed_grad, exact)
    partial, grad_up.received = stage(grad_down, partial, grad_up.received)
    grad_down.sum_two()
    grad_up.own()
    partial = stage(grad_up, grad_down, partial)
    grad_up.send_one()
    grad_down.send_three()
    dq, dk, dv, sums_qv = attend_back_call(
        pos, (half, blocks), query, key, value, seg_k, seg_q, lse, mixed_grad, exact, partial
    )
    back, sums_prev = first_grad_prev_call(lay, pos, dk, dv, tokens_prev, qkv.parts, width)

    def qkv_tile(left, ins, xs):
        late = left[0][:, rows:]
        q = dot(late, jnp.concatenate([ins[1][x] for x in xs], axis=1))
        out = []
        for i, x in enumerate(xs):
            kv = dot(left[0][...], jnp.concatenate([ins[2][x], ins[3][x]], axis=1))
            out.append(jnp.concatenate([q[:, i * width : (i + 1) * width], kv], axis=1))
        return out

    grad_qkv = Scatter(
        lay, pos, 3 * width, (0,), qkv_tile, (first, dq, dk, dv),
        [
            whole(first),
            at_lead(2, rows, width, place=z_place),
            at_lead(2, 2 * rows, width, place=z_place),
            at_lead(2, 2 * rows, width, place=z_place),
        ],
    )
    grad_qkv.away()
    grad_qkv.sent, dq, dk, dv = stage(grad_up, grad_down, grad_qkv.sent, dq, dk, dv)
    grad_up.sum_one()
    grad_qkv.sent, dq, dk, dv = stage(grad_up, grad_qkv.sent, dq, dk, dv)
    grad_up.send_two()
    grad_qkv.swap()
    grad_down.sum_three((hidden,))
    grad_qkv.received, dq, dk, dv, grad_down.out = stage(grad_qkv.received, dq, dk, dv, grad_down.out)
    grad_qkv.own()
    dq, dk, dv, sums_prev = stage(grad_qkv, dq, dk, dv, sums_prev)
    grad_qkv.send_one()
    dq, dk, dv, sums_prev = stage(grad_up, dq, dk, dv, sums_prev)
    grad_up.sum_two()
    dq, dk, dv, sums_prev = stage(grad_up, dq, dk, dv, sums_prev)
    grad_up.send_three()
    first_grad, sums1 = first_grad_own_call(lay, pos, dq, dk, dv, tokens, qkv.parts, width)
    small = jnp.concatenate(
        [v.reshape(-1) for v in (sums2, grad_b_up, sums1 + sums_prev, sums_qv)]
    ).reshape(-1, 128)
    small = small + trade(small, "c", 2, 1)
    result = result_call(lay, pos, gelu, middle, row(b_down), down.parts, hidden)
    first_grad, small, result, back = stage(grad_qkv, first_grad, small, result, back)
    grad_qkv.sum_one()
    first_grad, small, back = stage(grad_qkv, first_grad, small, back)
    small = small + trade(small, "tx", 2, 1)
    grad_qkv.send_two()
    small, back = stage(small, back)
    back = lax.ppermute(back, "tx", [(1, 0)])
    small = sum(around(small, "fy", ny))
    small = stage(grad_up, small)
    grad_up.sum_three((hidden, width))
    small, grad_up.out = stage(grad_qkv, small, grad_up.out)
    grad_qkv.sum_two()
    small = stage(grad_qkv, small)
    small = around(small, "tz", nz)
    grad_qkv.send_three()
    back = stage(grad_qkv, back)
    small = sum(small).reshape(-1)
    grad_qkv.sum_three(((3, width),))
    unit, inverse = norm_parts(tokens.astype(F32))
    first_grad = first_grad + back.astype(F32)
    token_grad = (middle_grad + norm_backward(first_grad, unit, inverse, ln1_gain)).astype(BF)
    at = 4 * dim
    late = small[at + gelu.shape[1] :]
    return (
        result,
        token_grad,
        grad_qkv.out[0],
        late[2 * dim :].reshape(2, -1),
        grad_up.out[1],
        small[2 * dim : 3 * dim],
        grad_up.out[0],
        small[at : at + gelu.shape[1]],
        grad_down.out[0],
        small[3 * dim : at],
        late[:dim],
        late[dim : 2 * dim],
        small[:dim],
        small[dim : 2 * dim],
    )


def solution(mesh):
    n_fsdp, n_tp = mesh.devices.shape
    fine = Mesh(
        mesh.devices.reshape(n_fsdp // 2, 2, n_tp // 2, 2), ("fy", "c", "tz", "tx")
    )
    fsdp, tp, every = ("fy", "c"), ("tz", "tx"), ("fy", "c", "tz", "tx")
    tile = P(fsdp, tp)
    ins = (
        P(every, None),
        P(fsdp, None),
        P(fsdp, None, tp),
        P(),
        tile,
        P(),
        tile,
        P(),
        tile,
        P(),
        P(),
        P(),
        P(),
        P(),
        P(every, None),
    )
    outs = (
        P(every, None),
        P(every, None),
        P(fsdp, None, tp),
        P(),
        tile,
        P(),
        tile,
        P(),
        tile,
        P(),
        P(),
        P(),
        P(),
        P(),
    )
    return jax.shard_map(
        functools.partial(per_device, (n_fsdp // 2, n_tp // 2)),
        mesh=fine,
        in_specs=ins,
        out_specs=outs,
        check_vma=False,
    )
```

```python
import functools

import jax
import jax.numpy as jnp
from jax import lax
from jax.experimental import pallas as pl
from jax.experimental.pallas import tpu as pltpu
from jax.sharding import Mesh, PartitionSpec as P

HEAD_DIM = 64
EPS = 1e-05
BF = jnp.bfloat16
F32 = jnp.float32
NT = (((1,), (1,)), ((), ()))
TN = (((0,), (0,)), ((), ()))
MIB = 1 << 20


def dot(a, b):
    return jnp.dot(a, b, preferred_element_type=F32)


def dot_nt(a, b):
    return lax.dot_general(a, b, NT, preferred_element_type=F32)


def dot_tn(a, b):
    return lax.dot_general(a, b, TN, preferred_element_type=F32)


def aligned(value, multiple):
    return pl.multiple_of(value, multiple)


class Layout:
    def __init__(self, ny, nz, rows):
        self.ny, self.nz, self.rows = ny, nz, rows
        self.near = nz // 2

    def row_start(self, pos, dy, dc):
        block = lax.bitwise_xor(pos[0], jnp.int32(dy)) * 2 + lax.bitwise_xor(pos[1], jnp.int32(dc))
        return pl.multiple_of(block * self.rows, self.rows)

    def z_block(self, pos, dz):
        return lax.bitwise_xor(pos[2], jnp.int32(dz))

    def x_block(self, pos, dx):
        return lax.bitwise_xor(pos[3], jnp.int32(dx))


def trade(value, axis, size, distance):
    return lax.ppermute(value, axis, [(s, s ^ distance) for s in range(size)])


def around(value, axis, size):
    return [value] + [trade(value, axis, size, d) for d in range(1, size)]


class Gather:
    def __init__(self, lay, shard):
        self.lay, self.top, self.low = lay, [shard], []

    def one(self):
        near = self.lay.near
        pieces = around(self.top[0], "tz", self.lay.nz)
        self.top, self.low = pieces[:near], pieces[near:]

    def two(self):
        lay = self.lay
        self.top = around(jnp.stack(self.top), "tx", 2)
        self.low = around(jnp.stack(self.low), "fy", lay.ny)

    def three(self):
        lay = self.lay
        self.top = around(jnp.stack(self.top), "fy", lay.ny)
        self.low = around(jnp.stack(self.low), "tx", 2)

    def swap(self, which):
        if which == 0:
            self.twin = [trade(self.top[0], "c", 2, 1), trade(self.low[0], "c", 2, 1)]
        else:
            late = [trade(t, "c", 2, 1) for t in self.top[1:] + self.low[1:]]
            n = len(self.top) - 1
            self.parts = self.top + self.low + [self.twin[0], *late[:n], self.twin[1], *late[n:]]


def stage(*things):
    values = []
    for thing in things:
        values.append((thing.top, thing.low) if isinstance(thing, (Gather, Scatter)) else thing)
    values = lax.optimization_barrier(values)
    back = []
    for thing, value in zip(things, values):
        if isinstance(thing, (Gather, Scatter)):
            thing.top, thing.low = value
        else:
            back.append(value)
    return back[0] if len(back) == 1 else back


def start_loads(lay, pos, refs, wants, sem, dz):
    half = len(refs) // 2
    for dx in range(2):
        k = lay.z_block(pos, dz) * 2 + lay.x_block(pos, dx)
        for dc in range(2):
            mine = refs[dc * half : (dc + 1) * half]
            for dy in range(lay.ny):
                start = lay.row_start(pos, dy, dc)
                if len(refs) == 1:
                    block = refs[0].at[start // lay.rows * (2 * lay.nz) + k]
                elif dz < lay.near:
                    block = mine[dy].at[dx, dz]
                else:
                    block = mine[lay.ny + dx].at[dy, dz - lay.near]
                for i, (first, width, whole) in enumerate(wants):
                    pltpu.make_async_copy(
                        block.at[:, pl.ds(first, width)],
                        whole.at[pl.ds(start, lay.rows), pl.ds(aligned(k * width, width), width)],
                        sem.at[dz, i],
                    ).start()


def stream_loads(lay, pos, refs, wants, sem):
    step = pl.program_id(0)
    for dz in range(lay.nz):

        @pl.when(step == max(dz - 2, 0))
        def _(dz=dz):
            start_loads(lay, pos, refs, wants, sem, dz)

    wait_loads(lay, pos, step, wants, sem)


def all_loads(lay, pos, refs, wants, sem):
    for dz in range(lay.nz):
        start_loads(lay, pos, refs, wants, sem, dz)
    for dz in range(lay.nz):
        wait_loads(lay, pos, dz, wants, sem)


def wait_loads(lay, pos, dz, wants, sem):
    for i, (first, width, whole) in enumerate(wants):
        start = lax.bitwise_xor(pos[2], jnp.int32(dz)) * (2 * width)
        cols = whole.at[:, pl.ds(aligned(start, width), 2 * width)]
        pltpu.make_async_copy(cols, cols, sem.at[dz, i]).wait()


def kernel_call(body, pos, grid, ins, in_specs, outs, out_specs, scratch, aliases={}, room=60):
    return pl.pallas_call(
        body,
        out_shape=outs,
        grid_spec=pltpu.PrefetchScalarGridSpec(
            num_scalar_prefetch=1,
            grid=grid,
            in_specs=in_specs,
            out_specs=out_specs,
            scratch_shapes=scratch,
        ),
        input_output_aliases=aliases,
        compiler_params=pltpu.CompilerParams(
            dimension_semantics=("arbitrary",) * len(grid), vmem_limit_bytes=room * MIB
        ),
        cost_estimate=pl.CostEstimate(flops=1000, bytes_accessed=1000, transcendentals=0),
    )(pos, *ins)


def shape(dims, dtype):
    return jax.ShapeDtypeStruct(dims, dtype)


def full(dims):
    return pl.BlockSpec(dims, lambda *_: (0,) * len(dims))


def at_cols(rows, width, place=lambda k, pos: k):
    return pl.BlockSpec((rows, width), lambda k, pos: (0, place(k, pos)))


def at_lead(lead, *dims, place=lambda k, pos: k):
    return pl.BlockSpec((lead,) + dims, lambda k, pos: (place(k, pos),) + (0,) * len(dims))


def z_place(k, pos):
    return lax.bitwise_xor(pos[2], k)


ANY = pl.BlockSpec(memory_space=pl.ANY)


def norm_parts(values):
    centred = values - jnp.mean(values, axis=-1, keepdims=True)
    inverse = lax.rsqrt(jnp.mean(centred * centred, axis=-1, keepdims=True) + EPS)
    return centred * inverse, inverse


def norm_backward(grad, unit, inverse, gain):
    scaled = grad * gain
    return inverse * (
        scaled
        - jnp.mean(scaled, axis=-1, keepdims=True)
        - unit * jnp.mean(scaled * unit, axis=-1, keepdims=True)
    )


def qkv_call(lay, pos, first, bias_q, bias_v, weights, width):
    both, dim = first.shape
    rows = both // 2
    blocks = 2 * lay.nz
    n = len(weights)

    def body(pos_ref, first_ref, bq_ref, bv_ref, *rest):
        refs, (q_ref, k_ref, v_ref, whole_q, whole_kv, sem) = rest[:n], rest[n:]
        wants = ((0, width, whole_q), (width, 2 * width, whole_kv))
        dz = pl.program_id(0)

        stream_loads(lay, pos_ref, refs, wants, sem)
        z = z_place(dz, pos_ref)
        kv = dot(first_ref[...], whole_kv[:, pl.ds(aligned(z * 4 * width, width), 4 * width)])
        q = dot(first_ref[rows:], whole_q[:, pl.ds(aligned(z * 2 * width, width), 2 * width)])
        q = ((q + bq_ref[...]).astype(BF) * HEAD_DIM**-0.5).astype(BF)
        for x in range(2):
            q_ref[x] = q[:, x * width : (x + 1) * width]
            k_ref[x] = kv[:, 2 * x * width : (2 * x + 1) * width].astype(BF)
            bias = bv_ref[:, x * width : (x + 1) * width]
            v_ref[x] = (kv[:, (2 * x + 1) * width : (2 * x + 2) * width] + bias).astype(BF)

    return kernel_call(
        body,
        pos,
        (lay.nz,),
        (first, bias_q, bias_v, *weights),
        [full((both, dim)), at_cols(1, 2 * width, z_place), at_cols(1, 2 * width, z_place)] + [ANY] * n,
        [
            shape((blocks, rows, width), BF),
            shape((blocks, both, width), BF),
            shape((blocks, both, width), BF),
        ],
        [
            at_lead(2, rows, width, place=z_place),
            at_lead(2, both, width, place=z_place),
            at_lead(2, both, width, place=z_place),
        ],
        [
            pltpu.VMEM((dim, blocks * width), BF),
            pltpu.VMEM((dim, blocks * 2 * width), BF),
            pltpu.SemaphoreType.DMA((lay.nz, 2)),
        ],
    )


def mask_bias(seg_k, seg_q, rows):
    both = seg_k.shape[0]
    key_at = lax.broadcasted_iota(jnp.int32, (both, rows), 0) - (both - rows)
    query_at = lax.broadcasted_iota(jnp.int32, (both, rows), 1)
    return jnp.where((seg_k == seg_q) & (key_at <= query_at), 0.0, -1e30).astype(F32)


def head_only(block, head):
    lane = lax.broadcasted_iota(jnp.int32, block.shape, 1)
    inside = (lane >= head * HEAD_DIM) & (lane < (head + 1) * HEAD_DIM)
    return jnp.where(inside, block, jnp.zeros_like(block))


def attend_call(pos, query, key, value, seg_k, seg_q):
    blocks, both, width = key.shape
    rows = query.shape[1]
    heads = width // HEAD_DIM
    step = min(rows, 128)

    def body(pos_ref, q_ref, k_ref, v_ref, sk_ref, sq_ref, mixed_ref, exact_ref, lse_ref, bias):
        @pl.when(pl.program_id(0) == 0)
        def _():
            bias[...] = mask_bias(sk_ref[...], sq_ref[...], rows)

        for tile in range(rows // step):
            here = slice(tile * step, (tile + 1) * step)
            keys = both - rows + (tile + 1) * step
            outs = []
            for head in range(heads):
                scores = dot_nt(k_ref[0, :keys], head_only(q_ref[0, here], head)) + bias[:keys, here]
                top = jnp.max(scores, axis=0, keepdims=True)
                expo = jnp.exp(scores - top)
                total = jnp.sum(expo, axis=0, keepdims=True)
                share = jnp.broadcast_to(1.0 / total, (8, step)).T[:, :1]
                outs.append(dot_tn(expo.astype(BF), v_ref[0, :keys]) * share)
                lse_ref[0, head : head + 1, here] = top + jnp.log(total)
            lane = lax.broadcasted_iota(jnp.int32, outs[0].shape, 1)
            out = outs[0]
            for head in range(1, heads):
                out = jnp.where(lane < head * HEAD_DIM, out, outs[head])
            exact_ref[here] = out
            mixed_ref[here] = out.astype(BF)

    return kernel_call(
        body,
        pos,
        (blocks,),
        (query, key, value, seg_k, seg_q),
        [at_lead(1, rows, width), at_lead(1, both, width), at_lead(1, both, width), full((both, 1)), full((1, rows))],
        [
            shape((rows, blocks * width), BF),
            shape((rows, blocks * width), F32),
            shape((blocks, heads, rows), F32),
        ],
        [at_cols(rows, width), at_cols(rows, width), at_lead(1, heads, rows)],
        [pltpu.VMEM((both, rows), F32)],
    )


def branch_call(lay, pos, mixed, tokens, b_out, gain, shift, weights, first, width):
    rows, dim = tokens.shape
    blocks = 2 * lay.nz
    n = len(weights)

    def body(pos_ref, mixed_ref, tok_ref, bias_ref, gain_ref, shift_ref, *rest):
        refs, (middle_ref, second_ref, whole, sem) = rest[:n], rest[n:]
        wants = ((first, width, whole),)
        all_loads(lay, pos_ref, refs, wants, sem)
        branch = dot_nt(mixed_ref[...], whole[...])
        middle = tok_ref[...].astype(F32) + branch + bias_ref[...]
        middle_ref[...] = middle
        second_ref[...] = (norm_parts(middle)[0] * gain_ref[...] + shift_ref[...]).astype(BF)

    return kernel_call(
        body,
        pos,
        (),
        (mixed, tokens, b_out, gain, shift, *weights),
        [full(mixed.shape), full(tokens.shape)] + [full((1, dim))] * 3 + [ANY] * n,
        [shape((rows, dim), F32), shape((rows, dim), BF)],
        [full((rows, dim)), full((rows, dim))],
        [pltpu.VMEM((dim, blocks * width), BF), pltpu.SemaphoreType.DMA((lay.nz, 1))],
    )


def up_call(lay, pos, second, b_up, weights, width):
    rows, dim = second.shape
    blocks = 2 * lay.nz
    n = len(weights)

    def body(pos_ref, second_ref, bias_ref, *rest):
        refs, (gelu_ref, slope_ref, whole, sem) = rest[:n], rest[n:]
        wants = ((0, width, whole),)
        dz = pl.program_id(0)

        stream_loads(lay, pos_ref, refs, wants, sem)
        z = z_place(dz, pos_ref)
        for x in range(2):
            here = slice(x * width, (x + 1) * width)
            cols = pl.ds(aligned((z * 2 + x) * width, width), width)
            u = dot(second_ref[...], whole[:, cols]) + bias_ref[:, here]
            scale = 0.7978845608028654
            square = u * u
            half = 0.5 + 0.5 * jnp.tanh(u * (scale + (scale * 0.044715) * square))
            gelu = u * half
            gelu_ref[:, here] = gelu.astype(BF)
            bend = 2.0 * scale + (6.0 * scale * 0.044715) * square
            slope_ref[:, here] = (half + gelu * (1.0 - half) * bend).astype(BF)

    return kernel_call(
        body,
        pos,
        (lay.nz,),
        (second, b_up, *weights),
        [full(second.shape), at_cols(1, 2 * width, z_place)] + [ANY] * n,
        [shape((rows, blocks * width), BF)] * 2,
        [at_cols(rows, 2 * width, z_place)] * 2,
        [pltpu.VMEM((dim, blocks * width), BF), pltpu.SemaphoreType.DMA((lay.nz, 1))],
    )


def result_call(lay, pos, gelu, middle, b_down, weights, width):
    rows, dim = middle.shape
    blocks = 2 * lay.nz
    n = len(weights)

    def body(pos_ref, gelu_ref, middle_ref, bias_ref, *rest):
        refs, (result_ref, whole, acc, sem) = rest[:n], rest[n:]
        wants = ((0, width, whole),)
        dz = pl.program_id(0)

        stream_loads(lay, pos_ref, refs, wants, sem)

        @pl.when(dz == 0)
        def _():
            acc[...] = middle_ref[...] + bias_ref[...]

        cols = pl.ds(aligned(z_place(dz, pos_ref) * 2 * width, width), 2 * width)
        acc[...] += dot_nt(gelu_ref[...], whole[:, cols])

        @pl.when(dz == lay.nz - 1)
        def _():
            result_ref[...] = acc[...].astype(BF)

    return kernel_call(
        body,
        pos,
        (lay.nz,),
        (gelu, middle, b_down, *weights),
        [at_cols(rows, 2 * width, z_place), full((rows, dim)), full((1, dim))] + [ANY] * n,
        [shape((rows, dim), BF)],
        [full((rows, dim))],
        [
            pltpu.VMEM((dim, blocks * width), BF),
            pltpu.VMEM((rows, dim), F32),
            pltpu.SemaphoreType.DMA((lay.nz, 1)),
        ],
    )[0]


def pre_call(lay, pos, slope, grad, weights, width):
    rows, dim = grad.shape
    blocks = 2 * lay.nz
    n = len(weights)

    def body(pos_ref, slope_ref, grad_ref, *rest):
        refs, (pre_ref, hidden_ref, whole, sem) = rest[:n], rest[n:]
        wants = ((0, width, whole),)
        dz = pl.program_id(0)

        stream_loads(lay, pos_ref, refs, wants, sem)
        cols = pl.ds(aligned(z_place(dz, pos_ref) * 2 * width, width), 2 * width)
        pre = (dot(grad_ref[...], whole[:, cols]) * slope_ref[...].astype(F32)).astype(BF)
        pre_ref[...] = pre
        hidden_ref[...] = jnp.sum(pre.astype(F32), axis=0, keepdims=True)

    return kernel_call(
        body,
        pos,
        (lay.nz,),
        (slope, grad, *weights),
        [at_cols(rows, 2 * width, z_place), full((rows, dim))] + [ANY] * n,
        [shape((rows, blocks * width), BF), shape((1, blocks * width), F32)],
        [at_cols(rows, 2 * width, z_place), at_cols(1, 2 * width, z_place)],
        [pltpu.VMEM((dim, blocks * width), BF), pltpu.SemaphoreType.DMA((lay.nz, 1))],
    )


def second_back_call(lay, pos, pre, grad, middle, gain, weights, width):
    rows, dim = middle.shape
    blocks = 2 * lay.nz
    n = len(weights)

    def body(pos_ref, pre_ref, grad_ref, middle_ref, gain_ref, *rest):
        refs, (mgrad_ref, low_ref, sums_ref, whole, acc, sem) = rest[:n], rest[n:]
        wants = ((0, width, whole),)
        dz = pl.program_id(0)

        stream_loads(lay, pos_ref, refs, wants, sem)

        @pl.when(dz == 0)
        def _():
            acc[...] = jnp.zeros_like(acc)

        cols = pl.ds(aligned(z_place(dz, pos_ref) * 2 * width, width), 2 * width)
        acc[...] += dot_nt(pre_ref[...], whole[:, cols])

        @pl.when(dz == lay.nz - 1)
        def _():
            unit, inverse = norm_parts(middle_ref[...])
            second_grad = acc[...]
            sums_ref[0:1] = jnp.sum(second_grad * unit, axis=0, keepdims=True)
            sums_ref[1:2] = jnp.sum(second_grad, axis=0, keepdims=True)
            out = grad_ref[...].astype(F32)
            sums_ref[3:4] = jnp.sum(out, axis=0, keepdims=True)
            out = out + norm_backward(second_grad, unit, inverse, gain_ref[...])
            sums_ref[2:3] = jnp.sum(out, axis=0, keepdims=True)
            mgrad_ref[...] = out
            low_ref[...] = out.astype(BF)

    return kernel_call(
        body,
        pos,
        (lay.nz,),
        (pre, grad, middle, gain, *weights),
        [at_cols(rows, 2 * width, z_place)] + [full((rows, dim))] * 2 + [full((1, dim))] + [ANY] * n,
        [shape((rows, dim), F32), shape((rows, dim), BF), shape((4, dim), F32)],
        [full((rows, dim))] * 2 + [full((4, dim))],
        [
            pltpu.VMEM((dim, blocks * width), BF),
            pltpu.VMEM((rows, dim), F32),
            pltpu.SemaphoreType.DMA((lay.nz, 1)),
        ],
    )


def mixed_grad_call(lay, pos, low, weights, first, width):
    rows, dim = low.shape
    blocks = 2 * lay.nz
    n = len(weights)

    def body(pos_ref, low_ref, *rest):
        refs, (out_ref, whole, sem) = rest[:n], rest[n:]
        wants = ((first, width, whole),)
        all_loads(lay, pos_ref, refs, wants, sem)
        out_ref[...] = dot(low_ref[...], whole[...]).astype(BF)

    return kernel_call(
        body,
        pos,
        (),
        (low, *weights),
        [full((rows, dim))] + [ANY] * n,
        [shape((rows, blocks * width), BF)],
        [full((rows, blocks * width))],
        [pltpu.VMEM((dim, blocks * width), BF), pltpu.SemaphoreType.DMA((lay.nz, 1))],
    )[0]


def attend_back_call(pos, span, query, key, value, seg_k, seg_q, lse, mixed_grad, exact, earlier=()):
    blocks, both, width = key.shape
    rows = query.shape[1]
    heads = width // HEAD_DIM
    step = min(rows, 256)
    begin = span[0]
    n = len(earlier)

    def body(pos_ref, q_ref, k_ref, v_ref, sk_ref, sq_ref, lse_ref, grad_ref, exact_ref, *rest):
        dq_ref, dk_ref, dv_ref, sums_ref, bias, dq_t, dk, dv = rest[n:]

        @pl.when(pl.program_id(0) == 0)
        def _():
            bias[...] = mask_bias(sk_ref[...], sq_ref[...], rows)

        key_t = k_ref[0].T
        inner_t = (grad_ref[...].astype(F32) * exact_ref[...]).T
        dk[...] = jnp.zeros_like(dk)
        dv[...] = jnp.zeros_like(dv)
        for tile in range(rows // step):
            here = slice(tile * step, (tile + 1) * step)
            keys = both - rows + (tile + 1) * step
            for head in range(heads):
                lanes = slice(head * HEAD_DIM, (head + 1) * HEAD_DIM)
                q_head = head_only(q_ref[0, here], head)
                g_head = head_only(grad_ref[here], head)
                scores = dot_nt(k_ref[0, :keys], q_head) + bias[:keys, here]
                probs = jnp.exp(scores - lse_ref[0, head : head + 1, here])
                prob_grad = dot_nt(v_ref[0, :keys], g_head)
                inner = jnp.sum(inner_t[lanes, here], axis=0, keepdims=True)
                score_grad = (probs * (prob_grad - inner)).astype(BF)
                dv[:keys] += dot(probs.astype(BF), g_head)
                dk[:keys] += dot(score_grad, q_head)
                dq_t[lanes, here] = dot(key_t[lanes, :keys], score_grad)
        dq = (dq_t[...].T * HEAD_DIM**-0.5).astype(BF)
        dv_low = dv[...].astype(BF)
        dq_ref[0] = dq
        dk_ref[0] = dk[...].astype(BF)
        dv_ref[0] = dv_low
        sums_ref[0:1] = jnp.sum(dq.astype(F32), axis=0, keepdims=True)
        sums_ref[1:2] = jnp.sum(dv_low.astype(F32), axis=0, keepdims=True)

    at = lambda k, pos: k + begin
    return kernel_call(
        body,
        pos,
        (span[1] - span[0],),
        (query, key, value, seg_k, seg_q, lse, mixed_grad, exact, *earlier),
        [
            at_lead(1, rows, width, place=at),
            at_lead(1, both, width, place=at),
            at_lead(1, both, width, place=at),
            full((both, 1)),
            full((1, rows)),
            at_lead(1, heads, rows, place=at),
            at_cols(rows, width, at),
            at_cols(rows, width, at),
        ]
        + [ANY] * n,
        [
            shape((blocks, rows, width), BF),
            shape((blocks, both, width), BF),
            shape((blocks, both, width), BF),
            shape((2, blocks * width), F32),
        ],
        [
            at_lead(1, rows, width, place=at),
            at_lead(1, both, width, place=at),
            at_lead(1, both, width, place=at),
            at_cols(2, width, at),
        ],
        [
            pltpu.VMEM((both, rows), F32),
            pltpu.VMEM((width, rows), F32),
            pltpu.VMEM((both, width), F32),
            pltpu.VMEM((both, width), F32),
        ],
        {9: 0, 10: 1, 11: 2, 12: 3} if n else {},
    )


def sides(ref, which, rows):
    here = slice(0, rows) if which == 0 else slice(rows, 2 * rows)
    return [ref[x, here] for x in range(2)]


def first_grad_prev_call(lay, pos, dk, dv, tokens, gain, weights, width):
    rows, dim = tokens.shape
    blocks = 2 * lay.nz
    n = len(weights)

    def body(pos_ref, dk_ref, dv_ref, tok_ref, gain_ref, *rest):
        refs, (grad_ref, sums_ref, whole, acc, sem) = rest[:n], rest[n:]
        wants = ((width, 2 * width, whole),)
        dz = pl.program_id(0)

        stream_loads(lay, pos_ref, refs, wants, sem)

        @pl.when(dz == 0)
        def _():
            acc[...] = jnp.zeros_like(acc)

        keys, values = sides(dk_ref, 0, rows), sides(dv_ref, 0, rows)
        part = jnp.concatenate([keys[0], values[0], keys[1], values[1]], axis=1)
        cols = pl.ds(aligned(z_place(dz, pos_ref) * 4 * width, width), 4 * width)
        acc[...] += dot_nt(part, whole[:, cols])

        @pl.when(dz == lay.nz - 1)
        def _():
            grad = acc[...]
            unit, inverse = norm_parts(tok_ref[...].astype(F32))
            grad_ref[...] = norm_backward(grad, unit, inverse, gain_ref[...]).astype(BF)
            sums_ref[0:1] = jnp.sum(grad * unit, axis=0, keepdims=True)
            sums_ref[1:2] = jnp.sum(grad, axis=0, keepdims=True)

    both = at_lead(2, rows, width, place=z_place)
    return kernel_call(
        body,
        pos,
        (lay.nz,),
        (dk, dv, tokens, gain, *weights),
        [both, both, full((rows, dim)), full((1, dim))] + [ANY] * n,
        [shape((rows, dim), BF), shape((2, dim), F32)],
        [full((rows, dim)), full((2, dim))],
        [
            pltpu.VMEM((dim, blocks * 2 * width), BF),
            pltpu.VMEM((rows, dim), F32),
            pltpu.SemaphoreType.DMA((lay.nz, 1)),
        ],
    )


def first_grad_own_call(lay, pos, dq, dk, dv, tokens, middle_grad, gain, weights, width):
    rows, dim = tokens.shape
    blocks = 2 * lay.nz
    n = len(weights)

    def body(pos_ref, dq_ref, dk_ref, dv_ref, tok_ref, middle_ref, gain_ref, *rest):
        refs, (grad_ref, sums_ref, whole_q, whole_kv, sem) = rest[:n], rest[n:]
        wants = ((0, width, whole_q), (width, 2 * width, whole_kv))
        dz = pl.program_id(0)

        stream_loads(lay, pos_ref, refs, wants, sem)

        @pl.when(dz == 0)
        def _():
            grad_ref[...] = jnp.zeros_like(grad_ref)

        z = z_place(dz, pos_ref)
        keys, values = sides(dk_ref, 1, rows), sides(dv_ref, 1, rows)
        part = jnp.concatenate([keys[0], values[0], keys[1], values[1]], axis=1)
        more = dot_nt(part, whole_kv[:, pl.ds(aligned(z * 4 * width, width), 4 * width)])
        part = jnp.concatenate([dq_ref[0], dq_ref[1]], axis=1)
        more += dot_nt(part, whole_q[:, pl.ds(aligned(z * 2 * width, width), 2 * width)])
        grad_ref[...] += more

        @pl.when(dz == lay.nz - 1)
        def _():
            grad = grad_ref[...]
            unit, inverse = norm_parts(tok_ref[...].astype(F32))
            sums_ref[0:1] = jnp.sum(grad * unit, axis=0, keepdims=True)
            sums_ref[1:2] = jnp.sum(grad, axis=0, keepdims=True)
            grad_ref[...] = middle_ref[...] + norm_backward(grad, unit, inverse, gain_ref[...])

    both = at_lead(2, 2 * rows, width, place=z_place)
    return kernel_call(
        body,
        pos,
        (lay.nz,),
        (dq, dk, dv, tokens, middle_grad, gain, *weights),
        [at_lead(2, rows, width, place=z_place), both, both]
        + [full((rows, dim))] * 2
        + [full((1, dim))]
        + [ANY] * n,
        [shape((rows, dim), F32), shape((2, dim), F32)],
        [full((rows, dim)), full((2, dim))],
        [
            pltpu.VMEM((dim, blocks * width), BF),
            pltpu.VMEM((dim, blocks * 2 * width), BF),
            pltpu.SemaphoreType.DMA((lay.nz, 2)),
        ],
    )


def half_grad_call(lay, pos, *, half, columns, lefts, tile, operands, specs, received):
    ny, nz, near, rows = lay.ny, lay.nz, lay.near, lay.rows
    n = len(operands)

    def body(pos_ref, *refs):
        ins, rest = refs[:n], refs[n:]
        got, rest = (rest[0], rest[1:]) if half == 0 else (None, rest)
        count = ny + 2 if half == 0 else 1
        outs, turned, spare = rest[:count], rest[count : count + len(lefts)], rest[count + len(lefts) :]
        dz = pl.program_id(0)

        @pl.when(dz == 0)
        def _():
            for index, ref in zip(lefts, turned):
                if rows % 128:
                    spare[0][...] = ins[index][...].T
                for dy in range(ny):
                    span = pl.ds(lay.row_start(pos_ref, dy, half), rows)
                    piece = spare[0][span] if rows % 128 else ins[index][:, span].T
                    ref[dy * rows : (dy + 1) * rows] = piece

        def make(put):
            blocks = tile(turned, ins, [lay.x_block(pos_ref, dx) for dx in range(2)])
            for dx in range(2):
                for dy in range(ny):
                    block = blocks[dx][dy * rows : (dy + 1) * rows]
                    if half == 0:
                        block = block + got[0, dx, dy].astype(F32)
                    put(dx, dy, block.astype(BF))

        if half == 1:

            def put(dx, dy, block):
                outs[0][0, dx, dy] = block

            make(put)
            return

        @pl.when(dz < near)
        def _():
            def put(dx, dy, block):
                outs[dy][0, dx] = block

            make(put)

        @pl.when(dz >= near)
        def _():
            def put(dx, dy, block):
                outs[ny + dx][0, dy] = block

            make(put)

    def step(*dims, at=lambda dz: dz):
        return pl.BlockSpec((1,) + dims, lambda dz, pos: (at(dz),) + (0,) * len(dims))

    if half == 0:
        operands = (*operands, received)
        specs = [*specs, step(2, ny, rows, columns)]
        outs = [shape((near, 2, rows, columns), BF)] * ny + [shape((nz - near, ny, rows, columns), BF)] * 2
        out_specs = [step(2, rows, columns, at=lambda dz: jnp.minimum(dz, near - 1))] * ny
        out_specs += [step(ny, rows, columns, at=lambda dz: jnp.maximum(dz - near, 0))] * 2
    else:
        outs = [shape((nz, 2, ny, rows, columns), BF)]
        out_specs = [step(2, ny, rows, columns)]
    scratch = [pltpu.VMEM((ny * rows, operands[index].shape[0]), BF) for index in lefts]
    if rows % 128:
        scratch.append(pltpu.VMEM(operands[lefts[0]].shape[::-1], BF))
    return kernel_call(body, pos, (nz,), operands, specs, outs, out_specs, scratch)


def sum_call(pos, groups, outs, build, steps=1):
    cut = lambda dims: (dims[0] // steps,) + dims[1:]
    spec = lambda r: pl.BlockSpec(cut(r.shape), lambda k, pos: (k,) + (0,) * (len(r.shape) - 1))
    flat = [r for g in groups for r in g]

    def body(pos_ref, *refs):
        ins, given = refs[: len(flat)], refs[len(flat) :]
        at, sums = 0, []
        for g in groups:
            mine = ins[at : at + len(g)]
            at += len(g)
            sums.append(lambda index, mine=mine: sum(
                (r[index].astype(F32) for r in mine[1:]), mine[0][index].astype(F32)
            ))
        build(sums, given)

    return kernel_call(
        body, pos, (steps,), flat, [spec(r) for r in flat], outs, [spec(o) for o in outs], [], {}, 63
    )


class Scatter:
    def __init__(self, lay, pos, columns, lefts, tile, operands, specs):
        self.lay, self.pos, self.columns = lay, pos, columns
        self.half = functools.partial(
            half_grad_call, lay, pos, columns=columns, lefts=lefts, tile=tile, operands=operands,
            specs=specs,
        )

    def away(self):
        self.sent = self.half(half=1, received=None)[0]

    def swap(self):
        self.received = trade(self.sent, "c", 2, 1)

    def own(self):
        parts = self.half(half=0, received=self.received)
        self.top, self.low = parts[: self.lay.ny], parts[self.lay.ny :]

    def send_one(self):
        self.top = [self.top[0]] + [trade(self.top[d], "fy", self.lay.ny, d) for d in range(1, self.lay.ny)]
        self.low = [self.low[0], trade(self.low[1], "tx", 2, 1)]

    def sum_one(self):
        ny, rows, near, far = self.lay.ny, self.lay.rows, self.lay.near, self.lay.nz - self.lay.near

        def build(sums, given):
            for dx in range(2):
                given[dx][...] = sums[0]((slice(None), dx)).astype(BF)
            for dy in range(ny):
                given[2 + dy][...] = sums[1]((slice(None), dy)).astype(BF)

        outs = [shape((near, rows, self.columns), BF)] * 2 + [shape((far, rows, self.columns), BF)] * ny
        out = sum_call(self.pos, [self.top, self.low], outs, build, near if near == far else 1)
        self.top, self.low = out[:2], out[2:]

    def send_two(self):
        self.top = [self.top[0], trade(self.top[1], "tx", 2, 1)]
        self.low = [self.low[0]] + [trade(self.low[d], "fy", self.lay.ny, d) for d in range(1, self.lay.ny)]

    def sum_two(self):
        near, nz = self.lay.near, self.lay.nz

        def build(sums, given):
            for dz in range(nz):
                given[dz][...] = (sums[0](dz) if dz < near else sums[1](dz - near)).astype(BF)

        outs = [shape((self.lay.rows, self.columns), BF)] * nz
        self.top = sum_call(self.pos, [self.top, self.low], outs, build)
        self.low = []

    def send_three(self):
        self.top = [self.top[0]] + [trade(self.top[d], "tz", self.lay.nz, d) for d in range(1, self.lay.nz)]

    def sum_three(self, cuts):
        rows = self.lay.rows
        outs = [shape((c[0], rows, c[1]) if isinstance(c, tuple) else (rows, c), F32) for c in cuts]

        def build(sums, given):
            at = 0
            for ref, c in zip(given, cuts):
                if isinstance(c, tuple):
                    for i in range(c[0]):
                        ref[i] = sums[0]((slice(None), slice(at, at + c[1])))
                        at += c[1]
                else:
                    ref[...] = sums[0]((slice(None), slice(at, at + c)))
                    at += c

        self.out = sum_call(self.pos, [self.top], outs, build)


def per_device(
    sizes,
    tokens,
    segment_ids,
    w_qkv,
    b_qv,
    w_out,
    b_out,
    w_up,
    b_up,
    w_down,
    b_down,
    ln1_gain,
    ln1_shift,
    ln2_gain,
    ln2_shift,
    grad_out,
):
    ny, nz = sizes
    rows, dim = tokens.shape
    length = segment_ids.shape[1]
    width = w_qkv.shape[2]
    hidden = w_up.shape[1]
    lay = Layout(ny, nz, w_qkv.shape[0])
    axes = ("fy", "c", "tz", "tx")
    pos = jnp.stack([lax.axis_index(axis) for axis in axes]).astype(jnp.int32)
    row = lambda v: v.reshape(1, -1)

    blocks = 2 * nz
    half = nz
    up_parts = [lax.all_gather(jnp.concatenate([w_up, w_out], axis=1), axes, axis=0, tiled=False)]
    qkv = Gather(lay, w_qkv.reshape(lay.rows, 3 * width))
    down = Gather(lay, w_down)
    qkv.one()
    tokens_prev = lax.ppermute(tokens, "tx", [(0, 1)])
    tokens_prev = stage(qkv, tokens_prev)
    qkv.two()
    qkv.three()
    qkv.swap(0)

    sequence = (pos[2] * 2 + pos[3]) // 2
    later = pos[3] > 0
    ids = lax.dynamic_slice_in_dim(segment_ids, sequence, 1, 0)
    seg_q = jnp.where(later, ids[:, rows:], ids[:, :rows])
    seg_prev = jnp.where(later, ids[:, :rows], -1)
    seg_k = jnp.concatenate([seg_prev, seg_q], axis=1).reshape(length, 1)
    both = jnp.concatenate([tokens_prev, tokens], axis=0).astype(F32)
    first = (norm_parts(both)[0] * ln1_gain + ln1_shift).astype(BF)
    first, seg_k, seg_q = stage(qkv, down, first, seg_k, seg_q)
    qkv.swap(1)
    down.one()
    qkv.parts, first = stage(qkv.parts, first)
    query, key, value = qkv_call(lay, pos, first, b_qv[0:1], b_qv[1:2], qkv.parts, width)
    mixed, exact, lse = attend_call(pos, query, key, value, seg_k, seg_q)
    mixed, up_parts = stage(down, mixed, up_parts)
    down.two()
    middle, second = branch_call(
        lay, pos, mixed, tokens, row(b_out), row(ln2_gain), row(ln2_shift), up_parts, hidden, width
    )
    middle, second = stage(down, middle, second)
    down.three()
    down.swap(0)
    gelu, slope = up_call(lay, pos, second, row(b_up), up_parts, hidden)

    whole = lambda v: full(v.shape)
    at_z = lambda size: at_cols(rows, 2 * size, z_place)
    block = lambda ref, x, size: ref[:, pl.ds(aligned(x * size, size), size)]

    def down_tile(left, ins, xs):
        return [dot(left[0][...], block(ins[1], x, hidden)) for x in xs]

    grad_down = Scatter(
        lay, pos, hidden, (0,), down_tile, (grad_out, gelu), [whole(grad_out), at_z(hidden)]
    )
    grad_down.away()
    grad_down.sent, slope, down.twin = stage(down, grad_down.sent, slope, down.twin)
    down.swap(1)
    slope, down.parts, grad_down.sent = stage(slope, down.parts, grad_down.sent)
    grad_down.swap()
    pre, grad_b_up = pre_call(lay, pos, slope, grad_out, down.parts, hidden)
    grad_down.received, pre = stage(grad_down.received, pre)
    grad_down.own()
    pre = stage(grad_down, pre)
    grad_down.send_one()
    middle_grad, middle_low, sums2 = second_back_call(
        lay, pos, pre, grad_out, middle, row(ln2_gain), up_parts, hidden
    )

    def up_tile(left, ins, xs):
        return [
            jnp.concatenate(
                [dot(left[0][...], block(ins[1], x, hidden)), dot(left[1][...], block(ins[3], x, width))],
                axis=1,
            )
            for x in xs
        ]

    grad_up = Scatter(
        lay, pos, hidden + width, (0, 2), up_tile, (second, pre, middle_low, mixed),
        [whole(second), at_z(hidden), whole(middle_low), at_z(width)],
    )
    mixed_grad = mixed_grad_call(lay, pos, middle_low, up_parts, hidden, width)
    grad_up.away()
    grad_up.sent, mixed_grad = stage(grad_down, grad_up.sent, mixed_grad)
    grad_down.sum_one()
    grad_up.sent, mixed_grad = stage(grad_down, grad_up.sent, mixed_grad)
    grad_down.send_two()
    grad_up.swap()
    partial = attend_back_call(pos, (0, half), query, key, value, seg_k, seg_q, lse, mixed_grad, exact)
    partial, grad_up.received = stage(grad_down, partial, grad_up.received)
    grad_down.sum_two()
    grad_up.own()
    partial = stage(grad_up, grad_down, partial)
    grad_up.send_one()
    grad_down.send_three()
    dq, dk, dv, sums_qv = attend_back_call(
        pos, (half, blocks), query, key, value, seg_k, seg_q, lse, mixed_grad, exact, partial
    )

    def qkv_tile(left, ins, xs):
        late = left[0][:, rows:]
        q = dot(late, jnp.concatenate([ins[1][x] for x in xs], axis=1))
        out = []
        for i, x in enumerate(xs):
            kv = dot(left[0][...], jnp.concatenate([ins[2][x], ins[3][x]], axis=1))
            out.append(jnp.concatenate([q[:, i * width : (i + 1) * width], kv], axis=1))
        return out

    grad_qkv = Scatter(
        lay, pos, 3 * width, (0,), qkv_tile, (first, dq, dk, dv),
        [
            whole(first),
            at_lead(2, rows, width, place=z_place),
            at_lead(2, 2 * rows, width, place=z_place),
            at_lead(2, 2 * rows, width, place=z_place),
        ],
    )
    grad_qkv.away()
    grad_qkv.sent, dq, dk, dv = stage(grad_up, grad_down, grad_qkv.sent, dq, dk, dv)
    grad_up.sum_one()
    grad_qkv.sent, dq, dk, dv = stage(grad_up, grad_qkv.sent, dq, dk, dv)
    grad_up.send_two()
    grad_qkv.swap()
    back, sums_prev = first_grad_prev_call(
        lay, pos, dk, dv, tokens_prev, row(ln1_gain), qkv.parts, width
    )
    grad_qkv.received, dq, dk, dv, back, sums_prev = stage(
        grad_qkv.received, dq, dk, dv, back, sums_prev
    )
    grad_qkv.own()
    dq, dk, dv, gelu = stage(grad_qkv, grad_up, dq, dk, dv, gelu)
    grad_qkv.send_one()
    grad_up.sum_two()
    gelu, dq, dk, dv = stage(grad_up, gelu, dq, dk, dv)
    grad_up.send_three()
    first_grad, sums1 = first_grad_own_call(
        lay, pos, dq, dk, dv, tokens, middle_grad, row(ln1_gain), qkv.parts, width
    )
    result = result_call(lay, pos, gelu, middle, row(b_down), down.parts, hidden)
    small = jnp.concatenate(
        [v.reshape(-1) for v in (sums2, grad_b_up, sums1 + sums_prev, sums_qv)]
    ).reshape(-1, 128)
    small, first_grad, result, back = stage(grad_qkv, grad_up, small, first_grad, result, back)
    grad_qkv.sum_one()
    small, back = stage(grad_qkv, small, back)
    grad_qkv.send_two()
    grad_down.sum_three((hidden,))
    both_cores = [((c, x), (c ^ 1, x ^ 1)) for c in range(2) for x in range(2)]
    both_cores = [(s[0] * 2 + s[1], t[0] * 2 + t[1]) for s, t in both_cores]
    pieces = [
        small,
        trade(small, "c", 2, 1),
        trade(small, "tx", 2, 1),
        lax.ppermute(small, ("c", "tx"), both_cores),
    ]
    pieces, back, grad_down.out = stage(grad_qkv, pieces, back, grad_down.out)
    small = (pieces[0] + pieces[1]) + (pieces[2] + pieces[3])
    grad_qkv.sum_two()
    small, back = stage(grad_qkv, small, back)
    grad_qkv.send_three()
    pieces = around(small, "fy", ny)
    back = lax.ppermute(back, "tx", [(1, 0)])
    grad_up.sum_three((hidden, width))
    pieces, grad_up.out = stage(grad_qkv, pieces, grad_up.out)
    small = sum(around(sum(pieces), "tz", nz)).reshape(-1)
    token_grad = (first_grad + back.astype(F32)).astype(BF)
    grad_qkv.sum_three(((3, width),))
    at = 4 * dim
    late = small[at + gelu.shape[1] :]
    return (
        result,
        token_grad,
        jnp.transpose(grad_qkv.out[0], (1, 0, 2)),
        late[2 * dim :].reshape(2, -1),
        grad_up.out[1],
        small[2 * dim : 3 * dim],
        grad_up.out[0],
        small[at : at + gelu.shape[1]],
        grad_down.out[0],
        small[3 * dim : at],
        late[:dim],
        late[dim : 2 * dim],
        small[:dim],
        small[dim : 2 * dim],
    )


def solution(mesh):
    n_fsdp, n_tp = mesh.devices.shape
    fine = Mesh(
        mesh.devices.reshape(n_fsdp // 2, 2, n_tp // 2, 2), ("fy", "c", "tz", "tx")
    )
    fsdp, tp, every = ("fy", "c"), ("tz", "tx"), ("fy", "c", "tz", "tx")
    tile = P(fsdp, tp)
    ins = (
        P(every, None),
        P(fsdp, None),
        P(fsdp, None, tp),
        P(),
        tile,
        P(),
        tile,
        P(),
        tile,
        P(),
        P(),
        P(),
        P(),
        P(),
        P(every, None),
    )
    outs = (
        P(every, None),
        P(every, None),
        P(fsdp, None, tp),
        P(),
        tile,
        P(),
        tile,
        P(),
        tile,
        P(),
        P(),
        P(),
        P(),
        P(),
    )
    return jax.shard_map(
        functools.partial(per_device, (n_fsdp // 2, n_tp // 2)),
        mesh=fine,
        in_specs=ins,
        out_specs=outs,
        check_vma=False,
    )
```

```python
import functools

import jax
import jax.numpy as jnp
from jax import lax
from jax.experimental import pallas as pl
from jax.experimental.pallas import tpu as pltpu
from jax.sharding import Mesh, PartitionSpec as P

HEAD_DIM = 64
EPS = 1e-05
BF = jnp.bfloat16
F32 = jnp.float32
NT = (((1,), (1,)), ((), ()))
TN = (((0,), (0,)), ((), ()))
MIB = 1 << 20


def dot(a, b):
    return jnp.dot(a, b, preferred_element_type=F32)


def dot_nt(a, b):
    return lax.dot_general(a, b, NT, preferred_element_type=F32)


def dot_tn(a, b):
    return lax.dot_general(a, b, TN, preferred_element_type=F32)


def aligned(value, multiple):
    return pl.multiple_of(value, multiple)


class Layout:
    def __init__(self, ny, nz, rows):
        self.ny, self.nz, self.rows = ny, nz, rows
        self.near = nz // 2

    def row_start(self, pos, dy, dc):
        block = lax.bitwise_xor(pos[0], jnp.int32(dy)) * 2 + lax.bitwise_xor(pos[1], jnp.int32(dc))
        return pl.multiple_of(block * self.rows, self.rows)

    def z_block(self, pos, dz):
        return lax.bitwise_xor(pos[2], jnp.int32(dz))

    def x_block(self, pos, dx):
        return lax.bitwise_xor(pos[3], jnp.int32(dx))


def trade(value, axis, size, distance):
    return lax.ppermute(value, axis, [(s, s ^ distance) for s in range(size)])


def around(value, axis, size):
    return [value] + [trade(value, axis, size, d) for d in range(1, size)]


class Gather:
    def __init__(self, lay, shard):
        self.lay, self.top, self.low = lay, [shard], []

    def one(self):
        near = self.lay.near
        pieces = around(self.top[0], "tz", self.lay.nz)
        self.top, self.low = pieces[:near], pieces[near:]

    def two(self):
        lay = self.lay
        self.top = around(jnp.stack(self.top), "tx", 2)
        self.low = around(jnp.stack(self.low), "fy", lay.ny)

    def three(self):
        lay = self.lay
        self.top = around(jnp.stack(self.top), "fy", lay.ny)
        self.low = around(jnp.stack(self.low), "tx", 2)

    def swap(self, which):
        if which == 0:
            self.twin = [trade(self.top[0], "c", 2, 1), trade(self.low[0], "c", 2, 1)]
        else:
            late = [trade(t, "c", 2, 1) for t in self.top[1:] + self.low[1:]]
            n = len(self.top) - 1
            self.parts = self.top + self.low + [self.twin[0], *late[:n], self.twin[1], *late[n:]]


def stage(*things):
    values = []
    for thing in things:
        values.append((thing.top, thing.low) if isinstance(thing, (Gather, Scatter)) else thing)
    values = lax.optimization_barrier(values)
    back = []
    for thing, value in zip(things, values):
        if isinstance(thing, (Gather, Scatter)):
            thing.top, thing.low = value
        else:
            back.append(value)
    return back[0] if len(back) == 1 else back


def start_loads(lay, pos, refs, wants, sem, dz):
    half = len(refs) // 2
    for dx in range(2):
        k = lay.z_block(pos, dz) * 2 + lay.x_block(pos, dx)
        for dc in range(2):
            mine = refs[dc * half : (dc + 1) * half]
            for dy in range(lay.ny):
                start = lay.row_start(pos, dy, dc)
                if len(refs) == 1:
                    block = refs[0].at[start // lay.rows * (2 * lay.nz) + k]
                elif dz < lay.near:
                    block = mine[dy].at[dx, dz]
                else:
                    block = mine[lay.ny + dx].at[dy, dz - lay.near]
                for i, (first, width, whole) in enumerate(wants):
                    pltpu.make_async_copy(
                        block.at[:, pl.ds(first, width)],
                        whole.at[pl.ds(start, lay.rows), pl.ds(aligned(k * width, width), width)],
                        sem.at[dz, i],
                    ).start()


def stream_loads(lay, pos, refs, wants, sem):
    step = pl.program_id(0)
    for dz in range(lay.nz):

        @pl.when(step == max(dz - 2, 0))
        def _(dz=dz):
            start_loads(lay, pos, refs, wants, sem, dz)

    wait_loads(lay, pos, step, wants, sem)


def all_loads(lay, pos, refs, wants, sem):
    for dz in range(lay.nz):
        start_loads(lay, pos, refs, wants, sem, dz)
    for dz in range(lay.nz):
        wait_loads(lay, pos, dz, wants, sem)


def wait_loads(lay, pos, dz, wants, sem):
    for i, (first, width, whole) in enumerate(wants):
        start = lax.bitwise_xor(pos[2], jnp.int32(dz)) * (2 * width)
        cols = whole.at[:, pl.ds(aligned(start, width), 2 * width)]
        pltpu.make_async_copy(cols, cols, sem.at[dz, i]).wait()


def kernel_call(body, pos, grid, ins, in_specs, outs, out_specs, scratch, aliases={}, room=60):
    return pl.pallas_call(
        body,
        out_shape=outs,
        grid_spec=pltpu.PrefetchScalarGridSpec(
            num_scalar_prefetch=1,
            grid=grid,
            in_specs=in_specs,
            out_specs=out_specs,
            scratch_shapes=scratch,
        ),
        input_output_aliases=aliases,
        compiler_params=pltpu.CompilerParams(
            dimension_semantics=("arbitrary",) * len(grid), vmem_limit_bytes=room * MIB
        ),
        cost_estimate=pl.CostEstimate(flops=1000, bytes_accessed=1000, transcendentals=0),
    )(pos, *ins)


def shape(dims, dtype):
    return jax.ShapeDtypeStruct(dims, dtype)


def full(dims):
    return pl.BlockSpec(dims, lambda *_: (0,) * len(dims))


def at_cols(rows, width, place=lambda k, pos: k):
    return pl.BlockSpec((rows, width), lambda k, pos: (0, place(k, pos)))


def at_lead(lead, *dims, place=lambda k, pos: k):
    return pl.BlockSpec((lead,) + dims, lambda k, pos: (place(k, pos),) + (0,) * len(dims))


def z_place(k, pos):
    return lax.bitwise_xor(pos[2], k)


ANY = pl.BlockSpec(memory_space=pl.ANY)


def norm_parts(values):
    centred = values - jnp.mean(values, axis=-1, keepdims=True)
    inverse = lax.rsqrt(jnp.mean(centred * centred, axis=-1, keepdims=True) + EPS)
    return centred * inverse, inverse


def norm_backward(grad, unit, inverse, gain):
    scaled = grad * gain
    return inverse * (
        scaled
        - jnp.mean(scaled, axis=-1, keepdims=True)
        - unit * jnp.mean(scaled * unit, axis=-1, keepdims=True)
    )


def qkv_call(lay, pos, first, bias_q, bias_v, weights, width):
    both, dim = first.shape
    rows = both // 2
    blocks = 2 * lay.nz
    n = len(weights)

    def body(pos_ref, first_ref, bq_ref, bv_ref, *rest):
        refs, (q_ref, k_ref, v_ref, whole_q, whole_kv, sem) = rest[:n], rest[n:]
        wants = ((0, width, whole_q), (width, 2 * width, whole_kv))
        dz = pl.program_id(0)

        stream_loads(lay, pos_ref, refs, wants, sem)
        z = z_place(dz, pos_ref)
        kv = dot(first_ref[...], whole_kv[:, pl.ds(aligned(z * 4 * width, width), 4 * width)])
        q = dot(first_ref[rows:], whole_q[:, pl.ds(aligned(z * 2 * width, width), 2 * width)])
        q = ((q + bq_ref[...]).astype(BF) * HEAD_DIM**-0.5).astype(BF)
        for x in range(2):
            q_ref[x] = q[:, x * width : (x + 1) * width]
            k_ref[x] = kv[:, 2 * x * width : (2 * x + 1) * width].astype(BF)
            bias = bv_ref[:, x * width : (x + 1) * width]
            v_ref[x] = (kv[:, (2 * x + 1) * width : (2 * x + 2) * width] + bias).astype(BF)

    return kernel_call(
        body,
        pos,
        (lay.nz,),
        (first, bias_q, bias_v, *weights),
        [full((both, dim)), at_cols(1, 2 * width, z_place), at_cols(1, 2 * width, z_place)] + [ANY] * n,
        [
            shape((blocks, rows, width), BF),
            shape((blocks, both, width), BF),
            shape((blocks, both, width), BF),
        ],
        [
            at_lead(2, rows, width, place=z_place),
            at_lead(2, both, width, place=z_place),
            at_lead(2, both, width, place=z_place),
        ],
        [
            pltpu.VMEM((dim, blocks * width), BF),
            pltpu.VMEM((dim, blocks * 2 * width), BF),
            pltpu.SemaphoreType.DMA((lay.nz, 2)),
        ],
    )


def mask_bias(seg_k, seg_q, rows):
    both = seg_k.shape[0]
    key_at = lax.broadcasted_iota(jnp.int32, (both, rows), 0) - (both - rows)
    query_at = lax.broadcasted_iota(jnp.int32, (both, rows), 1)
    return jnp.where((seg_k == seg_q) & (key_at <= query_at), 0.0, -1e30).astype(F32)


def head_only(block, head):
    lane = lax.broadcasted_iota(jnp.int32, block.shape, 1)
    inside = (lane >= head * HEAD_DIM) & (lane < (head + 1) * HEAD_DIM)
    return jnp.where(inside, block, jnp.zeros_like(block))


def attend_call(pos, query, key, value, seg_k, seg_q):
    blocks, both, width = key.shape
    rows = query.shape[1]
    heads = width // HEAD_DIM
    step = min(rows, 128)

    def body(pos_ref, q_ref, k_ref, v_ref, sk_ref, sq_ref, mixed_ref, exact_ref, lse_ref, bias):
        @pl.when(pl.program_id(0) == 0)
        def _():
            bias[...] = mask_bias(sk_ref[...], sq_ref[...], rows)

        for tile in range(rows // step):
            here = slice(tile * step, (tile + 1) * step)
            keys = both - rows + (tile + 1) * step
            outs = []
            for head in range(heads):
                scores = dot_nt(k_ref[0, :keys], head_only(q_ref[0, here], head)) + bias[:keys, here]
                top = jnp.max(scores, axis=0, keepdims=True)
                expo = jnp.exp(scores - top)
                total = jnp.sum(expo, axis=0, keepdims=True)
                share = jnp.broadcast_to(1.0 / total, (8, step)).T[:, :1]
                outs.append(dot_tn(expo.astype(BF), v_ref[0, :keys]) * share)
                lse_ref[0, head : head + 1, here] = top + jnp.log(total)
            lane = lax.broadcasted_iota(jnp.int32, outs[0].shape, 1)
            out = outs[0]
            for head in range(1, heads):
                out = jnp.where(lane < head * HEAD_DIM, out, outs[head])
            exact_ref[here] = out
            mixed_ref[here] = out.astype(BF)

    return kernel_call(
        body,
        pos,
        (blocks,),
        (query, key, value, seg_k, seg_q),
        [at_lead(1, rows, width), at_lead(1, both, width), at_lead(1, both, width), full((both, 1)), full((1, rows))],
        [
            shape((rows, blocks * width), BF),
            shape((rows, blocks * width), F32),
            shape((blocks, heads, rows), F32),
        ],
        [at_cols(rows, width), at_cols(rows, width), at_lead(1, heads, rows)],
        [pltpu.VMEM((both, rows), F32)],
    )


def branch_call(lay, pos, mixed, tokens, b_out, gain, shift, weights, first, width):
    rows, dim = tokens.shape
    blocks = 2 * lay.nz
    n = len(weights)

    def body(pos_ref, mixed_ref, tok_ref, bias_ref, gain_ref, shift_ref, *rest):
        refs, (middle_ref, second_ref, whole, sem) = rest[:n], rest[n:]
        wants = ((first, width, whole),)
        all_loads(lay, pos_ref, refs, wants, sem)
        branch = dot_nt(mixed_ref[...], whole[...])
        middle = tok_ref[...].astype(F32) + branch + bias_ref[...]
        middle_ref[...] = middle
        second_ref[...] = (norm_parts(middle)[0] * gain_ref[...] + shift_ref[...]).astype(BF)

    return kernel_call(
        body,
        pos,
        (),
        (mixed, tokens, b_out, gain, shift, *weights),
        [full(mixed.shape), full(tokens.shape)] + [full((1, dim))] * 3 + [ANY] * n,
        [shape((rows, dim), F32), shape((rows, dim), BF)],
        [full((rows, dim)), full((rows, dim))],
        [pltpu.VMEM((dim, blocks * width), BF), pltpu.SemaphoreType.DMA((lay.nz, 1))],
    )


def up_call(lay, pos, second, b_up, weights, width):
    rows, dim = second.shape
    blocks = 2 * lay.nz
    n = len(weights)

    def body(pos_ref, second_ref, bias_ref, *rest):
        refs, (gelu_ref, slope_ref, whole, sem) = rest[:n], rest[n:]
        wants = ((0, width, whole),)
        dz = pl.program_id(0)

        stream_loads(lay, pos_ref, refs, wants, sem)
        z = z_place(dz, pos_ref)
        for x in range(2):
            here = slice(x * width, (x + 1) * width)
            cols = pl.ds(aligned((z * 2 + x) * width, width), width)
            u = dot(second_ref[...], whole[:, cols]) + bias_ref[:, here]
            scale = 0.7978845608028654
            square = u * u
            half = 0.5 + 0.5 * jnp.tanh(u * (scale + (scale * 0.044715) * square))
            gelu = u * half
            gelu_ref[:, here] = gelu.astype(BF)
            bend = 2.0 * scale + (6.0 * scale * 0.044715) * square
            slope_ref[:, here] = (half + gelu * (1.0 - half) * bend).astype(BF)

    return kernel_call(
        body,
        pos,
        (lay.nz,),
        (second, b_up, *weights),
        [full(second.shape), at_cols(1, 2 * width, z_place)] + [ANY] * n,
        [shape((rows, blocks * width), BF)] * 2,
        [at_cols(rows, 2 * width, z_place)] * 2,
        [pltpu.VMEM((dim, blocks * width), BF), pltpu.SemaphoreType.DMA((lay.nz, 1))],
    )


def result_call(lay, pos, gelu, middle, b_down, weights, width):
    rows, dim = middle.shape
    blocks = 2 * lay.nz
    n = len(weights)

    def body(pos_ref, gelu_ref, middle_ref, bias_ref, *rest):
        refs, (result_ref, whole, acc, sem) = rest[:n], rest[n:]
        wants = ((0, width, whole),)
        dz = pl.program_id(0)

        stream_loads(lay, pos_ref, refs, wants, sem)

        @pl.when(dz == 0)
        def _():
            acc[...] = middle_ref[...] + bias_ref[...]

        cols = pl.ds(aligned(z_place(dz, pos_ref) * 2 * width, width), 2 * width)
        acc[...] += dot_nt(gelu_ref[...], whole[:, cols])

        @pl.when(dz == lay.nz - 1)
        def _():
            result_ref[...] = acc[...].astype(BF)

    return kernel_call(
        body,
        pos,
        (lay.nz,),
        (gelu, middle, b_down, *weights),
        [at_cols(rows, 2 * width, z_place), full((rows, dim)), full((1, dim))] + [ANY] * n,
        [shape((rows, dim), BF)],
        [full((rows, dim))],
        [
            pltpu.VMEM((dim, blocks * width), BF),
            pltpu.VMEM((rows, dim), F32),
            pltpu.SemaphoreType.DMA((lay.nz, 1)),
        ],
    )[0]


def pre_call(lay, pos, slope, grad, weights, width):
    rows, dim = grad.shape
    blocks = 2 * lay.nz
    n = len(weights)

    def body(pos_ref, slope_ref, grad_ref, *rest):
        refs, (pre_ref, hidden_ref, whole, sem) = rest[:n], rest[n:]
        wants = ((0, width, whole),)
        dz = pl.program_id(0)

        stream_loads(lay, pos_ref, refs, wants, sem)
        cols = pl.ds(aligned(z_place(dz, pos_ref) * 2 * width, width), 2 * width)
        pre = (dot(grad_ref[...], whole[:, cols]) * slope_ref[...].astype(F32)).astype(BF)
        pre_ref[...] = pre
        hidden_ref[...] = jnp.sum(pre.astype(F32), axis=0, keepdims=True)

    return kernel_call(
        body,
        pos,
        (lay.nz,),
        (slope, grad, *weights),
        [at_cols(rows, 2 * width, z_place), full((rows, dim))] + [ANY] * n,
        [shape((rows, blocks * width), BF), shape((1, blocks * width), F32)],
        [at_cols(rows, 2 * width, z_place), at_cols(1, 2 * width, z_place)],
        [pltpu.VMEM((dim, blocks * width), BF), pltpu.SemaphoreType.DMA((lay.nz, 1))],
    )


def second_back_call(lay, pos, pre, grad, middle, gain, weights, width):
    rows, dim = middle.shape
    blocks = 2 * lay.nz
    n = len(weights)

    def body(pos_ref, pre_ref, grad_ref, middle_ref, gain_ref, *rest):
        refs, (mgrad_ref, low_ref, sums_ref, whole, acc, sem) = rest[:n], rest[n:]
        wants = ((0, width, whole),)
        dz = pl.program_id(0)

        stream_loads(lay, pos_ref, refs, wants, sem)

        @pl.when(dz == 0)
        def _():
            acc[...] = jnp.zeros_like(acc)

        cols = pl.ds(aligned(z_place(dz, pos_ref) * 2 * width, width), 2 * width)
        acc[...] += dot_nt(pre_ref[...], whole[:, cols])

        @pl.when(dz == lay.nz - 1)
        def _():
            unit, inverse = norm_parts(middle_ref[...])
            second_grad = acc[...]
            sums_ref[0:1] = jnp.sum(second_grad * unit, axis=0, keepdims=True)
            sums_ref[1:2] = jnp.sum(second_grad, axis=0, keepdims=True)
            out = grad_ref[...].astype(F32)
            sums_ref[3:4] = jnp.sum(out, axis=0, keepdims=True)
            out = out + norm_backward(second_grad, unit, inverse, gain_ref[...])
            sums_ref[2:3] = jnp.sum(out, axis=0, keepdims=True)
            mgrad_ref[...] = out
            low_ref[...] = out.astype(BF)

    return kernel_call(
        body,
        pos,
        (lay.nz,),
        (pre, grad, middle, gain, *weights),
        [at_cols(rows, 2 * width, z_place)] + [full((rows, dim))] * 2 + [full((1, dim))] + [ANY] * n,
        [shape((rows, dim), F32), shape((rows, dim), BF), shape((4, dim), F32)],
        [full((rows, dim))] * 2 + [full((4, dim))],
        [
            pltpu.VMEM((dim, blocks * width), BF),
            pltpu.VMEM((rows, dim), F32),
            pltpu.SemaphoreType.DMA((lay.nz, 1)),
        ],
    )


def mixed_grad_call(lay, pos, low, weights, first, width):
    rows, dim = low.shape
    blocks = 2 * lay.nz
    n = len(weights)

    def body(pos_ref, low_ref, *rest):
        refs, (out_ref, whole, sem) = rest[:n], rest[n:]
        wants = ((first, width, whole),)
        all_loads(lay, pos_ref, refs, wants, sem)
        out_ref[...] = dot(low_ref[...], whole[...]).astype(BF)

    return kernel_call(
        body,
        pos,
        (),
        (low, *weights),
        [full((rows, dim))] + [ANY] * n,
        [shape((rows, blocks * width), BF)],
        [full((rows, blocks * width))],
        [pltpu.VMEM((dim, blocks * width), BF), pltpu.SemaphoreType.DMA((lay.nz, 1))],
    )[0]


def attend_back_call(pos, span, query, key, value, seg_k, seg_q, lse, mixed_grad, exact, earlier=()):
    blocks, both, width = key.shape
    rows = query.shape[1]
    heads = width // HEAD_DIM
    step = min(rows, 256)
    begin = span[0]
    n = len(earlier)

    def body(pos_ref, q_ref, k_ref, v_ref, sk_ref, sq_ref, lse_ref, grad_ref, exact_ref, *rest):
        dq_ref, dk_ref, dv_ref, sums_ref, bias, dq_t, dk, dv = rest[n:]

        @pl.when(pl.program_id(0) == 0)
        def _():
            bias[...] = mask_bias(sk_ref[...], sq_ref[...], rows)

        key_t = k_ref[0].T
        inner_t = (grad_ref[...].astype(F32) * exact_ref[...]).T
        dk[...] = jnp.zeros_like(dk)
        dv[...] = jnp.zeros_like(dv)
        for tile in range(rows // step):
            here = slice(tile * step, (tile + 1) * step)
            keys = both - rows + (tile + 1) * step
            for head in range(heads):
                lanes = slice(head * HEAD_DIM, (head + 1) * HEAD_DIM)
                q_head = head_only(q_ref[0, here], head)
                g_head = head_only(grad_ref[here], head)
                scores = dot_nt(k_ref[0, :keys], q_head) + bias[:keys, here]
                probs = jnp.exp(scores - lse_ref[0, head : head + 1, here])
                prob_grad = dot_nt(v_ref[0, :keys], g_head)
                inner = jnp.sum(inner_t[lanes, here], axis=0, keepdims=True)
                score_grad = (probs * (prob_grad - inner)).astype(BF)
                dv[:keys] += dot(probs.astype(BF), g_head)
                dk[:keys] += dot(score_grad, q_head)
                dq_t[lanes, here] = dot(key_t[lanes, :keys], score_grad)
        dq = (dq_t[...].T * HEAD_DIM**-0.5).astype(BF)
        dv_low = dv[...].astype(BF)
        dq_ref[0] = dq
        dk_ref[0] = dk[...].astype(BF)
        dv_ref[0] = dv_low
        sums_ref[0:1] = jnp.sum(dq.astype(F32), axis=0, keepdims=True)
        sums_ref[1:2] = jnp.sum(dv_low.astype(F32), axis=0, keepdims=True)

    at = lambda k, pos: k + begin
    return kernel_call(
        body,
        pos,
        (span[1] - span[0],),
        (query, key, value, seg_k, seg_q, lse, mixed_grad, exact, *earlier),
        [
            at_lead(1, rows, width, place=at),
            at_lead(1, both, width, place=at),
            at_lead(1, both, width, place=at),
            full((both, 1)),
            full((1, rows)),
            at_lead(1, heads, rows, place=at),
            at_cols(rows, width, at),
            at_cols(rows, width, at),
        ]
        + [ANY] * n,
        [
            shape((blocks, rows, width), BF),
            shape((blocks, both, width), BF),
            shape((blocks, both, width), BF),
            shape((2, blocks * width), F32),
        ],
        [
            at_lead(1, rows, width, place=at),
            at_lead(1, both, width, place=at),
            at_lead(1, both, width, place=at),
            at_cols(2, width, at),
        ],
        [
            pltpu.VMEM((both, rows), F32),
            pltpu.VMEM((width, rows), F32),
            pltpu.VMEM((both, width), F32),
            pltpu.VMEM((both, width), F32),
        ],
        {9: 0, 10: 1, 11: 2, 12: 3} if n else {},
    )


def sides(ref, which, rows):
    here = slice(0, rows) if which == 0 else slice(rows, 2 * rows)
    return [ref[x, here] for x in range(2)]


def first_grad_prev_call(lay, pos, dk, dv, tokens, gain, weights, width):
    rows, dim = tokens.shape
    blocks = 2 * lay.nz
    n = len(weights)

    def body(pos_ref, dk_ref, dv_ref, tok_ref, gain_ref, *rest):
        refs, (grad_ref, sums_ref, whole, acc, sem) = rest[:n], rest[n:]
        wants = ((width, 2 * width, whole),)
        dz = pl.program_id(0)

        stream_loads(lay, pos_ref, refs, wants, sem)

        @pl.when(dz == 0)
        def _():
            acc[...] = jnp.zeros_like(acc)

        keys, values = sides(dk_ref, 0, rows), sides(dv_ref, 0, rows)
        part = jnp.concatenate([keys[0], values[0], keys[1], values[1]], axis=1)
        cols = pl.ds(aligned(z_place(dz, pos_ref) * 4 * width, width), 4 * width)
        acc[...] += dot_nt(part, whole[:, cols])

        @pl.when(dz == lay.nz - 1)
        def _():
            grad = acc[...]
            unit, inverse = norm_parts(tok_ref[...].astype(F32))
            grad_ref[...] = norm_backward(grad, unit, inverse, gain_ref[...]).astype(BF)
            sums_ref[0:1] = jnp.sum(grad * unit, axis=0, keepdims=True)
            sums_ref[1:2] = jnp.sum(grad, axis=0, keepdims=True)

    both = at_lead(2, rows, width, place=z_place)
    return kernel_call(
        body,
        pos,
        (lay.nz,),
        (dk, dv, tokens, gain, *weights),
        [both, both, full((rows, dim)), full((1, dim))] + [ANY] * n,
        [shape((rows, dim), BF), shape((2, dim), F32)],
        [full((rows, dim)), full((2, dim))],
        [
            pltpu.VMEM((dim, blocks * 2 * width), BF),
            pltpu.VMEM((rows, dim), F32),
            pltpu.SemaphoreType.DMA((lay.nz, 1)),
        ],
    )


def first_grad_own_call(lay, pos, dq, dk, dv, tokens, middle_grad, gain, weights, width):
    rows, dim = tokens.shape
    blocks = 2 * lay.nz
    n = len(weights)

    def body(pos_ref, dq_ref, dk_ref, dv_ref, tok_ref, middle_ref, gain_ref, *rest):
        refs, (grad_ref, sums_ref, whole_q, whole_kv, sem) = rest[:n], rest[n:]
        wants = ((0, width, whole_q), (width, 2 * width, whole_kv))
        dz = pl.program_id(0)

        stream_loads(lay, pos_ref, refs, wants, sem)

        @pl.when(dz == 0)
        def _():
            grad_ref[...] = jnp.zeros_like(grad_ref)

        z = z_place(dz, pos_ref)
        keys, values = sides(dk_ref, 1, rows), sides(dv_ref, 1, rows)
        part = jnp.concatenate([keys[0], values[0], keys[1], values[1]], axis=1)
        more = dot_nt(part, whole_kv[:, pl.ds(aligned(z * 4 * width, width), 4 * width)])
        part = jnp.concatenate([dq_ref[0], dq_ref[1]], axis=1)
        more += dot_nt(part, whole_q[:, pl.ds(aligned(z * 2 * width, width), 2 * width)])
        grad_ref[...] += more

        @pl.when(dz == lay.nz - 1)
        def _():
            grad = grad_ref[...]
            unit, inverse = norm_parts(tok_ref[...].astype(F32))
            sums_ref[0:1] = jnp.sum(grad * unit, axis=0, keepdims=True)
            sums_ref[1:2] = jnp.sum(grad, axis=0, keepdims=True)
            grad_ref[...] = middle_ref[...] + norm_backward(grad, unit, inverse, gain_ref[...])

    both = at_lead(2, 2 * rows, width, place=z_place)
    return kernel_call(
        body,
        pos,
        (lay.nz,),
        (dq, dk, dv, tokens, middle_grad, gain, *weights),
        [at_lead(2, rows, width, place=z_place), both, both]
        + [full((rows, dim))] * 2
        + [full((1, dim))]
        + [ANY] * n,
        [shape((rows, dim), F32), shape((2, dim), F32)],
        [full((rows, dim)), full((2, dim))],
        [
            pltpu.VMEM((dim, blocks * width), BF),
            pltpu.VMEM((dim, blocks * 2 * width), BF),
            pltpu.SemaphoreType.DMA((lay.nz, 2)),
        ],
    )


def half_grad_call(lay, pos, *, half, columns, lefts, tile, operands, specs, received):
    ny, nz, near, rows = lay.ny, lay.nz, lay.near, lay.rows
    n = len(operands)

    def body(pos_ref, *refs):
        ins, rest = refs[:n], refs[n:]
        got, rest = (rest[0], rest[1:]) if half == 0 else (None, rest)
        count = ny + 2 if half == 0 else 1
        outs, turned, spare = rest[:count], rest[count : count + len(lefts)], rest[count + len(lefts) :]
        dz = pl.program_id(0)

        @pl.when(dz == 0)
        def _():
            for index, ref in zip(lefts, turned):
                if rows % 128:
                    spare[0][...] = ins[index][...].T
                for dy in range(ny):
                    span = pl.ds(lay.row_start(pos_ref, dy, half), rows)
                    piece = spare[0][span] if rows % 128 else ins[index][:, span].T
                    ref[dy * rows : (dy + 1) * rows] = piece

        def make(put):
            blocks = tile(turned, ins, [lay.x_block(pos_ref, dx) for dx in range(2)])
            for dx in range(2):
                for dy in range(ny):
                    block = blocks[dx][dy * rows : (dy + 1) * rows]
                    if half == 0:
                        block = block + got[0, dx, dy].astype(F32)
                    put(dx, dy, block.astype(BF))

        if half == 1:

            def put(dx, dy, block):
                outs[0][0, dx, dy] = block

            make(put)
            return

        @pl.when(dz < near)
        def _():
            def put(dx, dy, block):
                outs[dy][0, dx] = block

            make(put)

        @pl.when(dz >= near)
        def _():
            def put(dx, dy, block):
                outs[ny + dx][0, dy] = block

            make(put)

    def step(*dims, at=lambda dz: dz):
        return pl.BlockSpec((1,) + dims, lambda dz, pos: (at(dz),) + (0,) * len(dims))

    if half == 0:
        operands = (*operands, received)
        specs = [*specs, step(2, ny, rows, columns)]
        outs = [shape((near, 2, rows, columns), BF)] * ny + [shape((nz - near, ny, rows, columns), BF)] * 2
        out_specs = [step(2, rows, columns, at=lambda dz: jnp.minimum(dz, near - 1))] * ny
        out_specs += [step(ny, rows, columns, at=lambda dz: jnp.maximum(dz - near, 0))] * 2
    else:
        outs = [shape((nz, 2, ny, rows, columns), BF)]
        out_specs = [step(2, ny, rows, columns)]
    scratch = [pltpu.VMEM((ny * rows, operands[index].shape[0]), BF) for index in lefts]
    if rows % 128:
        scratch.append(pltpu.VMEM(operands[lefts[0]].shape[::-1], BF))
    return kernel_call(body, pos, (nz,), operands, specs, outs, out_specs, scratch)


def sum_call(pos, groups, outs, build, steps=1):
    cut = lambda dims: (dims[0] // steps,) + dims[1:]
    spec = lambda r: pl.BlockSpec(cut(r.shape), lambda k, pos: (k,) + (0,) * (len(r.shape) - 1))
    flat = [r for g in groups for r in g]

    def body(pos_ref, *refs):
        ins, given = refs[: len(flat)], refs[len(flat) :]
        at, sums = 0, []
        for g in groups:
            mine = ins[at : at + len(g)]
            at += len(g)
            sums.append(lambda index, mine=mine: sum(
                (r[index].astype(F32) for r in mine[1:]), mine[0][index].astype(F32)
            ))
        build(sums, given)

    return kernel_call(
        body, pos, (steps,), flat, [spec(r) for r in flat], outs, [spec(o) for o in outs], [], {}, 63
    )


class Scatter:
    def __init__(self, lay, pos, columns, lefts, tile, operands, specs):
        self.lay, self.pos, self.columns = lay, pos, columns
        self.half = functools.partial(
            half_grad_call, lay, pos, columns=columns, lefts=lefts, tile=tile, operands=operands,
            specs=specs,
        )

    def away(self):
        self.sent = self.half(half=1, received=None)[0]

    def swap(self):
        self.received = trade(self.sent, "c", 2, 1)

    def own(self):
        parts = self.half(half=0, received=self.received)
        self.top, self.low = parts[: self.lay.ny], parts[self.lay.ny :]

    def send_one(self):
        self.top = [self.top[0]] + [trade(self.top[d], "fy", self.lay.ny, d) for d in range(1, self.lay.ny)]
        self.low = [self.low[0], trade(self.low[1], "tx", 2, 1)]

    def sum_one(self):
        ny, rows, near, far = self.lay.ny, self.lay.rows, self.lay.near, self.lay.nz - self.lay.near

        def build(sums, given):
            for dx in range(2):
                given[dx][...] = sums[0]((slice(None), dx)).astype(BF)
            for dy in range(ny):
                given[2 + dy][...] = sums[1]((slice(None), dy)).astype(BF)

        outs = [shape((near, rows, self.columns), BF)] * 2 + [shape((far, rows, self.columns), BF)] * ny
        out = sum_call(self.pos, [self.top, self.low], outs, build, near if near == far else 1)
        self.top, self.low = out[:2], out[2:]

    def send_two(self):
        self.top = [self.top[0], trade(self.top[1], "tx", 2, 1)]
        self.low = [self.low[0]] + [trade(self.low[d], "fy", self.lay.ny, d) for d in range(1, self.lay.ny)]

    def sum_two(self):
        near, nz = self.lay.near, self.lay.nz

        def build(sums, given):
            for dz in range(nz):
                given[dz][...] = (sums[0](dz) if dz < near else sums[1](dz - near)).astype(BF)

        outs = [shape((self.lay.rows, self.columns), BF)] * nz
        self.top = sum_call(self.pos, [self.top, self.low], outs, build)
        self.low = []

    def send_three(self):
        self.top = [self.top[0]] + [trade(self.top[d], "tz", self.lay.nz, d) for d in range(1, self.lay.nz)]

    def sum_three(self, cuts):
        rows = self.lay.rows
        outs = [shape((c[0], rows, c[1]) if isinstance(c, tuple) else (rows, c), F32) for c in cuts]

        def build(sums, given):
            at = 0
            for ref, c in zip(given, cuts):
                if isinstance(c, tuple):
                    for i in range(c[0]):
                        ref[i] = sums[0]((slice(None), slice(at, at + c[1])))
                        at += c[1]
                else:
                    ref[...] = sums[0]((slice(None), slice(at, at + c)))
                    at += c

        self.out = sum_call(self.pos, [self.top], outs, build)


def per_device(
    sizes,
    tokens,
    segment_ids,
    w_qkv,
    b_qv,
    w_out,
    b_out,
    w_up,
    b_up,
    w_down,
    b_down,
    ln1_gain,
    ln1_shift,
    ln2_gain,
    ln2_shift,
    grad_out,
):
    ny, nz = sizes
    rows, dim = tokens.shape
    length = segment_ids.shape[1]
    width = w_qkv.shape[2]
    hidden = w_up.shape[1]
    lay = Layout(ny, nz, w_qkv.shape[0])
    axes = ("fy", "c", "tz", "tx")
    pos = jnp.stack([lax.axis_index(axis) for axis in axes]).astype(jnp.int32)
    row = lambda v: v.reshape(1, -1)

    blocks = 2 * nz
    half = nz
    up_parts = [lax.all_gather(jnp.concatenate([w_up, w_out], axis=1), axes, axis=0, tiled=False)]
    qkv = Gather(lay, w_qkv.reshape(lay.rows, 3 * width))
    down = Gather(lay, w_down)
    qkv.one()
    tokens_prev = lax.ppermute(tokens, "tx", [(0, 1)])
    tokens_prev = stage(qkv, tokens_prev)
    qkv.two()
    qkv.three()
    qkv.swap(0)

    sequence = (pos[2] * 2 + pos[3]) // 2
    later = pos[3] > 0
    ids = lax.dynamic_slice_in_dim(segment_ids, sequence, 1, 0)
    seg_q = jnp.where(later, ids[:, rows:], ids[:, :rows])
    seg_prev = jnp.where(later, ids[:, :rows], -1)
    seg_k = jnp.concatenate([seg_prev, seg_q], axis=1).reshape(length, 1)
    both = jnp.concatenate([tokens_prev, tokens], axis=0).astype(F32)
    first = (norm_parts(both)[0] * ln1_gain + ln1_shift).astype(BF)
    first, seg_k, seg_q = stage(qkv, down, first, seg_k, seg_q)
    qkv.swap(1)
    down.one()
    qkv.parts, first = stage(qkv.parts, first)
    query, key, value = qkv_call(lay, pos, first, b_qv[0:1], b_qv[1:2], qkv.parts, width)
    mixed, exact, lse = attend_call(pos, query, key, value, seg_k, seg_q)
    mixed, up_parts = stage(down, mixed, up_parts)
    down.two()
    middle, second = branch_call(
        lay, pos, mixed, tokens, row(b_out), row(ln2_gain), row(ln2_shift), up_parts, hidden, width
    )
    middle, second = stage(down, middle, second)
    down.three()
    down.swap(0)
    gelu, slope = up_call(lay, pos, second, row(b_up), up_parts, hidden)

    whole = lambda v: full(v.shape)
    at_z = lambda size: at_cols(rows, 2 * size, z_place)
    block = lambda ref, x, size: ref[:, pl.ds(aligned(x * size, size), size)]

    def down_tile(left, ins, xs):
        return [dot(left[0][...], block(ins[1], x, hidden)) for x in xs]

    grad_down = Scatter(
        lay, pos, hidden, (0,), down_tile, (grad_out, gelu), [whole(grad_out), at_z(hidden)]
    )
    grad_down.away()
    grad_down.sent, slope, down.twin = stage(down, grad_down.sent, slope, down.twin)
    down.swap(1)
    slope, down.parts, grad_down.sent = stage(slope, down.parts, grad_down.sent)
    grad_down.swap()
    pre, grad_b_up = pre_call(lay, pos, slope, grad_out, down.parts, hidden)
    grad_down.received, pre = stage(grad_down.received, pre)
    grad_down.own()
    pre = stage(grad_down, pre)
    grad_down.send_one()
    middle_grad, middle_low, sums2 = second_back_call(
        lay, pos, pre, grad_out, middle, row(ln2_gain), up_parts, hidden
    )

    def up_tile(left, ins, xs):
        tail = dot(left[1][...], jnp.concatenate([block(ins[3], x, width) for x in xs], axis=1))
        return [
            jnp.concatenate(
                [dot(left[0][...], block(ins[1], x, hidden)), tail[:, i * width : (i + 1) * width]], axis=1
            )
            for i, x in enumerate(xs)
        ]

    grad_up = Scatter(
        lay, pos, hidden + width, (0, 2), up_tile, (second, pre, middle_low, mixed),
        [whole(second), at_z(hidden), whole(middle_low), at_z(width)],
    )
    mixed_grad = mixed_grad_call(lay, pos, middle_low, up_parts, hidden, width)
    grad_up.away()
    grad_up.sent, mixed_grad = stage(grad_down, grad_up.sent, mixed_grad)
    grad_down.sum_one()
    grad_up.sent, mixed_grad = stage(grad_down, grad_up.sent, mixed_grad)
    grad_down.send_two()
    grad_up.swap()
    partial = attend_back_call(pos, (0, half), query, key, value, seg_k, seg_q, lse, mixed_grad, exact)
    partial, grad_up.received = stage(grad_down, partial, grad_up.received)
    grad_down.sum_two()
    grad_up.own()
    partial = stage(grad_up, grad_down, partial)
    grad_up.send_one()
    grad_down.send_three()
    dq, dk, dv, sums_qv = attend_back_call(
        pos, (half, blocks), query, key, value, seg_k, seg_q, lse, mixed_grad, exact, partial
    )

    def qkv_tile(left, ins, xs):
        late = left[0][:, rows:]
        q = dot(late, jnp.concatenate([ins[1][x] for x in xs], axis=1))
        out = []
        for i, x in enumerate(xs):
            kv = dot(left[0][...], jnp.concatenate([ins[2][x], ins[3][x]], axis=1))
            out.append(jnp.concatenate([q[:, i * width : (i + 1) * width], kv], axis=1))
        return out

    grad_qkv = Scatter(
        lay, pos, 3 * width, (0,), qkv_tile, (first, dq, dk, dv),
        [
            whole(first),
            at_lead(2, rows, width, place=z_place),
            at_lead(2, 2 * rows, width, place=z_place),
            at_lead(2, 2 * rows, width, place=z_place),
        ],
    )
    grad_qkv.away()
    grad_qkv.sent, dq, dk, dv = stage(grad_up, grad_down, grad_qkv.sent, dq, dk, dv)
    grad_up.sum_one()
    grad_qkv.sent, dq, dk, dv = stage(grad_up, grad_qkv.sent, dq, dk, dv)
    grad_up.send_two()
    grad_qkv.swap()
    grad_down.sum_three((hidden,))
    grad_qkv.received, grad_down.out, dq, dk, dv = stage(
        grad_qkv.received, grad_down.out, dq, dk, dv
    )
    grad_qkv.own()
    dq, dk, dv = stage(grad_qkv, grad_up, dq, dk, dv)
    grad_qkv.send_one()
    grad_up.sum_two()
    dq, dk, dv = stage(grad_up, dq, dk, dv)
    grad_up.send_three()
    first_grad, sums1 = first_grad_own_call(
        lay, pos, dq, dk, dv, tokens, middle_grad, row(ln1_gain), qkv.parts, width
    )
    nearer = grad_up.top[: nz - 1]
    nearer, first_grad, sums1, dk, dv = stage(grad_qkv, nearer, first_grad, sums1, dk, dv)
    grad_up.top = [*nearer, grad_up.top[-1]]
    grad_qkv.sum_one()
    dk, dv = stage(grad_qkv, dk, dv)
    grad_qkv.send_two()
    back, sums_prev = first_grad_prev_call(
        lay, pos, dk, dv, tokens_prev, row(ln1_gain), qkv.parts, width
    )
    back, sums_prev, gelu = stage(grad_qkv, back, sums_prev, gelu)
    small = jnp.concatenate(
        [v.reshape(-1) for v in (sums2, grad_b_up, sums1 + sums_prev, sums_qv)]
    ).reshape(-1, 128)
    small = small + trade(small, "c", 2, 1)
    grad_qkv.sum_two()
    small, back, gelu = stage(grad_qkv, grad_up, small, back, gelu)
    grad_qkv.send_three()
    pieces = around(small, "fy", ny)
    back = lax.ppermute(back, "tx", [(1, 0)])
    grad_up.sum_three((hidden, width))
    result = result_call(lay, pos, gelu, middle, row(b_down), down.parts, hidden)
    pieces, result, grad_up.out = stage(grad_qkv, pieces, result, grad_up.out)
    small = sum(pieces)
    small = small + trade(small, "tx", 2, 1)
    small = sum(around(small, "tz", nz)).reshape(-1)
    token_grad = (first_grad + back.astype(F32)).astype(BF)
    grad_qkv.sum_three(((3, width),))
    at = 4 * dim
    late = small[at + gelu.shape[1] :]
    return (
        result,
        token_grad,
        jnp.transpose(grad_qkv.out[0], (1, 0, 2)),
        late[2 * dim :].reshape(2, -1),
        grad_up.out[1],
        small[2 * dim : 3 * dim],
        grad_up.out[0],
        small[at : at + gelu.shape[1]],
        grad_down.out[0],
        small[3 * dim : at],
        late[:dim],
        late[dim : 2 * dim],
        small[:dim],
        small[dim : 2 * dim],
    )


def solution(mesh):
    n_fsdp, n_tp = mesh.devices.shape
    fine = Mesh(
        mesh.devices.reshape(n_fsdp // 2, 2, n_tp // 2, 2), ("fy", "c", "tz", "tx")
    )
    fsdp, tp, every = ("fy", "c"), ("tz", "tx"), ("fy", "c", "tz", "tx")
    tile = P(fsdp, tp)
    ins = (
        P(every, None),
        P(fsdp, None),
        P(fsdp, None, tp),
        P(),
        tile,
        P(),
        tile,
        P(),
        tile,
        P(),
        P(),
        P(),
        P(),
        P(),
        P(every, None),
    )
    outs = (
        P(every, None),
        P(every, None),
        P(fsdp, None, tp),
        P(),
        tile,
        P(),
        tile,
        P(),
        tile,
        P(),
        P(),
        P(),
        P(),
        P(),
    )
    return jax.shard_map(
        functools.partial(per_device, (n_fsdp // 2, n_tp // 2)),
        mesh=fine,
        in_specs=ins,
        out_specs=outs,
        check_vma=False,
    )
```

```python
import functools

import jax
import jax.numpy as jnp
from jax import lax
from jax.experimental import pallas as pl
from jax.experimental.pallas import tpu as pltpu
from jax.sharding import Mesh, PartitionSpec as P

HEAD_DIM = 64
EPS = 1e-05
BF = jnp.bfloat16
F32 = jnp.float32
NT = (((1,), (1,)), ((), ()))
TN = (((0,), (0,)), ((), ()))
MIB = 1 << 20


def dot(a, b):
    return jnp.dot(a, b, preferred_element_type=F32)


def dot_nt(a, b):
    return lax.dot_general(a, b, NT, preferred_element_type=F32)


def dot_tn(a, b):
    return lax.dot_general(a, b, TN, preferred_element_type=F32)


def aligned(value, multiple):
    return pl.multiple_of(value, multiple)


class Layout:
    def __init__(self, ny, nz, rows):
        self.ny, self.nz, self.rows = ny, nz, rows
        self.near = nz // 2

    def row_start(self, pos, dy, dc):
        block = lax.bitwise_xor(pos[0], jnp.int32(dy)) * 2 + lax.bitwise_xor(pos[1], jnp.int32(dc))
        return pl.multiple_of(block * self.rows, self.rows)

    def z_block(self, pos, dz):
        return lax.bitwise_xor(pos[2], jnp.int32(dz))

    def x_block(self, pos, dx):
        return lax.bitwise_xor(pos[3], jnp.int32(dx))


def trade(value, axis, size, distance):
    return lax.ppermute(value, axis, [(s, s ^ distance) for s in range(size)])


def around(value, axis, size):
    return [value] + [trade(value, axis, size, d) for d in range(1, size)]


class Gather:
    def __init__(self, lay, shard):
        self.lay, self.top, self.low = lay, [shard], []

    def one(self):
        near = self.lay.near
        pieces = around(self.top[0], "tz", self.lay.nz)
        self.top, self.low = pieces[:near], pieces[near:]

    def two(self):
        lay = self.lay
        self.top = around(jnp.stack(self.top), "tx", 2)
        self.low = around(jnp.stack(self.low), "fy", lay.ny)

    def three(self):
        lay = self.lay
        self.top = around(jnp.stack(self.top), "fy", lay.ny)
        self.low = around(jnp.stack(self.low), "tx", 2)

    def swap(self, which):
        if which == 0:
            self.twin = [trade(self.top[0], "c", 2, 1), trade(self.low[0], "c", 2, 1)]
        else:
            late = [trade(t, "c", 2, 1) for t in self.top[1:] + self.low[1:]]
            n = len(self.top) - 1
            self.parts = self.top + self.low + [self.twin[0], *late[:n], self.twin[1], *late[n:]]


def stage(*things):
    values = []
    for thing in things:
        values.append((thing.top, thing.low) if isinstance(thing, (Gather, Scatter)) else thing)
    values = lax.optimization_barrier(values)
    back = []
    for thing, value in zip(things, values):
        if isinstance(thing, (Gather, Scatter)):
            thing.top, thing.low = value
        else:
            back.append(value)
    return back[0] if len(back) == 1 else back


def start_loads(lay, pos, refs, wants, sem, dz):
    half = len(refs) // 2
    for dx in range(2):
        k = lay.z_block(pos, dz) * 2 + lay.x_block(pos, dx)
        for dc in range(2):
            mine = refs[dc * half : (dc + 1) * half]
            for dy in range(lay.ny):
                start = lay.row_start(pos, dy, dc)
                if len(refs) == 1:
                    block = refs[0].at[start // lay.rows * (2 * lay.nz) + k]
                elif dz < lay.near:
                    block = mine[dy].at[dx, dz]
                else:
                    block = mine[lay.ny + dx].at[dy, dz - lay.near]
                for i, (first, width, whole) in enumerate(wants):
                    pltpu.make_async_copy(
                        block.at[:, pl.ds(first, width)],
                        whole.at[pl.ds(start, lay.rows), pl.ds(aligned(k * width, width), width)],
                        sem.at[dz, i],
                    ).start()


def stream_loads(lay, pos, refs, wants, sem):
    step = pl.program_id(0)
    for dz in range(lay.nz):

        @pl.when(step == max(dz - 2, 0))
        def _(dz=dz):
            start_loads(lay, pos, refs, wants, sem, dz)

    wait_loads(lay, pos, step, wants, sem)


def all_loads(lay, pos, refs, wants, sem):
    for dz in range(lay.nz):
        start_loads(lay, pos, refs, wants, sem, dz)
    for dz in range(lay.nz):
        wait_loads(lay, pos, dz, wants, sem)


def wait_loads(lay, pos, dz, wants, sem):
    for i, (first, width, whole) in enumerate(wants):
        start = lax.bitwise_xor(pos[2], jnp.int32(dz)) * (2 * width)
        cols = whole.at[:, pl.ds(aligned(start, width), 2 * width)]
        pltpu.make_async_copy(cols, cols, sem.at[dz, i]).wait()


def kernel_call(body, pos, grid, ins, in_specs, outs, out_specs, scratch, aliases={}, room=60):
    return pl.pallas_call(
        body,
        out_shape=outs,
        grid_spec=pltpu.PrefetchScalarGridSpec(
            num_scalar_prefetch=1,
            grid=grid,
            in_specs=in_specs,
            out_specs=out_specs,
            scratch_shapes=scratch,
        ),
        input_output_aliases=aliases,
        compiler_params=pltpu.CompilerParams(
            dimension_semantics=("arbitrary",) * len(grid), vmem_limit_bytes=room * MIB
        ),
        cost_estimate=pl.CostEstimate(flops=1000, bytes_accessed=1000, transcendentals=0),
    )(pos, *ins)


def shape(dims, dtype):
    return jax.ShapeDtypeStruct(dims, dtype)


def full(dims):
    return pl.BlockSpec(dims, lambda *_: (0,) * len(dims))


def at_cols(rows, width, place=lambda k, pos: k):
    return pl.BlockSpec((rows, width), lambda k, pos: (0, place(k, pos)))


def at_lead(lead, *dims, place=lambda k, pos: k):
    return pl.BlockSpec((lead,) + dims, lambda k, pos: (place(k, pos),) + (0,) * len(dims))


def z_place(k, pos):
    return lax.bitwise_xor(pos[2], k)


ANY = pl.BlockSpec(memory_space=pl.ANY)


def norm_parts(values):
    centred = values - jnp.mean(values, axis=-1, keepdims=True)
    inverse = lax.rsqrt(jnp.mean(centred * centred, axis=-1, keepdims=True) + EPS)
    return centred * inverse, inverse


def norm_backward(grad, unit, inverse, gain):
    scaled = grad * gain
    return inverse * (
        scaled
        - jnp.mean(scaled, axis=-1, keepdims=True)
        - unit * jnp.mean(scaled * unit, axis=-1, keepdims=True)
    )


def qkv_call(lay, pos, first, bias_q, bias_v, weights, width):
    both, dim = first.shape
    rows = both // 2
    blocks = 2 * lay.nz
    n = len(weights)

    def body(pos_ref, first_ref, bq_ref, bv_ref, *rest):
        refs, (q_ref, k_ref, v_ref, whole_q, whole_kv, sem) = rest[:n], rest[n:]
        wants = ((0, width, whole_q), (width, 2 * width, whole_kv))
        dz = pl.program_id(0)

        stream_loads(lay, pos_ref, refs, wants, sem)
        z = z_place(dz, pos_ref)
        kv = dot(first_ref[...], whole_kv[:, pl.ds(aligned(z * 4 * width, width), 4 * width)])
        q = dot(first_ref[rows:], whole_q[:, pl.ds(aligned(z * 2 * width, width), 2 * width)])
        q = ((q + bq_ref[...]).astype(BF) * HEAD_DIM**-0.5).astype(BF)
        for x in range(2):
            q_ref[x] = q[:, x * width : (x + 1) * width]
            k_ref[x] = kv[:, 2 * x * width : (2 * x + 1) * width].astype(BF)
            bias = bv_ref[:, x * width : (x + 1) * width]
            v_ref[x] = (kv[:, (2 * x + 1) * width : (2 * x + 2) * width] + bias).astype(BF)

    return kernel_call(
        body,
        pos,
        (lay.nz,),
        (first, bias_q, bias_v, *weights),
        [full((both, dim)), at_cols(1, 2 * width, z_place), at_cols(1, 2 * width, z_place)] + [ANY] * n,
        [
            shape((blocks, rows, width), BF),
            shape((blocks, both, width), BF),
            shape((blocks, both, width), BF),
        ],
        [
            at_lead(2, rows, width, place=z_place),
            at_lead(2, both, width, place=z_place),
            at_lead(2, both, width, place=z_place),
        ],
        [
            pltpu.VMEM((dim, blocks * width), BF),
            pltpu.VMEM((dim, blocks * 2 * width), BF),
            pltpu.SemaphoreType.DMA((lay.nz, 2)),
        ],
    )


def mask_bias(seg_k, seg_q, rows):
    both = seg_k.shape[0]
    key_at = lax.broadcasted_iota(jnp.int32, (both, rows), 0) - (both - rows)
    query_at = lax.broadcasted_iota(jnp.int32, (both, rows), 1)
    return jnp.where((seg_k == seg_q) & (key_at <= query_at), 0.0, -1e30).astype(F32)


def head_only(block, head):
    lane = lax.broadcasted_iota(jnp.int32, block.shape, 1)
    inside = (lane >= head * HEAD_DIM) & (lane < (head + 1) * HEAD_DIM)
    return jnp.where(inside, block, jnp.zeros_like(block))


def attend_call(pos, query, key, value, seg_k, seg_q):
    blocks, both, width = key.shape
    rows = query.shape[1]
    heads = width // HEAD_DIM
    step = min(rows, 128)

    def body(pos_ref, q_ref, k_ref, v_ref, sk_ref, sq_ref, mixed_ref, exact_ref, probs_ref, bias):
        @pl.when(pl.program_id(0) == 0)
        def _():
            bias[...] = mask_bias(sk_ref[...], sq_ref[...], rows)

        for tile in range(rows // step):
            here = slice(tile * step, (tile + 1) * step)
            keys = both - rows + (tile + 1) * step
            outs = []
            for head in range(heads):
                scores = dot_nt(k_ref[0, :keys], head_only(q_ref[0, here], head)) + bias[:keys, here]
                top = jnp.max(scores, axis=0, keepdims=True)
                expo = jnp.exp(scores - top)
                total = jnp.sum(expo, axis=0, keepdims=True)
                probs = (expo * (1.0 / total)).astype(BF)
                outs.append(dot_tn(probs, v_ref[0, :keys]))
                probs_ref[0, head, :keys, here] = probs
                end = both - rows + min(rows, (tile // 2 + 1) * 2 * step)
                if end > keys:
                    probs_ref[0, head, keys:end, here] = jnp.zeros((end - keys, step), BF)
            lane = lax.broadcasted_iota(jnp.int32, outs[0].shape, 1)
            out = outs[0]
            for head in range(1, heads):
                out = jnp.where(lane < head * HEAD_DIM, out, outs[head])
            exact_ref[here] = out
            mixed_ref[here] = out.astype(BF)

    return kernel_call(
        body,
        pos,
        (blocks,),
        (query, key, value, seg_k, seg_q),
        [at_lead(1, rows, width), at_lead(1, both, width), at_lead(1, both, width), full((both, 1)), full((1, rows))],
        [
            shape((rows, blocks * width), BF),
            shape((rows, blocks * width), F32),
            shape((blocks, heads, both, rows), BF),
        ],
        [at_cols(rows, width), at_cols(rows, width), at_lead(1, heads, both, rows)],
        [pltpu.VMEM((both, rows), F32)],
    )


def branch_call(lay, pos, mixed, tokens, b_out, gain, shift, weights, first, width):
    rows, dim = tokens.shape
    blocks = 2 * lay.nz
    n = len(weights)

    def body(pos_ref, mixed_ref, tok_ref, bias_ref, gain_ref, shift_ref, *rest):
        refs, (middle_ref, second_ref, whole, sem) = rest[:n], rest[n:]
        wants = ((first, width, whole),)
        all_loads(lay, pos_ref, refs, wants, sem)
        branch = dot_nt(mixed_ref[...], whole[...])
        middle = tok_ref[...].astype(F32) + branch + bias_ref[...]
        middle_ref[...] = middle
        second_ref[...] = (norm_parts(middle)[0] * gain_ref[...] + shift_ref[...]).astype(BF)

    return kernel_call(
        body,
        pos,
        (),
        (mixed, tokens, b_out, gain, shift, *weights),
        [full(mixed.shape), full(tokens.shape)] + [full((1, dim))] * 3 + [ANY] * n,
        [shape((rows, dim), F32), shape((rows, dim), BF)],
        [full((rows, dim)), full((rows, dim))],
        [pltpu.VMEM((dim, blocks * width), BF), pltpu.SemaphoreType.DMA((lay.nz, 1))],
    )


def up_call(lay, pos, second, b_up, weights, width):
    rows, dim = second.shape
    blocks = 2 * lay.nz
    n = len(weights)

    def body(pos_ref, second_ref, bias_ref, *rest):
        refs, (gelu_ref, slope_ref, whole, sem) = rest[:n], rest[n:]
        wants = ((0, width, whole),)
        dz = pl.program_id(0)

        stream_loads(lay, pos_ref, refs, wants, sem)
        z = z_place(dz, pos_ref)
        for x in range(2):
            here = slice(x * width, (x + 1) * width)
            cols = pl.ds(aligned((z * 2 + x) * width, width), width)
            u = dot(second_ref[...], whole[:, cols]) + bias_ref[:, here]
            scale = 0.7978845608028654
            square = u * u
            half = 0.5 + 0.5 * jnp.tanh(u * (scale + (scale * 0.044715) * square))
            gelu = u * half
            gelu_ref[:, here] = gelu.astype(BF)
            bend = 2.0 * scale + (6.0 * scale * 0.044715) * square
            slope_ref[:, here] = (half + gelu * (1.0 - half) * bend).astype(BF)

    return kernel_call(
        body,
        pos,
        (lay.nz,),
        (second, b_up, *weights),
        [full(second.shape), at_cols(1, 2 * width, z_place)] + [ANY] * n,
        [shape((rows, blocks * width), BF)] * 2,
        [at_cols(rows, 2 * width, z_place)] * 2,
        [pltpu.VMEM((dim, blocks * width), BF), pltpu.SemaphoreType.DMA((lay.nz, 1))],
    )


def result_call(lay, pos, gelu, middle, b_down, weights, width):
    rows, dim = middle.shape
    blocks = 2 * lay.nz
    n = len(weights)

    def body(pos_ref, gelu_ref, middle_ref, bias_ref, *rest):
        refs, (result_ref, whole, acc, sem) = rest[:n], rest[n:]
        wants = ((0, width, whole),)
        dz = pl.program_id(0)

        stream_loads(lay, pos_ref, refs, wants, sem)

        @pl.when(dz == 0)
        def _():
            acc[...] = middle_ref[...] + bias_ref[...]

        cols = pl.ds(aligned(z_place(dz, pos_ref) * 2 * width, width), 2 * width)
        acc[...] += dot_nt(gelu_ref[...], whole[:, cols])

        @pl.when(dz == lay.nz - 1)
        def _():
            result_ref[...] = acc[...].astype(BF)

    return kernel_call(
        body,
        pos,
        (lay.nz,),
        (gelu, middle, b_down, *weights),
        [at_cols(rows, 2 * width, z_place), full((rows, dim)), full((1, dim))] + [ANY] * n,
        [shape((rows, dim), BF)],
        [full((rows, dim))],
        [
            pltpu.VMEM((dim, blocks * width), BF),
            pltpu.VMEM((rows, dim), F32),
            pltpu.SemaphoreType.DMA((lay.nz, 1)),
        ],
    )[0]


def pre_call(lay, pos, slope, grad, weights, width):
    rows, dim = grad.shape
    blocks = 2 * lay.nz
    n = len(weights)

    def body(pos_ref, slope_ref, grad_ref, *rest):
        refs, (pre_ref, hidden_ref, whole, sem) = rest[:n], rest[n:]
        wants = ((0, width, whole),)
        dz = pl.program_id(0)

        stream_loads(lay, pos_ref, refs, wants, sem)
        cols = pl.ds(aligned(z_place(dz, pos_ref) * 2 * width, width), 2 * width)
        pre = (dot(grad_ref[...], whole[:, cols]) * slope_ref[...].astype(F32)).astype(BF)
        pre_ref[...] = pre
        hidden_ref[...] = jnp.sum(pre.astype(F32), axis=0, keepdims=True)

    return kernel_call(
        body,
        pos,
        (lay.nz,),
        (slope, grad, *weights),
        [at_cols(rows, 2 * width, z_place), full((rows, dim))] + [ANY] * n,
        [shape((rows, blocks * width), BF), shape((1, blocks * width), F32)],
        [at_cols(rows, 2 * width, z_place), at_cols(1, 2 * width, z_place)],
        [pltpu.VMEM((dim, blocks * width), BF), pltpu.SemaphoreType.DMA((lay.nz, 1))],
    )


def second_back_call(lay, pos, pre, grad, middle, gain, weights, width):
    rows, dim = middle.shape
    blocks = 2 * lay.nz
    n = len(weights)

    def body(pos_ref, pre_ref, grad_ref, middle_ref, gain_ref, *rest):
        refs, (mgrad_ref, low_ref, sums_ref, whole, acc, sem) = rest[:n], rest[n:]
        wants = ((0, width, whole),)
        dz = pl.program_id(0)

        stream_loads(lay, pos_ref, refs, wants, sem)

        @pl.when(dz == 0)
        def _():
            acc[...] = jnp.zeros_like(acc)

        cols = pl.ds(aligned(z_place(dz, pos_ref) * 2 * width, width), 2 * width)
        acc[...] += dot_nt(pre_ref[...], whole[:, cols])

        @pl.when(dz == lay.nz - 1)
        def _():
            unit, inverse = norm_parts(middle_ref[...])
            second_grad = acc[...]
            sums_ref[0:1] = jnp.sum(second_grad * unit, axis=0, keepdims=True)
            sums_ref[1:2] = jnp.sum(second_grad, axis=0, keepdims=True)
            out = grad_ref[...].astype(F32)
            sums_ref[3:4] = jnp.sum(out, axis=0, keepdims=True)
            out = out + norm_backward(second_grad, unit, inverse, gain_ref[...])
            sums_ref[2:3] = jnp.sum(out, axis=0, keepdims=True)
            mgrad_ref[...] = out
            low_ref[...] = out.astype(BF)

    return kernel_call(
        body,
        pos,
        (lay.nz,),
        (pre, grad, middle, gain, *weights),
        [at_cols(rows, 2 * width, z_place)] + [full((rows, dim))] * 2 + [full((1, dim))] + [ANY] * n,
        [shape((rows, dim), F32), shape((rows, dim), BF), shape((4, dim), F32)],
        [full((rows, dim))] * 2 + [full((4, dim))],
        [
            pltpu.VMEM((dim, blocks * width), BF),
            pltpu.VMEM((rows, dim), F32),
            pltpu.SemaphoreType.DMA((lay.nz, 1)),
        ],
    )


def mixed_grad_call(lay, pos, low, weights, first, width):
    rows, dim = low.shape
    blocks = 2 * lay.nz
    n = len(weights)

    def body(pos_ref, low_ref, *rest):
        refs, (out_ref, whole, sem) = rest[:n], rest[n:]
        wants = ((first, width, whole),)
        all_loads(lay, pos_ref, refs, wants, sem)
        out_ref[...] = dot(low_ref[...], whole[...]).astype(BF)

    return kernel_call(
        body,
        pos,
        (),
        (low, *weights),
        [full((rows, dim))] + [ANY] * n,
        [shape((rows, blocks * width), BF)],
        [full((rows, blocks * width))],
        [pltpu.VMEM((dim, blocks * width), BF), pltpu.SemaphoreType.DMA((lay.nz, 1))],
    )[0]


def attend_back_call(pos, span, query, key, value, probs, mixed_grad, exact, earlier=()):
    blocks, both, width = key.shape
    rows = query.shape[1]
    heads = width // HEAD_DIM
    step = min(rows, 256)
    begin = span[0]
    n = len(earlier)

    def body(pos_ref, q_ref, k_ref, v_ref, p_ref, grad_ref, exact_ref, *rest):
        dq_ref, dk_ref, dv_ref, sums_ref, dq_t, dk, dv = rest[n:]

        key_t = k_ref[0].T
        inner_t = (grad_ref[...].astype(F32) * exact_ref[...]).T
        dk[...] = jnp.zeros_like(dk)
        dv[...] = jnp.zeros_like(dv)
        for tile in range(rows // step):
            here = slice(tile * step, (tile + 1) * step)
            keys = both - rows + (tile + 1) * step
            for head in range(heads):
                lanes = slice(head * HEAD_DIM, (head + 1) * HEAD_DIM)
                q_head = head_only(q_ref[0, here], head)
                g_head = head_only(grad_ref[here], head)
                low = p_ref[0, head, :keys, here]
                prob_grad = dot_nt(v_ref[0, :keys], g_head)
                inner = jnp.sum(inner_t[lanes, here], axis=0, keepdims=True)
                score_grad = (low.astype(F32) * (prob_grad - inner)).astype(BF)
                dv[:keys] += dot(low, g_head)
                dk[:keys] += dot(score_grad, q_head)
                dq_t[lanes, here] = dot(key_t[lanes, :keys], score_grad)
        dq = (dq_t[...].T * HEAD_DIM**-0.5).astype(BF)
        dv_low = dv[...].astype(BF)
        dq_ref[0] = dq
        dk_ref[0] = dk[...].astype(BF)
        dv_ref[0] = dv_low
        sums_ref[0:1] = jnp.sum(dq.astype(F32), axis=0, keepdims=True)
        sums_ref[1:2] = jnp.sum(dv_low.astype(F32), axis=0, keepdims=True)

    at = lambda k, pos: k + begin
    return kernel_call(
        body,
        pos,
        (span[1] - span[0],),
        (query, key, value, probs, mixed_grad, exact, *earlier),
        [
            at_lead(1, rows, width, place=at),
            at_lead(1, both, width, place=at),
            at_lead(1, both, width, place=at),
            at_lead(1, heads, both, rows, place=at),
            at_cols(rows, width, at),
            at_cols(rows, width, at),
        ]
        + [ANY] * n,
        [
            shape((blocks, rows, width), BF),
            shape((blocks, both, width), BF),
            shape((blocks, both, width), BF),
            shape((2, blocks * width), F32),
        ],
        [
            at_lead(1, rows, width, place=at),
            at_lead(1, both, width, place=at),
            at_lead(1, both, width, place=at),
            at_cols(2, width, at),
        ],
        [
            pltpu.VMEM((width, rows), F32),
            pltpu.VMEM((both, width), F32),
            pltpu.VMEM((both, width), F32),
        ],
        {7: 0, 8: 1, 9: 2, 10: 3} if n else {},
    )


def sides(ref, which, rows):
    here = slice(0, rows) if which == 0 else slice(rows, 2 * rows)
    return [ref[x, here] for x in range(2)]


def first_grad_prev_call(lay, pos, dk, dv, tokens, gain, weights, width):
    rows, dim = tokens.shape
    blocks = 2 * lay.nz
    n = len(weights)

    def body(pos_ref, dk_ref, dv_ref, tok_ref, gain_ref, *rest):
        refs, (grad_ref, sums_ref, whole, acc, sem) = rest[:n], rest[n:]
        wants = ((width, 2 * width, whole),)
        dz = pl.program_id(0)

        stream_loads(lay, pos_ref, refs, wants, sem)

        @pl.when(dz == 0)
        def _():
            acc[...] = jnp.zeros_like(acc)

        keys, values = sides(dk_ref, 0, rows), sides(dv_ref, 0, rows)
        part = jnp.concatenate([keys[0], values[0], keys[1], values[1]], axis=1)
        cols = pl.ds(aligned(z_place(dz, pos_ref) * 4 * width, width), 4 * width)
        acc[...] += dot_nt(part, whole[:, cols])

        @pl.when(dz == lay.nz - 1)
        def _():
            grad = acc[...]
            unit, inverse = norm_parts(tok_ref[...].astype(F32))
            grad_ref[...] = norm_backward(grad, unit, inverse, gain_ref[...]).astype(BF)
            sums_ref[0:1] = jnp.sum(grad * unit, axis=0, keepdims=True)
            sums_ref[1:2] = jnp.sum(grad, axis=0, keepdims=True)

    both = at_lead(2, rows, width, place=z_place)
    return kernel_call(
        body,
        pos,
        (lay.nz,),
        (dk, dv, tokens, gain, *weights),
        [both, both, full((rows, dim)), full((1, dim))] + [ANY] * n,
        [shape((rows, dim), BF), shape((2, dim), F32)],
        [full((rows, dim)), full((2, dim))],
        [
            pltpu.VMEM((dim, blocks * 2 * width), BF),
            pltpu.VMEM((rows, dim), F32),
            pltpu.SemaphoreType.DMA((lay.nz, 1)),
        ],
    )


def first_grad_own_call(lay, pos, dq, dk, dv, tokens, middle_grad, gain, weights, width):
    rows, dim = tokens.shape
    blocks = 2 * lay.nz
    n = len(weights)

    def body(pos_ref, dq_ref, dk_ref, dv_ref, tok_ref, middle_ref, gain_ref, *rest):
        refs, (grad_ref, sums_ref, whole_q, whole_kv, sem) = rest[:n], rest[n:]
        wants = ((0, width, whole_q), (width, 2 * width, whole_kv))
        dz = pl.program_id(0)

        stream_loads(lay, pos_ref, refs, wants, sem)

        @pl.when(dz == 0)
        def _():
            grad_ref[...] = jnp.zeros_like(grad_ref)

        z = z_place(dz, pos_ref)
        keys, values = sides(dk_ref, 1, rows), sides(dv_ref, 1, rows)
        part = jnp.concatenate([keys[0], values[0], keys[1], values[1]], axis=1)
        more = dot_nt(part, whole_kv[:, pl.ds(aligned(z * 4 * width, width), 4 * width)])
        part = jnp.concatenate([dq_ref[0], dq_ref[1]], axis=1)
        more += dot_nt(part, whole_q[:, pl.ds(aligned(z * 2 * width, width), 2 * width)])
        grad_ref[...] += more

        @pl.when(dz == lay.nz - 1)
        def _():
            grad = grad_ref[...]
            unit, inverse = norm_parts(tok_ref[...].astype(F32))
            sums_ref[0:1] = jnp.sum(grad * unit, axis=0, keepdims=True)
            sums_ref[1:2] = jnp.sum(grad, axis=0, keepdims=True)
            grad_ref[...] = middle_ref[...] + norm_backward(grad, unit, inverse, gain_ref[...])

    both = at_lead(2, 2 * rows, width, place=z_place)
    return kernel_call(
        body,
        pos,
        (lay.nz,),
        (dq, dk, dv, tokens, middle_grad, gain, *weights),
        [at_lead(2, rows, width, place=z_place), both, both]
        + [full((rows, dim))] * 2
        + [full((1, dim))]
        + [ANY] * n,
        [shape((rows, dim), F32), shape((2, dim), F32)],
        [full((rows, dim)), full((2, dim))],
        [
            pltpu.VMEM((dim, blocks * width), BF),
            pltpu.VMEM((dim, blocks * 2 * width), BF),
            pltpu.SemaphoreType.DMA((lay.nz, 2)),
        ],
    )


def half_grad_call(lay, pos, *, half, columns, lefts, tile, operands, specs, received):
    ny, nz, near, rows = lay.ny, lay.nz, lay.near, lay.rows
    n = len(operands)

    def body(pos_ref, *refs):
        ins, rest = refs[:n], refs[n:]
        got, rest = (rest[0], rest[1:]) if half == 0 else (None, rest)
        count = ny + 2 if half == 0 else 1
        outs, turned, spare = rest[:count], rest[count : count + len(lefts)], rest[count + len(lefts) :]
        dz = pl.program_id(0)

        @pl.when(dz == 0)
        def _():
            for index, ref in zip(lefts, turned):
                if rows % 128:
                    spare[0][...] = ins[index][...].T
                for dy in range(ny):
                    span = pl.ds(lay.row_start(pos_ref, dy, half), rows)
                    piece = spare[0][span] if rows % 128 else ins[index][:, span].T
                    ref[dy * rows : (dy + 1) * rows] = piece

        def make(put):
            blocks = tile(turned, ins, [lay.x_block(pos_ref, dx) for dx in range(2)])
            for dx in range(2):
                for dy in range(ny):
                    block = blocks[dx][dy * rows : (dy + 1) * rows]
                    if half == 0:
                        block = block + got[0, dx, dy].astype(F32)
                    put(dx, dy, block.astype(BF))

        if half == 1:

            def put(dx, dy, block):
                outs[0][0, dx, dy] = block

            make(put)
            return

        @pl.when(dz < near)
        def _():
            def put(dx, dy, block):
                outs[dy][0, dx] = block

            make(put)

        @pl.when(dz >= near)
        def _():
            def put(dx, dy, block):
                outs[ny + dx][0, dy] = block

            make(put)

    def step(*dims, at=lambda dz: dz):
        return pl.BlockSpec((1,) + dims, lambda dz, pos: (at(dz),) + (0,) * len(dims))

    if half == 0:
        operands = (*operands, received)
        specs = [*specs, step(2, ny, rows, columns)]
        outs = [shape((near, 2, rows, columns), BF)] * ny + [shape((nz - near, ny, rows, columns), BF)] * 2
        out_specs = [step(2, rows, columns, at=lambda dz: jnp.minimum(dz, near - 1))] * ny
        out_specs += [step(ny, rows, columns, at=lambda dz: jnp.maximum(dz - near, 0))] * 2
    else:
        outs = [shape((nz, 2, ny, rows, columns), BF)]
        out_specs = [step(2, ny, rows, columns)]
    scratch = [pltpu.VMEM((ny * rows, operands[index].shape[0]), BF) for index in lefts]
    if rows % 128:
        scratch.append(pltpu.VMEM(operands[lefts[0]].shape[::-1], BF))
    return kernel_call(body, pos, (nz,), operands, specs, outs, out_specs, scratch)


def sum_call(pos, groups, outs, build, steps=1):
    cut = lambda dims: (dims[0] // steps,) + dims[1:]
    spec = lambda r: pl.BlockSpec(cut(r.shape), lambda k, pos: (k,) + (0,) * (len(r.shape) - 1))
    flat = [r for g in groups for r in g]

    def body(pos_ref, *refs):
        ins, given = refs[: len(flat)], refs[len(flat) :]
        at, sums = 0, []
        for g in groups:
            mine = ins[at : at + len(g)]
            at += len(g)
            sums.append(lambda index, mine=mine: sum(
                (r[index].astype(F32) for r in mine[1:]), mine[0][index].astype(F32)
            ))
        build(sums, given)

    return kernel_call(
        body, pos, (steps,), flat, [spec(r) for r in flat], outs, [spec(o) for o in outs], [], {}, 63
    )


class Scatter:
    def __init__(self, lay, pos, columns, lefts, tile, operands, specs):
        self.lay, self.pos, self.columns = lay, pos, columns
        self.half = functools.partial(
            half_grad_call, lay, pos, columns=columns, lefts=lefts, tile=tile, operands=operands,
            specs=specs,
        )

    def away(self):
        self.sent = self.half(half=1, received=None)[0]

    def swap(self):
        self.received = trade(self.sent, "c", 2, 1)

    def own(self):
        parts = self.half(half=0, received=self.received)
        self.top, self.low = parts[: self.lay.ny], parts[self.lay.ny :]

    def send_one(self):
        self.top = [self.top[0]] + [trade(self.top[d], "fy", self.lay.ny, d) for d in range(1, self.lay.ny)]
        self.low = [self.low[0], trade(self.low[1], "tx", 2, 1)]

    def sum_one(self):
        ny, rows, near, far = self.lay.ny, self.lay.rows, self.lay.near, self.lay.nz - self.lay.near

        def build(sums, given):
            for dx in range(2):
                given[dx][...] = sums[0]((slice(None), dx)).astype(BF)
            for dy in range(ny):
                given[2 + dy][...] = sums[1]((slice(None), dy)).astype(BF)

        outs = [shape((near, rows, self.columns), BF)] * 2 + [shape((far, rows, self.columns), BF)] * ny
        out = sum_call(self.pos, [self.top, self.low], outs, build, near if near == far else 1)
        self.top, self.low = out[:2], out[2:]

    def send_two(self):
        self.top = [self.top[0], trade(self.top[1], "tx", 2, 1)]
        self.low = [self.low[0]] + [trade(self.low[d], "fy", self.lay.ny, d) for d in range(1, self.lay.ny)]

    def sum_two(self):
        near, nz = self.lay.near, self.lay.nz

        def build(sums, given):
            for dz in range(nz):
                given[dz][...] = (sums[0](dz) if dz < near else sums[1](dz - near)).astype(BF)

        outs = [shape((self.lay.rows, self.columns), BF)] * nz
        self.top = sum_call(self.pos, [self.top, self.low], outs, build)
        self.low = []

    def send_three(self):
        self.top = [self.top[0]] + [trade(self.top[d], "tz", self.lay.nz, d) for d in range(1, self.lay.nz)]

    def sum_three(self, cuts):
        rows = self.lay.rows
        outs = [shape((c[0], rows, c[1]) if isinstance(c, tuple) else (rows, c), F32) for c in cuts]

        def build(sums, given):
            at = 0
            for ref, c in zip(given, cuts):
                if isinstance(c, tuple):
                    for i in range(c[0]):
                        ref[i] = sums[0]((slice(None), slice(at, at + c[1])))
                        at += c[1]
                else:
                    ref[...] = sums[0]((slice(None), slice(at, at + c)))
                    at += c

        self.out = sum_call(self.pos, [self.top], outs, build)


def per_device(
    sizes,
    tokens,
    segment_ids,
    w_qkv,
    b_qv,
    w_out,
    b_out,
    w_up,
    b_up,
    w_down,
    b_down,
    ln1_gain,
    ln1_shift,
    ln2_gain,
    ln2_shift,
    grad_out,
):
    ny, nz = sizes
    rows, dim = tokens.shape
    length = segment_ids.shape[1]
    width = w_qkv.shape[2]
    hidden = w_up.shape[1]
    lay = Layout(ny, nz, w_qkv.shape[0])
    axes = ("fy", "c", "tz", "tx")
    pos = jnp.stack([lax.axis_index(axis) for axis in axes]).astype(jnp.int32)
    row = lambda v: v.reshape(1, -1)

    blocks = 2 * nz
    half = nz
    up_parts = [lax.all_gather(jnp.concatenate([w_up, w_out], axis=1), axes, axis=0, tiled=False)]
    qkv = Gather(lay, w_qkv.reshape(lay.rows, 3 * width))
    down = Gather(lay, w_down)
    qkv.one()
    tokens_prev = lax.ppermute(tokens, "tx", [(0, 1)])
    tokens_prev = stage(qkv, tokens_prev)
    qkv.two()
    qkv.three()
    qkv.swap(0)

    sequence = (pos[2] * 2 + pos[3]) // 2
    later = pos[3] > 0
    ids = lax.dynamic_slice_in_dim(segment_ids, sequence, 1, 0)
    seg_q = jnp.where(later, ids[:, rows:], ids[:, :rows])
    seg_prev = jnp.where(later, ids[:, :rows], -1)
    seg_k = jnp.concatenate([seg_prev, seg_q], axis=1).reshape(length, 1)
    both = jnp.concatenate([tokens_prev, tokens], axis=0).astype(F32)
    first = (norm_parts(both)[0] * ln1_gain + ln1_shift).astype(BF)
    first, seg_k, seg_q = stage(qkv, down, first, seg_k, seg_q)
    qkv.swap(1)
    down.one()
    qkv.parts, first = stage(qkv.parts, first)
    query, key, value = qkv_call(lay, pos, first, b_qv[0:1], b_qv[1:2], qkv.parts, width)
    mixed, exact, probs = attend_call(pos, query, key, value, seg_k, seg_q)
    mixed, up_parts = stage(down, mixed, up_parts)
    down.two()
    middle, second = branch_call(
        lay, pos, mixed, tokens, row(b_out), row(ln2_gain), row(ln2_shift), up_parts, hidden, width
    )
    middle, second = stage(down, middle, second)
    down.three()
    down.swap(0)
    gelu, slope = up_call(lay, pos, second, row(b_up), up_parts, hidden)

    whole = lambda v: full(v.shape)
    at_z = lambda size: at_cols(rows, 2 * size, z_place)
    block = lambda ref, x, size: ref[:, pl.ds(aligned(x * size, size), size)]

    def down_tile(left, ins, xs):
        return [dot(left[0][...], block(ins[1], x, hidden)) for x in xs]

    grad_down = Scatter(
        lay, pos, hidden, (0,), down_tile, (grad_out, gelu), [whole(grad_out), at_z(hidden)]
    )
    grad_down.away()
    grad_down.sent, slope, down.twin = stage(down, grad_down.sent, slope, down.twin)
    down.swap(1)
    slope, down.parts, grad_down.sent = stage(slope, down.parts, grad_down.sent)
    grad_down.swap()
    pre, grad_b_up = pre_call(lay, pos, slope, grad_out, down.parts, hidden)
    grad_down.received, pre = stage(grad_down.received, pre)
    grad_down.own()
    pre = stage(grad_down, pre)
    grad_down.send_one()
    middle_grad, middle_low, sums2 = second_back_call(
        lay, pos, pre, grad_out, middle, row(ln2_gain), up_parts, hidden
    )

    def up_tile(left, ins, xs):
        tail = dot(left[1][...], jnp.concatenate([block(ins[3], x, width) for x in xs], axis=1))
        return [
            jnp.concatenate(
                [dot(left[0][...], block(ins[1], x, hidden)), tail[:, i * width : (i + 1) * width]], axis=1
            )
            for i, x in enumerate(xs)
        ]

    grad_up = Scatter(
        lay, pos, hidden + width, (0, 2), up_tile, (second, pre, middle_low, mixed),
        [whole(second), at_z(hidden), whole(middle_low), at_z(width)],
    )
    mixed_grad = mixed_grad_call(lay, pos, middle_low, up_parts, hidden, width)
    grad_up.away()
    grad_up.sent, mixed_grad = stage(grad_down, grad_up.sent, mixed_grad)
    grad_down.sum_one()
    grad_up.sent, mixed_grad = stage(grad_down, grad_up.sent, mixed_grad)
    grad_down.send_two()
    grad_up.swap()
    partial = attend_back_call(pos, (0, half), query, key, value, probs, mixed_grad, exact)
    partial, grad_up.received = stage(grad_down, partial, grad_up.received)
    grad_down.sum_two()
    grad_up.own()
    partial = stage(grad_up, grad_down, partial)
    grad_up.send_one()
    grad_down.send_three()
    dq, dk, dv, sums_qv = attend_back_call(
        pos, (half, blocks), query, key, value, probs, mixed_grad, exact, partial
    )

    def qkv_tile(left, ins, xs):
        late = left[0][:, rows:]
        q = dot(late, jnp.concatenate([ins[1][x] for x in xs], axis=1))
        out = []
        for i, x in enumerate(xs):
            kv = dot(left[0][...], jnp.concatenate([ins[2][x], ins[3][x]], axis=1))
            out.append(jnp.concatenate([q[:, i * width : (i + 1) * width], kv], axis=1))
        return out

    grad_qkv = Scatter(
        lay, pos, 3 * width, (0,), qkv_tile, (first, dq, dk, dv),
        [
            whole(first),
            at_lead(2, rows, width, place=z_place),
            at_lead(2, 2 * rows, width, place=z_place),
            at_lead(2, 2 * rows, width, place=z_place),
        ],
    )
    grad_qkv.away()
    grad_qkv.sent, dq, dk, dv = stage(grad_up, grad_down, grad_qkv.sent, dq, dk, dv)
    grad_up.sum_one()
    grad_qkv.sent, dq, dk, dv = stage(grad_up, grad_qkv.sent, dq, dk, dv)
    grad_up.send_two()
    grad_qkv.swap()
    grad_down.sum_three((hidden,))
    grad_qkv.received, grad_down.out, dq, dk, dv = stage(
        grad_qkv.received, grad_down.out, dq, dk, dv
    )
    grad_qkv.own()
    dq, dk, dv = stage(grad_qkv, grad_up, dq, dk, dv)
    grad_qkv.send_one()
    grad_up.sum_two()
    dq, dk, dv = stage(grad_up, dq, dk, dv)
    grad_up.send_three()
    first_grad, sums1 = first_grad_own_call(
        lay, pos, dq, dk, dv, tokens, middle_grad, row(ln1_gain), qkv.parts, width
    )
    nearer = grad_up.top[: nz - 1]
    nearer, first_grad, sums1, dk, dv = stage(grad_qkv, nearer, first_grad, sums1, dk, dv)
    grad_up.top = [*nearer, grad_up.top[-1]]
    grad_qkv.sum_one()
    dk, dv = stage(grad_qkv, dk, dv)
    grad_qkv.send_two()
    back, sums_prev = first_grad_prev_call(
        lay, pos, dk, dv, tokens_prev, row(ln1_gain), qkv.parts, width
    )
    back, sums_prev, gelu = stage(grad_qkv, back, sums_prev, gelu)
    small = jnp.concatenate(
        [v.reshape(-1) for v in (sums2, grad_b_up, sums1 + sums_prev, sums_qv)]
    ).reshape(-1, 128)
    small = small + trade(small, "c", 2, 1)
    grad_qkv.sum_two()
    small, back, gelu = stage(grad_qkv, grad_up, small, back, gelu)
    grad_qkv.send_three()
    pieces = around(small, "fy", ny)
    back = lax.ppermute(back, "tx", [(1, 0)])
    grad_up.sum_three((hidden, width))
    result = result_call(lay, pos, gelu, middle, row(b_down), down.parts, hidden)
    pieces, result, back, grad_up.out = stage(grad_qkv, pieces, result, back, grad_up.out)
    small = sum(pieces)
    token_grad = (first_grad + back.astype(F32)).astype(BF)
    small = small + trade(small, "tx", 2, 1)
    small, token_grad = stage(small, token_grad)
    small = sum(around(small, "tz", nz)).reshape(-1)
    grad_qkv.sum_three(((3, width),))
    at = 4 * dim
    late = small[at + gelu.shape[1] :]
    return (
        result,
        token_grad,
        jnp.transpose(grad_qkv.out[0], (1, 0, 2)),
        late[2 * dim :].reshape(2, -1),
        grad_up.out[1],
        small[2 * dim : 3 * dim],
        grad_up.out[0],
        small[at : at + gelu.shape[1]],
        grad_down.out[0],
        small[3 * dim : at],
        late[:dim],
        late[dim : 2 * dim],
        small[:dim],
        small[dim : 2 * dim],
    )


def solution(mesh):
    n_fsdp, n_tp = mesh.devices.shape
    fine = Mesh(
        mesh.devices.reshape(n_fsdp // 2, 2, n_tp // 2, 2), ("fy", "c", "tz", "tx")
    )
    fsdp, tp, every = ("fy", "c"), ("tz", "tx"), ("fy", "c", "tz", "tx")
    tile = P(fsdp, tp)
    ins = (
        P(every, None),
        P(fsdp, None),
        P(fsdp, None, tp),
        P(),
        tile,
        P(),
        tile,
        P(),
        tile,
        P(),
        P(),
        P(),
        P(),
        P(),
        P(every, None),
    )
    outs = (
        P(every, None),
        P(every, None),
        P(fsdp, None, tp),
        P(),
        tile,
        P(),
        tile,
        P(),
        tile,
        P(),
        P(),
        P(),
        P(),
        P(),
    )
    return jax.shard_map(
        functools.partial(per_device, (n_fsdp // 2, n_tp // 2)),
        mesh=fine,
        in_specs=ins,
        out_specs=outs,
        check_vma=False,
    )
```

```python
import functools

import jax
import jax.numpy as jnp
from jax import lax
from jax.experimental import pallas as pl
from jax.experimental.pallas import tpu as pltpu
from jax.sharding import Mesh, PartitionSpec as P

HEAD_DIM = 64
EPS = 1e-05
BF = jnp.bfloat16
F32 = jnp.float32
NT = (((1,), (1,)), ((), ()))
TN = (((0,), (0,)), ((), ()))
MIB = 1 << 20


def dot(a, b):
    return jnp.dot(a, b, preferred_element_type=F32)


def dot_nt(a, b):
    return lax.dot_general(a, b, NT, preferred_element_type=F32)


def dot_tn(a, b):
    return lax.dot_general(a, b, TN, preferred_element_type=F32)


def aligned(value, multiple):
    return pl.multiple_of(value, multiple)


class Layout:
    def __init__(self, ny, nz, rows):
        self.ny, self.nz, self.rows = ny, nz, rows
        self.near = nz // 2

    def row_start(self, pos, dy, dc):
        block = lax.bitwise_xor(pos[0], jnp.int32(dy)) * 2 + lax.bitwise_xor(pos[1], jnp.int32(dc))
        return pl.multiple_of(block * self.rows, self.rows)

    def z_block(self, pos, dz):
        return lax.bitwise_xor(pos[2], jnp.int32(dz))

    def x_block(self, pos, dx):
        return lax.bitwise_xor(pos[3], jnp.int32(dx))


def trade(value, axis, size, distance):
    return lax.ppermute(value, axis, [(s, s ^ distance) for s in range(size)])


def around(value, axis, size):
    return [value] + [trade(value, axis, size, d) for d in range(1, size)]


class Gather:
    def __init__(self, lay, shard):
        self.lay, self.top, self.low = lay, [shard], []

    def one(self):
        near = self.lay.near
        pieces = around(self.top[0], "tz", self.lay.nz)
        self.top, self.low = pieces[:near], pieces[near:]

    def two(self):
        lay = self.lay
        self.top = around(jnp.stack(self.top), "tx", 2)
        self.low = around(jnp.stack(self.low), "fy", lay.ny)

    def three(self):
        lay = self.lay
        self.top = around(jnp.stack(self.top), "fy", lay.ny)
        self.low = around(jnp.stack(self.low), "tx", 2)

    def swap(self, which):
        if which == 0:
            self.twin = [trade(self.top[0], "c", 2, 1), trade(self.low[0], "c", 2, 1)]
        else:
            late = [trade(t, "c", 2, 1) for t in self.top[1:] + self.low[1:]]
            n = len(self.top) - 1
            self.parts = self.top + self.low + [self.twin[0], *late[:n], self.twin[1], *late[n:]]


def stage(*things):
    values = []
    for thing in things:
        values.append((thing.top, thing.low) if isinstance(thing, (Gather, Scatter)) else thing)
    values = lax.optimization_barrier(values)
    back = []
    for thing, value in zip(things, values):
        if isinstance(thing, (Gather, Scatter)):
            thing.top, thing.low = value
        else:
            back.append(value)
    return back[0] if len(back) == 1 else back


def start_loads(lay, pos, refs, wants, sem, dz):
    half = len(refs) // 2
    for dx in range(2):
        k = lay.z_block(pos, dz) * 2 + lay.x_block(pos, dx)
        for dc in range(2):
            mine = refs[dc * half : (dc + 1) * half]
            for dy in range(lay.ny):
                start = lay.row_start(pos, dy, dc)
                if len(refs) == 1:
                    block = refs[0].at[start // lay.rows * (2 * lay.nz) + k]
                elif dz < lay.near:
                    block = mine[dy].at[dx, dz]
                else:
                    block = mine[lay.ny + dx].at[dy, dz - lay.near]
                for i, (first, width, whole) in enumerate(wants):
                    pltpu.make_async_copy(
                        block.at[:, pl.ds(first, width)],
                        whole.at[pl.ds(start, lay.rows), pl.ds(aligned(k * width, width), width)],
                        sem.at[dz, i],
                    ).start()


def stream_loads(lay, pos, refs, wants, sem):
    step = pl.program_id(0)
    for dz in range(lay.nz):

        @pl.when(step == max(dz - 2, 0))
        def _(dz=dz):
            start_loads(lay, pos, refs, wants, sem, dz)

    wait_loads(lay, pos, step, wants, sem)


def all_loads(lay, pos, refs, wants, sem):
    for dz in range(lay.nz):
        start_loads(lay, pos, refs, wants, sem, dz)
    for dz in range(lay.nz):
        wait_loads(lay, pos, dz, wants, sem)


def wait_loads(lay, pos, dz, wants, sem):
    for i, (first, width, whole) in enumerate(wants):
        start = lax.bitwise_xor(pos[2], jnp.int32(dz)) * (2 * width)
        cols = whole.at[:, pl.ds(aligned(start, width), 2 * width)]
        pltpu.make_async_copy(cols, cols, sem.at[dz, i]).wait()


def kernel_call(body, pos, grid, ins, in_specs, outs, out_specs, scratch, aliases={}, room=60):
    return pl.pallas_call(
        body,
        out_shape=outs,
        grid_spec=pltpu.PrefetchScalarGridSpec(
            num_scalar_prefetch=1,
            grid=grid,
            in_specs=in_specs,
            out_specs=out_specs,
            scratch_shapes=scratch,
        ),
        input_output_aliases=aliases,
        compiler_params=pltpu.CompilerParams(
            dimension_semantics=("arbitrary",) * len(grid), vmem_limit_bytes=room * MIB
        ),
        cost_estimate=pl.CostEstimate(flops=1000, bytes_accessed=1000, transcendentals=0),
    )(pos, *ins)


def shape(dims, dtype):
    return jax.ShapeDtypeStruct(dims, dtype)


def full(dims):
    return pl.BlockSpec(dims, lambda *_: (0,) * len(dims))


def at_cols(rows, width, place=lambda k, pos: k):
    return pl.BlockSpec((rows, width), lambda k, pos: (0, place(k, pos)))


def at_lead(lead, *dims, place=lambda k, pos: k):
    return pl.BlockSpec((lead,) + dims, lambda k, pos: (place(k, pos),) + (0,) * len(dims))


def z_place(k, pos):
    return lax.bitwise_xor(pos[2], k)


ANY = pl.BlockSpec(memory_space=pl.ANY)


def norm_parts(values):
    centred = values - jnp.mean(values, axis=-1, keepdims=True)
    inverse = lax.rsqrt(jnp.mean(centred * centred, axis=-1, keepdims=True) + EPS)
    return centred * inverse, inverse


def norm_backward(grad, unit, inverse, gain):
    scaled = grad * gain
    return inverse * (
        scaled
        - jnp.mean(scaled, axis=-1, keepdims=True)
        - unit * jnp.mean(scaled * unit, axis=-1, keepdims=True)
    )


def qkv_call(lay, pos, first, bias_q, bias_v, weights, width):
    both, dim = first.shape
    rows = both // 2
    blocks = 2 * lay.nz
    n = len(weights)

    def body(pos_ref, first_ref, bq_ref, bv_ref, *rest):
        refs, (q_ref, k_ref, v_ref, whole_q, whole_kv, sem) = rest[:n], rest[n:]
        wants = ((0, width, whole_q), (width, 2 * width, whole_kv))
        dz = pl.program_id(0)

        stream_loads(lay, pos_ref, refs, wants, sem)
        z = z_place(dz, pos_ref)
        kv = dot(first_ref[...], whole_kv[:, pl.ds(aligned(z * 4 * width, width), 4 * width)])
        q = dot(first_ref[rows:], whole_q[:, pl.ds(aligned(z * 2 * width, width), 2 * width)])
        q = ((q + bq_ref[...]).astype(BF) * HEAD_DIM**-0.5).astype(BF)
        for x in range(2):
            q_ref[x] = q[:, x * width : (x + 1) * width]
            k_ref[x] = kv[:, 2 * x * width : (2 * x + 1) * width].astype(BF)
            bias = bv_ref[:, x * width : (x + 1) * width]
            v_ref[x] = (kv[:, (2 * x + 1) * width : (2 * x + 2) * width] + bias).astype(BF)

    return kernel_call(
        body,
        pos,
        (lay.nz,),
        (first, bias_q, bias_v, *weights),
        [full((both, dim)), at_cols(1, 2 * width, z_place), at_cols(1, 2 * width, z_place)] + [ANY] * n,
        [
            shape((blocks, rows, width), BF),
            shape((blocks, both, width), BF),
            shape((blocks, both, width), BF),
        ],
        [
            at_lead(2, rows, width, place=z_place),
            at_lead(2, both, width, place=z_place),
            at_lead(2, both, width, place=z_place),
        ],
        [
            pltpu.VMEM((dim, blocks * width), BF),
            pltpu.VMEM((dim, blocks * 2 * width), BF),
            pltpu.SemaphoreType.DMA((lay.nz, 2)),
        ],
    )


def mask_bias(seg_k, seg_q, rows):
    both = seg_k.shape[0]
    key_at = lax.broadcasted_iota(jnp.int32, (both, rows), 0) - (both - rows)
    query_at = lax.broadcasted_iota(jnp.int32, (both, rows), 1)
    return jnp.where((seg_k == seg_q) & (key_at <= query_at), 0.0, -1e30).astype(F32)


def head_only(block, head):
    lane = lax.broadcasted_iota(jnp.int32, block.shape, 1)
    inside = (lane >= head * HEAD_DIM) & (lane < (head + 1) * HEAD_DIM)
    return jnp.where(inside, block, jnp.zeros_like(block))


def attend_call(pos, query, key, value, seg_k, seg_q):
    blocks, both, width = key.shape
    rows = query.shape[1]
    heads = width // HEAD_DIM
    step = min(rows, 128)

    def body(pos_ref, q_ref, k_ref, v_ref, sk_ref, sq_ref, mixed_ref, exact_ref, lse_ref, bias):
        @pl.when(pl.program_id(0) == 0)
        def _():
            bias[...] = mask_bias(sk_ref[...], sq_ref[...], rows)

        for tile in range(rows // step):
            here = slice(tile * step, (tile + 1) * step)
            keys = both - rows + (tile + 1) * step
            outs = []
            for head in range(heads):
                scores = dot_nt(k_ref[0, :keys], head_only(q_ref[0, here], head)) + bias[:keys, here]
                top = jnp.max(scores, axis=0, keepdims=True)
                expo = jnp.exp(scores - top)
                total = jnp.sum(expo, axis=0, keepdims=True)
                share = jnp.broadcast_to(1.0 / total, (8, step)).T[:, :1]
                outs.append(dot_tn(expo.astype(BF), v_ref[0, :keys]) * share)
                lse_ref[0, head : head + 1, here] = top + jnp.log(total)
            lane = lax.broadcasted_iota(jnp.int32, outs[0].shape, 1)
            out = outs[0]
            for head in range(1, heads):
                out = jnp.where(lane < head * HEAD_DIM, out, outs[head])
            exact_ref[here] = out
            mixed_ref[here] = out.astype(BF)

    return kernel_call(
        body,
        pos,
        (blocks,),
        (query, key, value, seg_k, seg_q),
        [at_lead(1, rows, width), at_lead(1, both, width), at_lead(1, both, width), full((both, 1)), full((1, rows))],
        [
            shape((rows, blocks * width), BF),
            shape((rows, blocks * width), F32),
            shape((blocks, heads, rows), F32),
        ],
        [at_cols(rows, width), at_cols(rows, width), at_lead(1, heads, rows)],
        [pltpu.VMEM((both, rows), F32)],
    )


def branch_call(lay, pos, mixed, tokens, b_out, gain, shift, weights, first, width):
    rows, dim = tokens.shape
    blocks = 2 * lay.nz
    n = len(weights)

    def body(pos_ref, mixed_ref, tok_ref, bias_ref, gain_ref, shift_ref, *rest):
        refs, (middle_ref, second_ref, whole, sem) = rest[:n], rest[n:]
        wants = ((first, width, whole),)
        all_loads(lay, pos_ref, refs, wants, sem)
        branch = dot_nt(mixed_ref[...], whole[...])
        middle = tok_ref[...].astype(F32) + branch + bias_ref[...]
        middle_ref[...] = middle
        second_ref[...] = (norm_parts(middle)[0] * gain_ref[...] + shift_ref[...]).astype(BF)

    return kernel_call(
        body,
        pos,
        (),
        (mixed, tokens, b_out, gain, shift, *weights),
        [full(mixed.shape), full(tokens.shape)] + [full((1, dim))] * 3 + [ANY] * n,
        [shape((rows, dim), F32), shape((rows, dim), BF)],
        [full((rows, dim)), full((rows, dim))],
        [pltpu.VMEM((dim, blocks * width), BF), pltpu.SemaphoreType.DMA((lay.nz, 1))],
    )


def up_call(lay, pos, second, b_up, weights, width):
    rows, dim = second.shape
    blocks = 2 * lay.nz
    n = len(weights)

    def body(pos_ref, second_ref, bias_ref, *rest):
        refs, (gelu_ref, slope_ref, whole, sem) = rest[:n], rest[n:]
        wants = ((0, width, whole),)
        dz = pl.program_id(0)

        stream_loads(lay, pos_ref, refs, wants, sem)
        z = z_place(dz, pos_ref)
        for x in range(2):
            here = slice(x * width, (x + 1) * width)
            cols = pl.ds(aligned((z * 2 + x) * width, width), width)
            u = dot(second_ref[...], whole[:, cols]) + bias_ref[:, here]
            scale = 0.7978845608028654
            square = u * u
            half = 0.5 + 0.5 * jnp.tanh(u * (scale + (scale * 0.044715) * square))
            gelu = u * half
            gelu_ref[:, here] = gelu.astype(BF)
            bend = 2.0 * scale + (6.0 * scale * 0.044715) * square
            slope_ref[:, here] = (half + gelu * (1.0 - half) * bend).astype(BF)

    return kernel_call(
        body,
        pos,
        (lay.nz,),
        (second, b_up, *weights),
        [full(second.shape), at_cols(1, 2 * width, z_place)] + [ANY] * n,
        [shape((rows, blocks * width), BF)] * 2,
        [at_cols(rows, 2 * width, z_place)] * 2,
        [pltpu.VMEM((dim, blocks * width), BF), pltpu.SemaphoreType.DMA((lay.nz, 1))],
    )


def result_call(lay, pos, gelu, middle, b_down, weights, width):
    rows, dim = middle.shape
    blocks = 2 * lay.nz
    n = len(weights)

    def body(pos_ref, gelu_ref, middle_ref, bias_ref, *rest):
        refs, (result_ref, whole, acc, sem) = rest[:n], rest[n:]
        wants = ((0, width, whole),)
        dz = pl.program_id(0)

        stream_loads(lay, pos_ref, refs, wants, sem)

        @pl.when(dz == 0)
        def _():
            acc[...] = middle_ref[...] + bias_ref[...]

        cols = pl.ds(aligned(z_place(dz, pos_ref) * 2 * width, width), 2 * width)
        acc[...] += dot_nt(gelu_ref[...], whole[:, cols])

        @pl.when(dz == lay.nz - 1)
        def _():
            result_ref[...] = acc[...].astype(BF)

    return kernel_call(
        body,
        pos,
        (lay.nz,),
        (gelu, middle, b_down, *weights),
        [at_cols(rows, 2 * width, z_place), full((rows, dim)), full((1, dim))] + [ANY] * n,
        [shape((rows, dim), BF)],
        [full((rows, dim))],
        [
            pltpu.VMEM((dim, blocks * width), BF),
            pltpu.VMEM((rows, dim), F32),
            pltpu.SemaphoreType.DMA((lay.nz, 1)),
        ],
    )[0]


def pre_call(lay, pos, slope, grad, weights, width):
    rows, dim = grad.shape
    blocks = 2 * lay.nz
    n = len(weights)

    def body(pos_ref, slope_ref, grad_ref, *rest):
        refs, (pre_ref, hidden_ref, whole, sem) = rest[:n], rest[n:]
        wants = ((0, width, whole),)
        dz = pl.program_id(0)

        stream_loads(lay, pos_ref, refs, wants, sem)
        cols = pl.ds(aligned(z_place(dz, pos_ref) * 2 * width, width), 2 * width)
        pre = (dot(grad_ref[...], whole[:, cols]) * slope_ref[...].astype(F32)).astype(BF)
        pre_ref[...] = pre
        hidden_ref[...] = jnp.sum(pre.astype(F32), axis=0, keepdims=True)

    return kernel_call(
        body,
        pos,
        (lay.nz,),
        (slope, grad, *weights),
        [at_cols(rows, 2 * width, z_place), full((rows, dim))] + [ANY] * n,
        [shape((rows, blocks * width), BF), shape((1, blocks * width), F32)],
        [at_cols(rows, 2 * width, z_place), at_cols(1, 2 * width, z_place)],
        [pltpu.VMEM((dim, blocks * width), BF), pltpu.SemaphoreType.DMA((lay.nz, 1))],
    )


def second_back_call(lay, pos, pre, grad, middle, gain, weights, width):
    rows, dim = middle.shape
    blocks = 2 * lay.nz
    n = len(weights)

    def body(pos_ref, pre_ref, grad_ref, middle_ref, gain_ref, *rest):
        refs, (mgrad_ref, low_ref, sums_ref, whole, acc, sem) = rest[:n], rest[n:]
        wants = ((0, width, whole),)
        dz = pl.program_id(0)

        stream_loads(lay, pos_ref, refs, wants, sem)

        @pl.when(dz == 0)
        def _():
            acc[...] = jnp.zeros_like(acc)

        cols = pl.ds(aligned(z_place(dz, pos_ref) * 2 * width, width), 2 * width)
        acc[...] += dot_nt(pre_ref[...], whole[:, cols])

        @pl.when(dz == lay.nz - 1)
        def _():
            unit, inverse = norm_parts(middle_ref[...])
            second_grad = acc[...]
            sums_ref[0:1] = jnp.sum(second_grad * unit, axis=0, keepdims=True)
            sums_ref[1:2] = jnp.sum(second_grad, axis=0, keepdims=True)
            out = grad_ref[...].astype(F32)
            sums_ref[3:4] = jnp.sum(out, axis=0, keepdims=True)
            out = out + norm_backward(second_grad, unit, inverse, gain_ref[...])
            sums_ref[2:3] = jnp.sum(out, axis=0, keepdims=True)
            mgrad_ref[...] = out
            low_ref[...] = out.astype(BF)

    return kernel_call(
        body,
        pos,
        (lay.nz,),
        (pre, grad, middle, gain, *weights),
        [at_cols(rows, 2 * width, z_place)] + [full((rows, dim))] * 2 + [full((1, dim))] + [ANY] * n,
        [shape((rows, dim), F32), shape((rows, dim), BF), shape((4, dim), F32)],
        [full((rows, dim))] * 2 + [full((4, dim))],
        [
            pltpu.VMEM((dim, blocks * width), BF),
            pltpu.VMEM((rows, dim), F32),
            pltpu.SemaphoreType.DMA((lay.nz, 1)),
        ],
    )


def mixed_grad_call(lay, pos, low, weights, first, width):
    rows, dim = low.shape
    blocks = 2 * lay.nz
    n = len(weights)

    def body(pos_ref, low_ref, *rest):
        refs, (out_ref, whole, sem) = rest[:n], rest[n:]
        wants = ((first, width, whole),)
        all_loads(lay, pos_ref, refs, wants, sem)
        out_ref[...] = dot(low_ref[...], whole[...]).astype(BF)

    return kernel_call(
        body,
        pos,
        (),
        (low, *weights),
        [full((rows, dim))] + [ANY] * n,
        [shape((rows, blocks * width), BF)],
        [full((rows, blocks * width))],
        [pltpu.VMEM((dim, blocks * width), BF), pltpu.SemaphoreType.DMA((lay.nz, 1))],
    )[0]


def attend_back_call(pos, span, query, key, value, seg_k, seg_q, lse, mixed_grad, exact, earlier=()):
    blocks, both, width = key.shape
    rows = query.shape[1]
    heads = width // HEAD_DIM
    step = min(rows, 256)
    begin = span[0]
    n = len(earlier)

    def body(pos_ref, q_ref, k_ref, v_ref, sk_ref, sq_ref, lse_ref, grad_ref, exact_ref, *rest):
        dq_ref, dk_ref, dv_ref, sums_ref, bias, dq_t, dk, dv = rest[n:]

        @pl.when(pl.program_id(0) == 0)
        def _():
            bias[...] = mask_bias(sk_ref[...], sq_ref[...], rows)

        key_t = k_ref[0].T
        inner_t = (grad_ref[...].astype(F32) * exact_ref[...]).T
        dk[...] = jnp.zeros_like(dk)
        dv[...] = jnp.zeros_like(dv)
        for tile in range(rows // step):
            here = slice(tile * step, (tile + 1) * step)
            keys = both - rows + (tile + 1) * step
            for head in range(heads):
                lanes = slice(head * HEAD_DIM, (head + 1) * HEAD_DIM)
                q_head = head_only(q_ref[0, here], head)
                g_head = head_only(grad_ref[here], head)
                scores = dot_nt(k_ref[0, :keys], q_head) + bias[:keys, here]
                probs = jnp.exp(scores - lse_ref[0, head : head + 1, here])
                prob_grad = dot_nt(v_ref[0, :keys], g_head)
                inner = jnp.sum(inner_t[lanes, here], axis=0, keepdims=True)
                score_grad = (probs * (prob_grad - inner)).astype(BF)
                dv[:keys] += dot(probs.astype(BF), g_head)
                dk[:keys] += dot(score_grad, q_head)
                dq_t[lanes, here] = dot(key_t[lanes, :keys], score_grad)
        dq = (dq_t[...].T * HEAD_DIM**-0.5).astype(BF)
        dv_low = dv[...].astype(BF)
        dq_ref[0] = dq
        dk_ref[0] = dk[...].astype(BF)
        dv_ref[0] = dv_low
        sums_ref[0:1] = jnp.sum(dq.astype(F32), axis=0, keepdims=True)
        sums_ref[1:2] = jnp.sum(dv_low.astype(F32), axis=0, keepdims=True)

    at = lambda k, pos: k + begin
    return kernel_call(
        body,
        pos,
        (span[1] - span[0],),
        (query, key, value, seg_k, seg_q, lse, mixed_grad, exact, *earlier),
        [
            at_lead(1, rows, width, place=at),
            at_lead(1, both, width, place=at),
            at_lead(1, both, width, place=at),
            full((both, 1)),
            full((1, rows)),
            at_lead(1, heads, rows, place=at),
            at_cols(rows, width, at),
            at_cols(rows, width, at),
        ]
        + [ANY] * n,
        [
            shape((blocks, rows, width), BF),
            shape((blocks, both, width), BF),
            shape((blocks, both, width), BF),
            shape((2, blocks * width), F32),
        ],
        [
            at_lead(1, rows, width, place=at),
            at_lead(1, both, width, place=at),
            at_lead(1, both, width, place=at),
            at_cols(2, width, at),
        ],
        [
            pltpu.VMEM((both, rows), F32),
            pltpu.VMEM((width, rows), F32),
            pltpu.VMEM((both, width), F32),
            pltpu.VMEM((both, width), F32),
        ],
        {9: 0, 10: 1, 11: 2, 12: 3} if n else {},
    )


def sides(ref, which, rows):
    here = slice(0, rows) if which == 0 else slice(rows, 2 * rows)
    return [ref[x, here] for x in range(2)]


def first_grad_prev_call(lay, pos, dk, dv, tokens, gain, weights, width):
    rows, dim = tokens.shape
    blocks = 2 * lay.nz
    n = len(weights)

    def body(pos_ref, dk_ref, dv_ref, tok_ref, gain_ref, *rest):
        refs, (grad_ref, sums_ref, whole, acc, sem) = rest[:n], rest[n:]
        wants = ((width, 2 * width, whole),)
        dz = pl.program_id(0)

        stream_loads(lay, pos_ref, refs, wants, sem)

        @pl.when(dz == 0)
        def _():
            acc[...] = jnp.zeros_like(acc)

        keys, values = sides(dk_ref, 0, rows), sides(dv_ref, 0, rows)
        part = jnp.concatenate([keys[0], values[0], keys[1], values[1]], axis=1)
        cols = pl.ds(aligned(z_place(dz, pos_ref) * 4 * width, width), 4 * width)
        acc[...] += dot_nt(part, whole[:, cols])

        @pl.when(dz == lay.nz - 1)
        def _():
            grad = acc[...]
            unit, inverse = norm_parts(tok_ref[...].astype(F32))
            grad_ref[...] = norm_backward(grad, unit, inverse, gain_ref[...]).astype(BF)
            sums_ref[0:1] = jnp.sum(grad * unit, axis=0, keepdims=True)
            sums_ref[1:2] = jnp.sum(grad, axis=0, keepdims=True)

    both = at_lead(2, rows, width, place=z_place)
    return kernel_call(
        body,
        pos,
        (lay.nz,),
        (dk, dv, tokens, gain, *weights),
        [both, both, full((rows, dim)), full((1, dim))] + [ANY] * n,
        [shape((rows, dim), BF), shape((2, dim), F32)],
        [full((rows, dim)), full((2, dim))],
        [
            pltpu.VMEM((dim, blocks * 2 * width), BF),
            pltpu.VMEM((rows, dim), F32),
            pltpu.SemaphoreType.DMA((lay.nz, 1)),
        ],
    )


def first_grad_own_call(lay, pos, dq, dk, dv, tokens, middle_grad, gain, weights, width):
    rows, dim = tokens.shape
    blocks = 2 * lay.nz
    n = len(weights)

    def body(pos_ref, dq_ref, dk_ref, dv_ref, tok_ref, middle_ref, gain_ref, *rest):
        refs, (grad_ref, sums_ref, whole_q, whole_kv, sem) = rest[:n], rest[n:]
        wants = ((0, width, whole_q), (width, 2 * width, whole_kv))
        dz = pl.program_id(0)

        stream_loads(lay, pos_ref, refs, wants, sem)

        @pl.when(dz == 0)
        def _():
            grad_ref[...] = jnp.zeros_like(grad_ref)

        z = z_place(dz, pos_ref)
        keys, values = sides(dk_ref, 1, rows), sides(dv_ref, 1, rows)
        part = jnp.concatenate([keys[0], values[0], keys[1], values[1]], axis=1)
        more = dot_nt(part, whole_kv[:, pl.ds(aligned(z * 4 * width, width), 4 * width)])
        part = jnp.concatenate([dq_ref[0], dq_ref[1]], axis=1)
        more += dot_nt(part, whole_q[:, pl.ds(aligned(z * 2 * width, width), 2 * width)])
        grad_ref[...] += more

        @pl.when(dz == lay.nz - 1)
        def _():
            grad = grad_ref[...]
            unit, inverse = norm_parts(tok_ref[...].astype(F32))
            sums_ref[0:1] = jnp.sum(grad * unit, axis=0, keepdims=True)
            sums_ref[1:2] = jnp.sum(grad, axis=0, keepdims=True)
            grad_ref[...] = middle_ref[...] + norm_backward(grad, unit, inverse, gain_ref[...])

    both = at_lead(2, 2 * rows, width, place=z_place)
    return kernel_call(
        body,
        pos,
        (lay.nz,),
        (dq, dk, dv, tokens, middle_grad, gain, *weights),
        [at_lead(2, rows, width, place=z_place), both, both]
        + [full((rows, dim))] * 2
        + [full((1, dim))]
        + [ANY] * n,
        [shape((rows, dim), F32), shape((2, dim), F32)],
        [full((rows, dim)), full((2, dim))],
        [
            pltpu.VMEM((dim, blocks * width), BF),
            pltpu.VMEM((dim, blocks * 2 * width), BF),
            pltpu.SemaphoreType.DMA((lay.nz, 2)),
        ],
    )


def half_grad_call(lay, pos, *, half, columns, lefts, tile, operands, specs, received):
    ny, nz, near, rows = lay.ny, lay.nz, lay.near, lay.rows
    n = len(operands)

    def body(pos_ref, *refs):
        ins, rest = refs[:n], refs[n:]
        got, rest = (rest[0], rest[1:]) if half == 0 else (None, rest)
        count = ny + 2 if half == 0 else 1
        outs, turned, spare = rest[:count], rest[count : count + len(lefts)], rest[count + len(lefts) :]
        dz = pl.program_id(0)

        @pl.when(dz == 0)
        def _():
            for index, ref in zip(lefts, turned):
                if rows % 128:
                    spare[0][...] = ins[index][...].T
                for dy in range(ny):
                    span = pl.ds(lay.row_start(pos_ref, dy, half), rows)
                    piece = spare[0][span] if rows % 128 else ins[index][:, span].T
                    ref[dy * rows : (dy + 1) * rows] = piece

        def make(put):
            blocks = tile(turned, ins, [lay.x_block(pos_ref, dx) for dx in range(2)])
            for dx in range(2):
                for dy in range(ny):
                    block = blocks[dx][dy * rows : (dy + 1) * rows]
                    if half == 0:
                        block = block + got[0, dx, dy].astype(F32)
                    put(dx, dy, block.astype(BF))

        if half == 1:

            def put(dx, dy, block):
                outs[0][0, dx, dy] = block

            make(put)
            return

        @pl.when(dz < near)
        def _():
            def put(dx, dy, block):
                outs[dy][0, dx] = block

            make(put)

        @pl.when(dz >= near)
        def _():
            def put(dx, dy, block):
                outs[ny + dx][0, dy] = block

            make(put)

    def step(*dims, at=lambda dz: dz):
        return pl.BlockSpec((1,) + dims, lambda dz, pos: (at(dz),) + (0,) * len(dims))

    if half == 0:
        operands = (*operands, received)
        specs = [*specs, step(2, ny, rows, columns)]
        outs = [shape((near, 2, rows, columns), BF)] * ny + [shape((nz - near, ny, rows, columns), BF)] * 2
        out_specs = [step(2, rows, columns, at=lambda dz: jnp.minimum(dz, near - 1))] * ny
        out_specs += [step(ny, rows, columns, at=lambda dz: jnp.maximum(dz - near, 0))] * 2
    else:
        outs = [shape((nz, 2, ny, rows, columns), BF)]
        out_specs = [step(2, ny, rows, columns)]
    scratch = [pltpu.VMEM((ny * rows, operands[index].shape[0]), BF) for index in lefts]
    if rows % 128:
        scratch.append(pltpu.VMEM(operands[lefts[0]].shape[::-1], BF))
    return kernel_call(body, pos, (nz,), operands, specs, outs, out_specs, scratch)


def sum_call(pos, groups, outs, build, steps=1):
    cut = lambda dims: (dims[0] // steps,) + dims[1:]
    spec = lambda r: pl.BlockSpec(cut(r.shape), lambda k, pos: (k,) + (0,) * (len(r.shape) - 1))
    flat = [r for g in groups for r in g]

    def body(pos_ref, *refs):
        ins, given = refs[: len(flat)], refs[len(flat) :]
        at, sums = 0, []
        for g in groups:
            mine = ins[at : at + len(g)]
            at += len(g)
            sums.append(lambda index, mine=mine: sum(
                (r[index].astype(F32) for r in mine[1:]), mine[0][index].astype(F32)
            ))
        build(sums, given)

    return kernel_call(
        body, pos, (steps,), flat, [spec(r) for r in flat], outs, [spec(o) for o in outs], [], {}, 63
    )


class Scatter:
    def __init__(self, lay, pos, columns, lefts, tile, operands, specs):
        self.lay, self.pos, self.columns = lay, pos, columns
        self.half = functools.partial(
            half_grad_call, lay, pos, columns=columns, lefts=lefts, tile=tile, operands=operands,
            specs=specs,
        )

    def away(self):
        self.sent = self.half(half=1, received=None)[0]

    def swap(self):
        self.received = trade(self.sent, "c", 2, 1)

    def own(self):
        parts = self.half(half=0, received=self.received)
        self.top, self.low = parts[: self.lay.ny], parts[self.lay.ny :]

    def send_one(self):
        self.top = [self.top[0]] + [trade(self.top[d], "fy", self.lay.ny, d) for d in range(1, self.lay.ny)]
        self.low = [self.low[0], trade(self.low[1], "tx", 2, 1)]

    def sum_one(self):
        ny, rows, near, far = self.lay.ny, self.lay.rows, self.lay.near, self.lay.nz - self.lay.near

        def build(sums, given):
            for dx in range(2):
                given[dx][...] = sums[0]((slice(None), dx)).astype(BF)
            for dy in range(ny):
                given[2 + dy][...] = sums[1]((slice(None), dy)).astype(BF)

        outs = [shape((near, rows, self.columns), BF)] * 2 + [shape((far, rows, self.columns), BF)] * ny
        out = sum_call(self.pos, [self.top, self.low], outs, build, near if near == far else 1)
        self.top, self.low = out[:2], out[2:]

    def send_two(self):
        self.top = [self.top[0], trade(self.top[1], "tx", 2, 1)]
        self.low = [self.low[0]] + [trade(self.low[d], "fy", self.lay.ny, d) for d in range(1, self.lay.ny)]

    def sum_two(self):
        near, nz = self.lay.near, self.lay.nz

        def build(sums, given):
            for dz in range(nz):
                given[dz][...] = (sums[0](dz) if dz < near else sums[1](dz - near)).astype(BF)

        outs = [shape((self.lay.rows, self.columns), BF)] * nz
        self.top = sum_call(self.pos, [self.top, self.low], outs, build)
        self.low = []

    def send_three(self):
        self.top = [self.top[0]] + [trade(self.top[d], "tz", self.lay.nz, d) for d in range(1, self.lay.nz)]

    def sum_three(self, cuts):
        rows = self.lay.rows
        outs = [shape((c[0], rows, c[1]) if isinstance(c, tuple) else (rows, c), F32) for c in cuts]

        def build(sums, given):
            at = 0
            for ref, c in zip(given, cuts):
                if isinstance(c, tuple):
                    for i in range(c[0]):
                        ref[i] = sums[0]((slice(None), slice(at, at + c[1])))
                        at += c[1]
                else:
                    ref[...] = sums[0]((slice(None), slice(at, at + c)))
                    at += c

        self.out = sum_call(self.pos, [self.top], outs, build)


def per_device(
    sizes,
    tokens,
    segment_ids,
    w_qkv,
    b_qv,
    w_out,
    b_out,
    w_up,
    b_up,
    w_down,
    b_down,
    ln1_gain,
    ln1_shift,
    ln2_gain,
    ln2_shift,
    grad_out,
):
    ny, nz = sizes
    rows, dim = tokens.shape
    length = segment_ids.shape[1]
    width = w_qkv.shape[2]
    hidden = w_up.shape[1]
    lay = Layout(ny, nz, w_qkv.shape[0])
    axes = ("fy", "c", "tz", "tx")
    pos = jnp.stack([lax.axis_index(axis) for axis in axes]).astype(jnp.int32)
    row = lambda v: v.reshape(1, -1)

    blocks = 2 * nz
    half = nz
    up_parts = [lax.all_gather(jnp.concatenate([w_up, w_out], axis=1), axes, axis=0, tiled=False)]
    qkv = Gather(lay, w_qkv.reshape(lay.rows, 3 * width))
    down = Gather(lay, w_down)
    qkv.one()
    tokens_prev = lax.ppermute(tokens, "tx", [(0, 1)])
    tokens_prev = stage(qkv, tokens_prev)
    qkv.two()
    qkv.three()
    qkv.swap(0)

    sequence = (pos[2] * 2 + pos[3]) // 2
    later = pos[3] > 0
    ids = lax.dynamic_slice_in_dim(segment_ids, sequence, 1, 0)
    seg_q = jnp.where(later, ids[:, rows:], ids[:, :rows])
    seg_prev = jnp.where(later, ids[:, :rows], -1)
    seg_k = jnp.concatenate([seg_prev, seg_q], axis=1).reshape(length, 1)
    both = jnp.concatenate([tokens_prev, tokens], axis=0).astype(F32)
    first = (norm_parts(both)[0] * ln1_gain + ln1_shift).astype(BF)
    first, seg_k, seg_q = stage(qkv, down, first, seg_k, seg_q)
    qkv.swap(1)
    down.one()
    qkv.parts, first = stage(qkv.parts, first)
    query, key, value = qkv_call(lay, pos, first, b_qv[0:1], b_qv[1:2], qkv.parts, width)
    mixed, exact, lse = attend_call(pos, query, key, value, seg_k, seg_q)
    mixed, up_parts = stage(down, mixed, up_parts)
    down.two()
    middle, second = branch_call(
        lay, pos, mixed, tokens, row(b_out), row(ln2_gain), row(ln2_shift), up_parts, hidden, width
    )
    middle, second = stage(down, middle, second)
    down.three()
    down.swap(0)
    gelu, slope = up_call(lay, pos, second, row(b_up), up_parts, hidden)

    whole = lambda v: full(v.shape)
    at_z = lambda size: at_cols(rows, 2 * size, z_place)
    block = lambda ref, x, size: ref[:, pl.ds(aligned(x * size, size), size)]

    def down_tile(left, ins, xs):
        return [dot(left[0][...], block(ins[1], x, hidden)) for x in xs]

    grad_down = Scatter(
        lay, pos, hidden, (0,), down_tile, (grad_out, gelu), [whole(grad_out), at_z(hidden)]
    )
    grad_down.away()
    grad_down.sent, slope, down.twin = stage(down, grad_down.sent, slope, down.twin)
    down.swap(1)
    slope, down.parts, grad_down.sent = stage(slope, down.parts, grad_down.sent)
    grad_down.swap()
    pre, grad_b_up = pre_call(lay, pos, slope, grad_out, down.parts, hidden)
    grad_down.received, pre = stage(grad_down.received, pre)
    grad_down.own()
    pre = stage(grad_down, pre)
    grad_down.send_one()
    middle_grad, middle_low, sums2 = second_back_call(
        lay, pos, pre, grad_out, middle, row(ln2_gain), up_parts, hidden
    )

    def up_tile(left, ins, xs):
        tail = dot(left[1][...], jnp.concatenate([block(ins[3], x, width) for x in xs], axis=1))
        return [
            jnp.concatenate(
                [dot(left[0][...], block(ins[1], x, hidden)), tail[:, i * width : (i + 1) * width]], axis=1
            )
            for i, x in enumerate(xs)
        ]

    grad_up = Scatter(
        lay, pos, hidden + width, (0, 2), up_tile, (second, pre, middle_low, mixed),
        [whole(second), at_z(hidden), whole(middle_low), at_z(width)],
    )
    mixed_grad = mixed_grad_call(lay, pos, middle_low, up_parts, hidden, width)
    grad_up.away()
    grad_up.sent, mixed_grad = stage(grad_down, grad_up.sent, mixed_grad)
    grad_down.sum_one()
    grad_up.sent, mixed_grad = stage(grad_down, grad_up.sent, mixed_grad)
    grad_down.send_two()
    grad_up.swap()
    partial = attend_back_call(pos, (0, half), query, key, value, seg_k, seg_q, lse, mixed_grad, exact)
    partial, grad_up.received = stage(grad_down, partial, grad_up.received)
    grad_down.sum_two()
    grad_up.own()
    partial = stage(grad_up, grad_down, partial)
    grad_up.send_one()
    grad_down.send_three()
    dq, dk, dv, sums_qv = attend_back_call(
        pos, (half, blocks), query, key, value, seg_k, seg_q, lse, mixed_grad, exact, partial
    )

    def qkv_tile(left, ins, xs):
        late = left[0][:, rows:]
        q = dot(late, jnp.concatenate([ins[1][x] for x in xs], axis=1))
        out = []
        for i, x in enumerate(xs):
            kv = dot(left[0][...], jnp.concatenate([ins[2][x], ins[3][x]], axis=1))
            out.append(jnp.concatenate([q[:, i * width : (i + 1) * width], kv], axis=1))
        return out

    grad_qkv = Scatter(
        lay, pos, 3 * width, (0,), qkv_tile, (first, dq, dk, dv),
        [
            whole(first),
            at_lead(2, rows, width, place=z_place),
            at_lead(2, 2 * rows, width, place=z_place),
            at_lead(2, 2 * rows, width, place=z_place),
        ],
    )
    grad_qkv.away()
    grad_qkv.sent, dq, dk, dv = stage(grad_up, grad_down, grad_qkv.sent, dq, dk, dv)
    grad_up.sum_one()
    grad_qkv.sent, dq, dk, dv = stage(grad_up, grad_qkv.sent, dq, dk, dv)
    grad_up.send_two()
    grad_qkv.swap()
    grad_down.sum_three((hidden,))
    grad_qkv.received, grad_down.out, dq, dk, dv = stage(
        grad_qkv.received, grad_down.out, dq, dk, dv
    )
    grad_qkv.own()
    dq, dk, dv = stage(grad_qkv, grad_up, dq, dk, dv)
    grad_qkv.send_one()
    grad_up.sum_two()
    dq, dk, dv = stage(grad_up, dq, dk, dv)
    grad_up.send_three()
    first_grad, sums1 = first_grad_own_call(
        lay, pos, dq, dk, dv, tokens, middle_grad, row(ln1_gain), qkv.parts, width
    )
    nearer = grad_up.top[: nz - 1]
    nearer, first_grad, sums1, dk, dv = stage(grad_qkv, nearer, first_grad, sums1, dk, dv)
    grad_up.top = [*nearer, grad_up.top[-1]]
    grad_qkv.sum_one()
    dk, dv = stage(grad_qkv, dk, dv)
    grad_qkv.send_two()
    back, sums_prev = first_grad_prev_call(
        lay, pos, dk, dv, tokens_prev, row(ln1_gain), qkv.parts, width
    )
    back, sums_prev, gelu = stage(grad_qkv, back, sums_prev, gelu)
    small = jnp.concatenate(
        [v.reshape(-1) for v in (sums2, grad_b_up, sums1 + sums_prev, sums_qv)]
    ).reshape(-1, 128)
    small = small + trade(small, "c", 2, 1)
    grad_qkv.sum_two()
    small, back, gelu = stage(grad_qkv, grad_up, small, back, gelu)
    grad_qkv.send_three()
    pieces = around(small, "fy", ny)
    back = lax.ppermute(back, "tx", [(1, 0)])
    grad_up.sum_three((hidden, width))
    result = result_call(lay, pos, gelu, middle, row(b_down), down.parts, hidden)
    pieces, result, back, grad_up.out = stage(grad_qkv, pieces, result, back, grad_up.out)
    small = sum(pieces)
    token_grad = (first_grad + back.astype(F32)).astype(BF)
    small = small + trade(small, "tx", 2, 1)
    small, token_grad = stage(small, token_grad)
    small = sum(around(small, "tz", nz)).reshape(-1)
    grad_qkv.sum_three(((3, width),))
    at = 4 * dim
    late = small[at + gelu.shape[1] :]
    return (
        result,
        token_grad,
        jnp.transpose(grad_qkv.out[0], (1, 0, 2)),
        late[2 * dim :].reshape(2, -1),
        grad_up.out[1],
        small[2 * dim : 3 * dim],
        grad_up.out[0],
        small[at : at + gelu.shape[1]],
        grad_down.out[0],
        small[3 * dim : at],
        late[:dim],
        late[dim : 2 * dim],
        small[:dim],
        small[dim : 2 * dim],
    )


def solution(mesh):
    n_fsdp, n_tp = mesh.devices.shape
    fine = Mesh(
        mesh.devices.reshape(n_fsdp // 2, 2, n_tp // 2, 2), ("fy", "c", "tz", "tx")
    )
    fsdp, tp, every = ("fy", "c"), ("tz", "tx"), ("fy", "c", "tz", "tx")
    tile = P(fsdp, tp)
    ins = (
        P(every, None),
        P(fsdp, None),
        P(fsdp, None, tp),
        P(),
        tile,
        P(),
        tile,
        P(),
        tile,
        P(),
        P(),
        P(),
        P(),
        P(),
        P(every, None),
    )
    outs = (
        P(every, None),
        P(every, None),
        P(fsdp, None, tp),
        P(),
        tile,
        P(),
        tile,
        P(),
        tile,
        P(),
        P(),
        P(),
        P(),
        P(),
    )
    return jax.shard_map(
        functools.partial(per_device, (n_fsdp // 2, n_tp // 2)),
        mesh=fine,
        in_specs=ins,
        out_specs=outs,
        check_vma=False,
    )
```
